256 devices in a mesh: sect: 2 (over x_hi), gx: 16 (over x_lo, y, core), gy: 8 (over z).
Axes of the slice: x: 4 (x_hi: 2, x_lo: 2; x = x_hi * 2 + x_lo), y: 4, z: 8, core: 2. Of those that a mesh axis runs over, the one named last changes fastest.
Arguments:
- air_profile_matrix: float32 [1024, 256, 256], P('gx', 'gy'), may hold values from -6 to 6
- spreading_numbers: float32 [256], replicated, may hold values from 0.025 to 0.2
- eastward_advection_number: float32 [256], replicated, may hold values from -0.2 to 0.2
- northward_advection_number: float32 [256], replicated, may hold values from -0.2 to 0.2
- landmass_warmth: float32 [1024, 256], P('gx', 'gy'), may hold values from -6 to 6
- physics_increments: int32 [1024, 64], P(None, 'gy'), may hold values from 1 to 4
- underlying_water_index: int32 [1024, 256], P('gx', 'gy'), may hold values from 0 to 511
- water_indicator: int32 [512, 128], P('gx', 'gy'), may hold values 0 or 1
- waterbody_profiles: float32 [2, 80, 512, 128], P(None, None, 'gx', 'gy'), may hold values from -6 to 6
- waterbody_drivers: float32 [2, 512, 128], P(None, 'gx', 'gy'), may hold values from -6 to 6
- inverted_blending_matrix: float32 [80, 80], replicated, may hold values from 0 to 0.55, as said below
- entry_layer_matrix: bfloat16 [256, 512], replicated, may hold values from -0.375 to 0.375
- entry_layer_offset: float32 [512], replicated, may hold values from -3 to 3
- exit_layer_matrix: bfloat16 [512, 256], replicated, may hold values from -0.25 to 0.25
Outputs:
- coupled: float32 [2, 2, 512, 128], P('sect', None, 'gx', 'gy')
The draws below stay inside these ranges and needn't reach their ends.
Inputs may be any that keep to these rules, and one draw needn't show every extreme that they name: `underlying_water_index`: a local row-major index into the same device's ocean block. `inverted_blending_matrix`: nonnegative entries; the diagonal is 0.5 or more.
All inputs are finite; a program needn't handle non-finite values. No bound on the sum of `water_indicator` on one device may be relied on, other than what follows from the above.
Results may differ from the reference program's by a relative error of at most 0.0019.
The reference program's roundings to bfloat16 on the way count: a program that leaves them out, or rounds other values in their place, can miss the bound.
Values sent between devices are 32-bit elements; how exact they have to be, the bound alone decides.
No kernel may reach another device: no remote copies, remote signals or barrier semaphores. Data moves between devices by JAX's collectives and lax.ppermute only.
A program may use at most 64 MiB of HBM per device.

```python
import math
import jax
import jax.numpy as jnp
from jax import lax

AIR_LAYERS = 128
LEV_O = 80
HID = 512
SUBMAX = 4
BS = 4
DSTEPS = 2
OSTEPS = 12
AX = 64
AY = 32
EASTWARD_COUNT = 1024
NORTHWARD_COUNT = 256
OX = 32
OY = 16
NXO = 512
NYO = 128


def draw_inverted_blending_matrix(key, part):
    key = jax.random.fold_in(key, 7)
    rows = jnp.arange(LEV_O)[:, None]
    cols = jnp.arange(LEV_O)[None, :]
    distance = jnp.abs(rows - cols).astype(jnp.float32)
    spread = jax.random.uniform(key, (LEV_O, LEV_O), jnp.float32, 0.0, 1.0)
    return 0.5 * (rows == cols).astype(jnp.float32) + 0.05 * spread * jnp.exp(-distance / 8.0)


def draw_physics_increments(key, part):
    key = jax.random.fold_in(key, 11)
    sun_key, level_key = jax.random.split(key)
    noon = jax.random.randint(sun_key, (), 0, EASTWARD_COUNT)
    rows = jnp.arange(EASTWARD_COUNT, dtype=jnp.int32)[:, None]
    sunlit = (rows - noon) % EASTWARD_COUNT < EASTWARD_COUNT // 2
    heavy = SUBMAX - jax.random.randint(level_key, (EASTWARD_COUNT, NORTHWARD_COUNT // BS), 0, 2)
    steps = jnp.where(sunlit, heavy, 1)
    steps = steps.at[noon, 0].set(SUBMAX)
    return steps.astype(jnp.int32)


def plant(values, own_key, low, high):
    place = [jax.random.randint(jax.random.fold_in(own_key, axis), (), 0, length) for axis, length in enumerate(values.shape)]
    widest = values.shape.index(max(values.shape))
    neighbour = place[:widest] + [(place[widest] + 1) % values.shape[widest]] + place[widest + 1:]
    return values.at[tuple(place)].set(low).at[tuple(neighbour)].set(high)


def shard_levels(key, dims, pieces, least, largest):
    factor_of, own = 1.0, jax.random.fold_in(key, 6)
    for position, shards_of in pieces:
        steps = jnp.exp(jax.random.uniform(jax.random.fold_in(own, position), (shards_of,), jnp.float32, least / len(pieces), largest / len(pieces)))
        factor_of = factor_of * jnp.repeat(steps, dims[position] // shards_of).reshape([-1 if axis == position else 1 for axis in range(len(dims))])
    return factor_of


def bell_draw(rng, extent, scale, limit, shards=(), kind=jnp.bfloat16):
    array = jax.random.normal(rng, extent, jnp.float32) * scale
    if len(shards) > 0:
        array = shard_levels(rng, extent, shards, -0.22, 0.18) * array
    return jnp.clip(array, min=-limit, max=limit).astype(kind)


def setup_inputs(seed: int = 0) -> dict:
    key_of = jax.random.split(jax.random.key(seed), 15)
    air_profile_matrix = bell_draw(key_of[0], (EASTWARD_COUNT, NORTHWARD_COUNT, 2 * AIR_LAYERS), 1.0, 6.0, ((0, 16), (1, 8)), jnp.float32)
    spreading_numbers = jnp.clip(jnp.exp(jax.random.uniform(key_of[1], (2 * AIR_LAYERS,), jnp.float32, math.log(0.025), math.log(0.2))), 0.025, 0.2)
    eastward_advection_number = jnp.clip(jax.random.uniform(key_of[2], (2 * AIR_LAYERS,), jnp.float32, -0.2, 0.2), -0.2, 0.2)
    northward_advection_number = jnp.clip(jax.random.uniform(key_of[3], (2 * AIR_LAYERS,), jnp.float32, -0.2, 0.2), -0.2, 0.2)
    landmass_warmth = bell_draw(key_of[4], (EASTWARD_COUNT, NORTHWARD_COUNT), 1.0, 6.0, ((0, 16), (1, 8)), jnp.float32)
    physics_increments = draw_physics_increments(jax.random.fold_in(key_of[14], 71), 0)
    underlying_water_index = plant(jax.random.randint(key_of[6], (EASTWARD_COUNT, NORTHWARD_COUNT), 0, OX * OY), jax.random.fold_in(key_of[6], 1), 0, (OX * OY) - 1).astype(jnp.int32)
    water_indicator = plant((jax.random.randint(key_of[7], (NXO, NYO), 0, 4) < 3).astype(jnp.int32), jax.random.fold_in(key_of[7], 1), 0, 1)
    waterbody_profiles = bell_draw(key_of[8], (2, LEV_O, NXO, NYO), 1.0, 6.0, ((2, 16), (3, 8)), jnp.float32)
    waterbody_drivers = bell_draw(key_of[9], (2, NXO, NYO), 1.0, 6.0, ((1, 16), (2, 8)), jnp.float32)
    inverted_blending_matrix = draw_inverted_blending_matrix(jax.random.fold_in(key_of[14], 71), 0)
    entry_layer_matrix = bell_draw(key_of[11], (2 * AIR_LAYERS, HID), (2 * AIR_LAYERS) ** -0.5, 0.375)
    entry_layer_offset = bell_draw(key_of[12], (HID,), 0.5, 3.0, (), jnp.float32)
    exit_layer_matrix = bell_draw(key_of[13], (HID, 2 * AIR_LAYERS), HID ** -0.5, 0.25)
    return {"air_profile_matrix": air_profile_matrix, "spreading_numbers": spreading_numbers, "eastward_advection_number": eastward_advection_number, "northward_advection_number": northward_advection_number, "landmass_warmth": landmass_warmth, "physics_increments": physics_increments, "underlying_water_index": underlying_water_index, "water_indicator": water_indicator, "waterbody_profiles": waterbody_profiles, "waterbody_drivers": waterbody_drivers, "inverted_blending_matrix": inverted_blending_matrix, "entry_layer_matrix": entry_layer_matrix, "entry_layer_offset": entry_layer_offset, "exit_layer_matrix": exit_layer_matrix}


THERMAL_FACTOR = 0.8
WETNESS_FACTOR = 0.6
OCEAN_STEP = 0.1


def advance(padded, spreading_numbers, eastward_advection_number, northward_advection_number):
    centre = padded[1:-1, 1:-1]
    plus_x = padded[2:, 1:-1]
    minus_x = padded[:-2, 1:-1]
    plus_y = padded[1:-1, 2:]
    minus_y = padded[1:-1, :-2]
    spread = plus_x + minus_x + plus_y + minus_y - 4.0 * centre
    return centre + spreading_numbers * spread - 0.5 * eastward_advection_number * (plus_x - minus_x) - 0.5 * northward_advection_number * (plus_y - minus_y)


def subcycle(states, counts, entry_layer_matrix, entry_layer_offset, exit_layer_matrix):
    total = states.shape[0]
    tile = math.gcd(total, 512)
    order = jnp.argsort(counts, stable=True).astype(jnp.int32)
    sorted_states = jnp.take(states, order, axis=0)
    sorted_counts = jnp.take(counts, order, axis=0)

    def one_tile(index, result):
        start = (index * tile).astype(jnp.int32)
        block = lax.dynamic_slice_in_dim(result, start, tile, 0)
        needed = lax.dynamic_slice_in_dim(sorted_counts, start, tile, 0)

        def one_round(round_index, current):
            hidden = jax.nn.gelu(jnp.dot(current.astype(jnp.bfloat16), entry_layer_matrix, preferred_element_type=jnp.float32) + entry_layer_offset).astype(jnp.bfloat16)
            stepped = current + jnp.dot(hidden, exit_layer_matrix, preferred_element_type=jnp.float32)
            return jnp.where((needed > round_index)[:, None], stepped, current)

        block = lax.fori_loop(jnp.int32(0), jnp.max(needed), one_round, block)
        return lax.dynamic_update_slice_in_dim(result, block, start, 0)

    done = lax.fori_loop(jnp.int32(0), jnp.int32(total // tile), one_tile, sorted_states)
    return jnp.zeros_like(states).at[order].set(done)


def reference(air_profile_matrix, spreading_numbers, eastward_advection_number, northward_advection_number, landmass_warmth, physics_increments, underlying_water_index, water_indicator, waterbody_profiles, waterbody_drivers, inverted_blending_matrix, entry_layer_matrix, entry_layer_offset, exit_layer_matrix):
    sea_cells = water_indicator == 1
    current = waterbody_profiles
    for step_index in range(OSTEPS):
        forced = current.at[:, 0].add(OCEAN_STEP * waterbody_drivers)
        mixed_cols = jnp.einsum("lk,fkxy->flxy", inverted_blending_matrix, forced, precision=lax.Precision.HIGHEST)
        current = jnp.where(sea_cells[None, None], mixed_cols, current)
    boundary_entries = current[:, 0]

    atm_field = air_profile_matrix
    for step_index in range(DSTEPS):
        padded = jnp.pad(atm_field, ((1, 1), (1, 1), (0, 0)), mode="wrap")
        atm_field = advance(padded, spreading_numbers, eastward_advection_number, northward_advection_number)
    channels = atm_field.shape[2]

    counts = jnp.repeat(physics_increments, BS, axis=1).reshape(EASTWARD_COUNT * NORTHWARD_COUNT).astype(jnp.int32)
    refreshed_result = subcycle(atm_field.reshape(EASTWARD_COUNT * NORTHWARD_COUNT, channels), counts, entry_layer_matrix, entry_layer_offset, exit_layer_matrix)

    col_x = jnp.arange(EASTWARD_COUNT, dtype=jnp.int32)[:, None]
    col_y = jnp.arange(NORTHWARD_COUNT, dtype=jnp.int32)[None, :]
    ocean_row = (col_x // AX) * OX + underlying_water_index // OY
    ocean_col = (col_y // AY) * OY + underlying_water_index % OY
    group_labels = (ocean_row * NYO + ocean_col).reshape(-1).astype(jnp.int32)

    oceanic_top_warmth = boundary_entries[0].reshape(-1)[group_labels]
    oceanic_profile = sea_cells.reshape(-1)[group_labels]
    interface_warmth = jnp.where(oceanic_profile, oceanic_top_warmth, landmass_warmth.reshape(-1))
    thermal_transfer = THERMAL_FACTOR * (interface_warmth - refreshed_result[:, 0])
    evaporation_transfer = WETNESS_FACTOR * (jnp.tanh(interface_warmth) - refreshed_result[:, AIR_LAYERS])
    ocean_cells = NXO * NYO
    tally = jax.ops.segment_sum(jnp.ones_like(thermal_transfer), group_labels, ocean_cells)
    sums_heat = jax.ops.segment_sum(thermal_transfer, group_labels, ocean_cells)
    sums_vapour = jax.ops.segment_sum(evaporation_transfer, group_labels, ocean_cells)
    fluxes = jnp.stack([sums_heat, sums_vapour]) / jnp.maximum(tally, 1.0)
    return jnp.stack([fluxes.reshape(2, NXO, NYO), boundary_entries])
```

```python
import functools

import jax
import jax.numpy as jnp
from jax import lax
from jax.experimental import pallas as pl
from jax.experimental.pallas import tpu as pltpu
from jax.sharding import PartitionSpec as P

BS = 4
PAIRS = 6
THERMAL_FACTOR = 0.8
WETNESS_FACTOR = 0.6
OCEAN_STEP = 0.1
TANH_SCALE = 0.7978845608028654
TANH_CUBE = 0.044715

GROUPS = 3
TILES = 5
LANES = 128
NT = (((1,), (1,)), ((), ()))
F32 = jnp.float32
BF16 = jnp.bfloat16
AXES = ("sect", "gx", "gy")


def iota(shape, dim):
    return lax.broadcasted_iota(jnp.int32, shape, dim)


def coefficients(spread, east, north):
    return (
        1.0 - 4.0 * spread,
        spread - 0.5 * east,
        spread + 0.5 * east,
        spread - 0.5 * north,
        spread + 0.5 * north,
    )


def combine(coefs, centre, plus_x, minus_x, plus_y, minus_y):
    c0, cxp, cxm, cyp, cym = coefs
    return c0 * centre + cxp * plus_x + cxm * minus_x + cyp * plus_y + cym * minus_y


def advance(block, coefs):
    centre = block[1:-1]
    size = centre.shape[1]
    plus_y = pltpu.roll(centre, size - 1, 1)
    minus_y = pltpu.roll(centre, 1, 1)
    return combine(coefs, centre, block[2:], block[:-2], plus_y, minus_y)


def hidden_of(state, w1, bias):
    half = jnp.dot(state.astype(BF16), w1, preferred_element_type=F32) + bias
    inner = half * (half * half * (8.0 * TANH_SCALE * TANH_CUBE) + 2.0 * TANH_SCALE)
    return (half * jnp.tanh(inner) + half).astype(BF16)


def physics(state, counts, w1, bias, w2, w2_last):
    for index in range(3):
        delta = jnp.dot(hidden_of(state, w1, bias), w2, preferred_element_type=F32)
        if index:
            needed = counts > float(index)
            delta = jnp.where(jnp.concatenate([needed, needed], 1), delta, 0.0)
        state = state + delta
    delta = jnp.dot(hidden_of(state, w1, bias), w2_last, preferred_element_type=F32)
    lane = iota((1, LANES), 1)
    kept = jnp.where(lane == 0, state[:, :LANES], pltpu.roll(state[:, LANES:], 1, 1))
    return kept + jnp.where(counts > 3.0, delta, 0.0)


def weights(w1_ref, b_ref, w2_ref):
    w1 = w1_ref[...] * jnp.asarray(0.5, BF16)
    bias = b_ref[...] * 0.5
    w2 = w2_ref[...]
    lane = iota((1, LANES), 1)
    low = w2[:, :LANES].astype(F32)
    high = pltpu.roll(w2[:, LANES:].astype(F32), 1, 1)
    last = jnp.where(lane == 0, low, jnp.where(lane == 1, high, 0.0)).astype(BF16)
    return w1, bias, w2, last


def expand_counts(row):
    square = (LANES, LANES)
    diagonal = jnp.where(iota(square, 0) == iota(square, 1), row, 0.0).astype(BF16)
    return jnp.dot(diagonal, jnp.ones(square, BF16), preferred_element_type=F32)


def split(row):
    high = row.astype(BF16).astype(F32)
    return high, row - high


def one_hots(cells, row):
    n = cells.shape[1]
    first = iota((32, n), 0) == jnp.right_shift(cells, 4)
    second = (iota((16, n), 0) == jnp.bitwise_and(cells, 15)) & (cells >= 0)
    return first, second.astype(F32).astype(BF16)


def scatter(values, first, second):
    rows = []
    for value in values:
        for part in split(value):
            rows.append(jnp.where(first, part, 0.0))
    stacked = jnp.concatenate(rows, 0).astype(BF16)
    return lax.dot_general(stacked, second, NT, preferred_element_type=F32)


def scatter_columns(kept, cells):
    n = kept.shape[0]
    rows = [jnp.transpose(kept[i : i + LANES])[:2] for i in range(0, n, LANES)]
    flat = jnp.concatenate(rows, 1)
    first, second = one_hots(cells, None)
    return scatter([flat[0:1], flat[1:2]], first, second)


def own_counts(inc_ref, size):
    gx = lax.axis_index("gx")
    start = pl.multiple_of((gx // 2) * LANES, LANES)
    block = inc_ref[:, pl.ds(start, LANES)].astype(F32)
    block = jnp.where(gx % 2 == 1, pltpu.roll(block, 64, 1), block)
    spread = (iota((size, 8), 0) // BS == iota((size, 8), 1)).astype(F32)
    return jnp.dot(spread.astype(BF16), block.astype(BF16), preferred_element_type=F32)


def coded_columns(idx_ref, inc_ref):
    counts = own_counts(inc_ref, idx_ref.shape[0])
    cells = idx_ref[...].astype(F32)
    cells = jnp.concatenate([cells, jnp.zeros_like(cells)], 1)
    return cells * 8.0 + counts


def decode(code):
    whole = code.astype(jnp.int32)
    return jnp.right_shift(whole, 3), jnp.bitwise_and(whole, 7).astype(F32)


def interior_kernel(
    range_ref, air_ref, spread_ref, east_ref, north_ref, idx_ref, inc_ref, w1_ref, b_ref, w2_ref,
    acc_ref, turned, cell_rows, count_rows,
):
    lo = range_ref[0]
    hi = range_ref[1]
    acc_ref[...] = jnp.zeros_like(acc_ref)

    @pl.when(hi > lo)
    def _():
        code = coded_columns(idx_ref, inc_ref)
        code = jnp.concatenate([code, jnp.zeros((96, LANES), F32)], 0)
        turned[...] = jnp.transpose(code)
        groups = GROUPS * TILES
        parts = [turned[pl.ds(2 + j, groups, stride=4), :][:, :32] for j in range(4)]
        cells, counts = decode(jnp.concatenate(parts, 1))
        y = jnp.bitwise_and(iota((1, LANES), 1), 31)
        cells = jnp.where((y >= 2) & (y < 30), cells, -1)
        cell_rows[pl.ds(0, groups), :] = cells
        count_rows[pl.ds(0, groups), :] = counts

        coefs = coefficients(spread_ref[...], east_ref[...], north_ref[...])
        w1, bias, w2, w2_last = weights(w1_ref, b_ref, w2_ref)

        @pl.loop(lo, hi)
        def _(tile):
            block = air_ref[pl.ds(tile * (4 * GROUPS), 4 * GROUPS + 4)]
            state = advance(advance(block, coefs), coefs).reshape(GROUPS * LANES, 256)
            rows = [cell_rows[pl.ds(tile * GROUPS + g, 1), :] for g in range(GROUPS)]
            needs = [expand_counts(count_rows[pl.ds(tile * GROUPS + g, 1), :]) for g in range(GROUPS)]
            kept = physics(state, jnp.concatenate(needs, 0), w1, bias, w2, w2_last)
            acc_ref[...] += scatter_columns(kept, jnp.concatenate(rows, 1))


def interior(bounds, air, small, big):
    vmem = pl.BlockSpec(memory_space=pltpu.VMEM)
    return pl.pallas_call(
        interior_kernel,
        out_shape=jax.ShapeDtypeStruct((LANES, 16), F32),
        in_specs=[pl.BlockSpec(memory_space=pltpu.SMEM)] + [vmem] * 9,
        out_specs=vmem,
        scratch_shapes=[
            pltpu.VMEM((LANES, LANES), F32),
            pltpu.VMEM((16, LANES), jnp.int32),
            pltpu.VMEM((16, LANES), F32),
        ],
        compiler_params=pltpu.CompilerParams(vmem_limit_bytes=32 << 20),
        cost_estimate=pl.CostEstimate(flops=1 << 30, bytes_accessed=2 << 20, transcendentals=1 << 20),
    )(bounds, air, *small, *big)


def slab_kernel(air_ref, low_ref, high_ref, low4_ref, high4_ref, low_blk, high_blk, sem):
    copies = []
    for side, block in ((0, low_blk), (1, high_blk)):
        for half in range(2):
            source = air_ref.at[:, pl.ds(24 * side, 8), pl.ds(half * LANES, LANES)]
            copy = pltpu.make_async_copy(source, block.at[half], sem.at[side, half])
            copy.start()
            copies.append(copy)
    for side, block, send, keep in ((0, low_blk, low_ref, low4_ref), (1, high_blk, high_ref, high4_ref)):
        for half in range(2):
            copies[2 * side + half].wait()
            flat = block.at[half].reshape(64 * 8, LANES)
            lanes = pl.ds(half * LANES, LANES)
            for k in range(4):
                row = flat[pl.ds(4 * side + k, 64, stride=8), :]
                keep[k, :, lanes] = row
                sent = k - 2 * side
                if 0 <= sent < 2:
                    send[pl.ds(sent * 64, 64), lanes] = row


def y_slabs(air):
    vmem = pl.BlockSpec(memory_space=pltpu.VMEM)
    return pl.pallas_call(
        slab_kernel,
        out_shape=[jax.ShapeDtypeStruct((LANES, 256), F32)] * 2
        + [jax.ShapeDtypeStruct((4, 64, 256), F32)] * 2,
        in_specs=[pl.BlockSpec(memory_space=pl.ANY)],
        out_specs=[vmem] * 4,
        scratch_shapes=[
            pltpu.VMEM((2, 64, 8, LANES), F32),
            pltpu.VMEM((2, 64, 8, LANES), F32),
            pltpu.SemaphoreType.DMA((2, 2)),
        ],
    )(air)


def shift_down(block, edge):
    row = iota(block.shape, 1)
    return jnp.where(row == 0, edge, pltpu.roll(block, 1, 1))


def shift_up(block, edge):
    row = iota(block.shape, 1)
    size = block.shape[1]
    return jnp.where(row == size - 1, edge, pltpu.roll(block, size - 1, 1))


def edge_states(air_ref, low4_ref, high4_ref, ylow, yhigh, xlow_ref, xhigh_ref, coefs):
    xlow = xlow_ref[...]
    xhigh = xhigh_ref[...]
    before = xlow[:64].reshape(2, 32, 256)
    after = xhigh[:64].reshape(2, 32, 256)
    first_low = advance(jnp.concatenate([before, air_ref[0:4]], 0), coefs)
    first_high = advance(jnp.concatenate([air_ref[60:64], after], 0), coefs)
    state_x = jnp.concatenate([advance(first_low, coefs), advance(first_high, coefs)], 0)

    def column(halo, corners, inner, at, side):
        far, near = (0, 1) if side else (1, 0)
        lo_y = corners[0:1] if at == 0 else halo[near, at - 1 : at]
        hi_y = corners[1:2] if at == 31 else halo[near, at + 1 : at + 2]
        centre = halo[near, at : at + 1]
        outer = halo[far, at : at + 1]
        plus_x, minus_x = (inner, outer) if side else (outer, inner)
        return combine(coefs, centre, plus_x, minus_x, hi_y, lo_y)

    states = []
    for low in (True, False):
        if low:
            block = jnp.concatenate([ylow, low4_ref[...]], 0)
            left = [xlow[64:65]] + [before[1, y : y + 1] for y in (0, 1, 2)]
            right = [xhigh[64:65]] + [after[0, y : y + 1] for y in (0, 1, 2)]
            targets = (0, 1)
        else:
            block = jnp.concatenate([high4_ref[...], yhigh], 0)
            left = [before[1, y : y + 1] for y in (29, 30, 31)] + [xlow[65:66]]
            right = [after[0, y : y + 1] for y in (29, 30, 31)] + [xhigh[65:66]]
            targets = (30, 31)
        centre = block[1:-1]
        once = combine(
            coefs,
            centre,
            shift_up(centre, jnp.stack(right, 0)),
            shift_down(centre, jnp.stack(left, 0)),
            block[2:],
            block[:-2],
        )
        left, right = [], []
        for y in targets:
            left.append(column(before, xlow[64:66], air_ref[0, y : y + 1, :], y, True))
            right.append(column(after, xhigh[64:66], air_ref[63, y : y + 1, :], y, False))
        centre = once[1:-1]
        twice = combine(
            coefs,
            centre,
            shift_up(centre, jnp.stack(right, 0)),
            shift_down(centre, jnp.stack(left, 0)),
            once[2:],
            once[:-2],
        )
        states.append(twice.reshape(LANES, 256))
    return jnp.concatenate(states, 0), state_x.reshape(LANES, 256)


def ocean_surface(water, driver, ocean_ref, mixing_ref, row_scratch):
    levels = mixing_ref.shape[0]
    matrix = mixing_ref[...]
    wide = jnp.concatenate([matrix, jnp.zeros((levels, LANES - levels), F32)], 1)
    tall = jnp.concatenate([wide, jnp.zeros((LANES - levels, LANES), F32)], 0)
    turned = jnp.transpose(tall)
    column = (iota((LANES, 1), 0) == 0).astype(F32)
    total = jnp.zeros((1, 1), F32)

    def pair(_, carry):
        column, total = carry
        row = jnp.sum(column * tall, axis=0, keepdims=True)
        total = total + row[:, 0:1]
        column = jnp.sum(turned * row, axis=1, keepdims=True)
        return column, total + column[0:1]

    column, total = lax.fori_loop(0, PAIRS, pair, (column, total))
    row = jnp.transpose(jnp.broadcast_to(column, (LANES, LANES)))[0:1, :levels]
    fields = []
    for field in range(2):
        block = ocean_ref[field]
        mixed = jnp.sum(block * row, axis=2)
        top = block[:, :, 0]
        mixed = jnp.transpose(mixed) + (OCEAN_STEP * total) * driver[field]
        fields.append(jnp.where(water == 1, mixed, jnp.transpose(top)))
    return fields


def land_sums(land, cells):
    lands = jnp.concatenate([land[y : y + 1] for y in range(32)], 1)
    places = jnp.concatenate([cells[y : y + 1] for y in range(32)], 1)
    first, second = one_hots(places, None)
    sums = scatter([lands, jnp.tanh(lands)], first, second)
    count = lax.dot_general(
        first.astype(F32).astype(BF16), second, NT, preferred_element_type=F32
    )
    return sums, count


def side_kernel(
    ocean_ref, water_ref, driver_ref, mixing_ref, land_ref, idx_ref, out_ref, row_scratch
):
    fields = ocean_surface(water_ref[...], driver_ref[...], ocean_ref, mixing_ref, row_scratch)
    sums, count = land_sums(land_ref[...], idx_ref[...])
    land = jnp.transpose(sums[0:32] + sums[32:64])
    warm = jnp.transpose(sums[64:96] + sums[96:128])
    count = jnp.transpose(count)
    sea = water_ref[...] == 1
    top = fields[0]
    out_ref[0] = fields[0]
    out_ref[1] = fields[1]
    out_ref[2] = jnp.where(sea, count * top, land)
    out_ref[3] = jnp.where(sea, count * jnp.tanh(top), warm)
    out_ref[4] = jnp.maximum(count, 1.0)


def side(ocean, water, driver, mixing, land, idx):
    vmem = pl.BlockSpec(memory_space=pltpu.VMEM)
    return pl.pallas_call(
        side_kernel,
        out_shape=jax.ShapeDtypeStruct((5, 16, 32), F32),
        in_specs=[vmem] * 6,
        out_specs=vmem,
        scratch_shapes=[pltpu.VMEM((8, LANES), F32)],
        compiler_params=pltpu.CompilerParams(vmem_limit_bytes=32 << 20),
        cost_estimate=pl.CostEstimate(flops=1 << 22, bytes_accessed=2 << 20, transcendentals=0),
    )(ocean, water, driver, mixing, land, idx)


def edge_kernel(
    air_ref, low4_ref, high4_ref, ylow_ref, yhigh_ref, xlow_ref, xhigh_ref, spread_ref, east_ref,
    north_ref, idx_ref, inc_ref, w1_ref, b_ref, w2_ref, side_ref, acc0_ref, acc1_ref, acc2_ref, out_ref,
):
    coefs = coefficients(spread_ref[...], east_ref[...], north_ref[...])
    w1, bias, w2, w2_last = weights(w1_ref, b_ref, w2_ref)
    ylow = ylow_ref[...].reshape(2, 64, 256)
    yhigh = yhigh_ref[...].reshape(2, 64, 256)
    by_y, by_x = edge_states(
        air_ref, low4_ref, high4_ref, ylow, yhigh, xlow_ref, xhigh_ref, coefs
    )
    code = coded_columns(idx_ref, inc_ref)
    rows_y = [
        jnp.concatenate([code[0:1, :64], code[1:2, :64]], 1),
        jnp.concatenate([code[30:31, :64], code[31:32, :64]], 1),
    ]
    code = jnp.concatenate([code, jnp.zeros((96, LANES), F32)], 0)
    turned = jnp.transpose(code)[:, :32]
    row_x = jnp.concatenate([turned[i : i + 1] for i in (0, 1, 62, 63)], 1)
    cells, counts = decode(jnp.concatenate(rows_y + [row_x], 1))
    place = iota(cells.shape, 1)
    y = jnp.bitwise_and(place, 31)
    cells = jnp.where((place < 2 * LANES) | ((y >= 2) & (y < 30)), cells, -1)
    needs = [expand_counts(counts[:, i : i + LANES]) for i in range(0, 3 * LANES, LANES)]
    state = jnp.concatenate([by_y, by_x], 0)
    kept = physics(state, jnp.concatenate(needs, 0), w1, bias, w2, w2_last)
    acc = scatter_columns(kept, cells) + acc0_ref[...] + acc1_ref[...] + acc2_ref[...]
    heat = jnp.transpose(acc[0:32] + acc[32:64])
    vapour = jnp.transpose(acc[64:96] + acc[96:128])
    below = side_ref[4]
    ocean = lax.axis_index("sect") == 1
    flux = THERMAL_FACTOR * (side_ref[2] - heat) / below
    out_ref[0] = jnp.where(ocean, side_ref[0], flux)
    flux = WETNESS_FACTOR * (side_ref[3] - vapour) / below
    out_ref[1] = jnp.where(ocean, side_ref[1], flux)


def edges(air, halos, small, big, others):
    vmem = pl.BlockSpec(memory_space=pltpu.VMEM)
    return pl.pallas_call(
        edge_kernel,
        out_shape=jax.ShapeDtypeStruct((2, 16, 32), F32),
        in_specs=[vmem] * 19,
        out_specs=vmem,
        compiler_params=pltpu.CompilerParams(vmem_limit_bytes=32 << 20),
        cost_estimate=pl.CostEstimate(flops=1 << 28, bytes_accessed=2 << 20, transcendentals=1 << 20),
    )(air, *halos, *small, *big, *others)


def neighbours(dx, dy):
    sections, nx, ny = (lax.axis_size(axis) for axis in AXES)

    def place(s, x, y):
        return (s * nx + x % nx) * ny + y % ny

    return [
        (place(s, x + dx, y + dy), place(s, x, y))
        for s in range(sections)
        for x in range(nx)
        for y in range(ny)
    ]


def tied(first, second):
    return lax.optimization_barrier((first, second))


def shards(
    air_profile_matrix,
    spreading_numbers,
    eastward_advection_number,
    northward_advection_number,
    landmass_warmth,
    physics_increments,
    underlying_water_index,
    water_indicator,
    waterbody_profiles,
    waterbody_drivers,
    inverted_blending_matrix,
    entry_layer_matrix,
    entry_layer_offset,
    exit_layer_matrix,
):
    air = air_profile_matrix
    idx = underlying_water_index.T
    small = (
        spreading_numbers.reshape(1, -1),
        eastward_advection_number.reshape(1, -1),
        northward_advection_number.reshape(1, -1),
        idx,
        physics_increments.T,
    )
    big = (entry_layer_matrix, entry_layer_offset.reshape(1, -1), exit_layer_matrix)
    gy = lax.axis_index("gy")
    early = jnp.where(gy < 2, 2, jnp.where(gy < 4, 1, 0)).astype(jnp.int32)
    middle = early + 2

    slab_low, slab_high, low4, high4 = y_slabs(air)
    acc0 = interior(jnp.stack([jnp.int32(0), early]), air, small, big)
    acc0, slab_low, slab_high = lax.optimization_barrier((acc0, slab_low, slab_high))
    ylow = lax.ppermute(slab_high, AXES, neighbours(0, -1))
    yhigh = lax.ppermute(slab_low, AXES, neighbours(0, 1))
    acc1 = interior(jnp.stack([early, middle]), air, small, big)
    acc1, ylow, yhigh = lax.optimization_barrier((acc1, ylow, yhigh))
    pad = jnp.zeros((6, 256), F32)
    send_high = jnp.concatenate(
        [air[62], air[63], ylow[127:128], yhigh[63:64], pad], 0
    )
    send_low = jnp.concatenate([air[0], air[1], ylow[64:65], yhigh[0:1], pad], 0)
    xlow = lax.ppermute(send_high, AXES, neighbours(-1, 0))
    xhigh = lax.ppermute(send_low, AXES, neighbours(1, 0))
    sides = side(
        waterbody_profiles.transpose(0, 2, 3, 1),
        water_indicator.T,
        waterbody_drivers.transpose(0, 2, 1),
        inverted_blending_matrix,
        landmass_warmth.T,
        idx,
    )
    acc2 = interior(jnp.stack([middle, jnp.int32(TILES)]), air, small, big)
    acc2, sides, xlow, xhigh = lax.optimization_barrier((acc2, sides, xlow, xhigh))
    result = edges(air, (low4, high4, ylow, yhigh, xlow, xhigh), small, big, (sides, acc0, acc1, acc2))
    return result.transpose(0, 2, 1)[None]


def solution(mesh):
    in_specs = (
        P("gx", "gy", None),
        P(),
        P(),
        P(),
        P("gx", "gy"),
        P(None, "gy"),
        P("gx", "gy"),
        P("gx", "gy"),
        P(None, None, "gx", "gy"),
        P(None, "gx", "gy"),
        P(),
        P(),
        P(),
        P(),
    )
    out_specs = P("sect", None, "gx", "gy")
    return jax.shard_map(shards, mesh=mesh, in_specs=in_specs, out_specs=out_specs, check_vma=False)
```

```python
import jax
import jax.numpy as jnp
from jax import lax
from jax.experimental import pallas as pl
from jax.experimental.pallas import tpu as pltpu
from jax.sharding import PartitionSpec as P

BS = 4
PAIRS = 6
THERMAL_FACTOR = 0.8
WETNESS_FACTOR = 0.6
OCEAN_STEP = 0.1
TANH_SCALE = 0.7978845608028654
TANH_CUBE = 0.044715

GROUPS = 5
TILES = 3
LANES = 128
NT = (((1,), (1,)), ((), ()))
F32 = jnp.float32
BF16 = jnp.bfloat16
AXES = ("sect", "gx", "gy")


def iota(shape, dim):
    return lax.broadcasted_iota(jnp.int32, shape, dim)


def combine(coefs, centre, plus_x, minus_x, plus_y, minus_y):
    c0, cxp, cxm, cyp, cym = coefs
    return c0 * centre + cxp * plus_x + cxm * minus_x + cyp * plus_y + cym * minus_y


def advance(block, coefs):
    centre = block[1:-1]
    size = centre.shape[1]
    plus_y = pltpu.roll(centre, size - 1, 1)
    minus_y = pltpu.roll(centre, 1, 1)
    return combine(coefs, centre, block[2:], block[:-2], plus_y, minus_y)


def lanes_of(half):
    return pl.ds(half * LANES, LANES)


def coefs_of(coef_ref, half):
    return [coef_ref[i : i + 1, lanes_of(half)] for i in range(5)]


def hidden_of(state, w1, bias):
    inputs = jnp.concatenate([part.astype(BF16) for part in state], 1)
    half = jnp.dot(inputs, w1, preferred_element_type=F32) + bias
    inner = half * (half * half * (8.0 * TANH_SCALE * TANH_CUBE) + 2.0 * TANH_SCALE)
    return (half * jnp.tanh(inner) + half).astype(BF16)


def physics(state, counts, matrices):
    w1, bias, w2, w2_last = matrices
    for index in range(3):
        delta = jnp.dot(hidden_of(state, w1, bias), w2, preferred_element_type=F32)
        parts = [delta[:, :LANES], delta[:, LANES:]]
        if index:
            needed = counts > float(index)
            parts = [jnp.where(needed, part, 0.0) for part in parts]
        state = [old + part for old, part in zip(state, parts)]
    delta = jnp.dot(hidden_of(state, w1, bias), w2_last, preferred_element_type=F32)
    lane = iota((1, LANES), 1)
    kept = jnp.where(lane == 0, state[0], pltpu.roll(state[1], 1, 1))
    return kept + jnp.where(counts > 3.0, delta, 0.0)


def expand_counts(row):
    square = (LANES, LANES)
    diagonal = jnp.where(iota(square, 0) == iota(square, 1), row, 0.0).astype(BF16)
    return jnp.dot(diagonal, jnp.ones(square, BF16), preferred_element_type=F32)


def split(row):
    high = row.astype(BF16).astype(F32)
    return high, row - high


def one_hots(cells):
    n = cells.shape[1]
    first = iota((32, n), 0) == jnp.right_shift(cells, 4)
    second = (iota((16, n), 0) == jnp.bitwise_and(cells, 15)) & (cells >= 0)
    return first, second.astype(F32).astype(BF16)


def scatter(values, first, second):
    rows = []
    for value in values:
        for part in split(value):
            rows.append(jnp.where(first, part, 0.0))
    stacked = jnp.concatenate(rows, 0).astype(BF16)
    return lax.dot_general(stacked, second, NT, preferred_element_type=F32)


def scatter_columns(kept, cells):
    n = kept.shape[0]
    rows = [jnp.transpose(kept[i : i + LANES])[:2] for i in range(0, n, LANES)]
    flat = jnp.concatenate(rows, 1)
    first, second = one_hots(cells)
    return scatter([flat[0:1], flat[1:2]], first, second)


def column_codes(idx_ref, inc_ref):
    gx = lax.axis_index("gx")
    start = pl.multiple_of((gx // 2) * LANES, LANES)
    block = inc_ref[:, pl.ds(start, LANES)].astype(F32)
    block = jnp.where(gx % 2 == 1, pltpu.roll(block, 64, 1), block)
    spread = (iota((32, 8), 0) // BS == iota((32, 8), 1)).astype(F32)
    counts = jnp.dot(spread.astype(BF16), block.astype(BF16), preferred_element_type=F32)
    cells = idx_ref[...].astype(F32)
    return jnp.concatenate([cells, jnp.zeros_like(cells)], 1) * 8.0 + counts


def group_rows(idx_ref, inc_ref, turned, cell_ref, count_ref):
    code = column_codes(idx_ref, inc_ref)
    turned[...] = jnp.transpose(jnp.concatenate([code, jnp.zeros((96, LANES), F32)], 0))
    count = GROUPS * TILES
    parts = [turned[pl.ds(2 + j, count, stride=4), :][:, :32] for j in range(4)]
    inner = jnp.concatenate(parts, 1)
    along_y = jnp.concatenate([turned[i : i + 1, :][:, :32] for i in (0, 1, 62, 63)], 1)
    along_x = [
        jnp.concatenate([code[i : i + 1, :64], code[i + 1 : i + 2, :64]], 1) for i in (0, 30)
    ]
    y = jnp.bitwise_and(iota((1, LANES), 1), 31)
    keep = (y >= 2) & (y < 30)
    whole = jnp.concatenate([inner, along_y] + along_x, 0).astype(jnp.int32)
    cells = jnp.right_shift(whole, 3)
    masked = (iota(whole.shape, 0) < count + 1) & ((y < 2) | (y >= 30))
    cell_ref[pl.ds(0, count + 3), :] = jnp.where(masked, -1, cells)
    count_ref[pl.ds(0, count + 3), :] = jnp.bitwise_and(whole, 7).astype(F32)


def row_at(ref, index):
    return ref[pl.ds(index, 1), :]


def matrices_of(w1_ref, bias_ref, w2_ref, last_ref):
    return w1_ref[...], bias_ref[...], w2_ref[...], last_ref[...]


def tile_state(air_ref, coef_ref, tile):
    state = []
    for half in range(2):
        block = air_ref[half, pl.ds(tile * (4 * GROUPS), 4 * GROUPS + 4)]
        coefs = coefs_of(coef_ref, half)
        state.append(advance(advance(block, coefs), coefs).reshape(GROUPS * LANES, LANES))
    return state


def finish(state, groups, matrices, cell_ref, count_ref):
    needs = [expand_counts(row_at(count_ref, g)) for g in groups]
    kept = physics(state, jnp.concatenate(needs, 0), matrices)
    cells = jnp.concatenate([row_at(cell_ref, g) for g in groups], 1)
    return scatter_columns(kept, cells)


def tiles(lo, hi, air_ref, coef_ref, matrix_refs, cell_ref, count_ref, acc_ref):
    @pl.loop(lo, hi)
    def _(tile):
        state = tile_state(air_ref, coef_ref, tile)
        groups = [tile * GROUPS + g for g in range(GROUPS)]
        acc_ref[...] += finish(state, groups, matrices_of(*matrix_refs), cell_ref, count_ref)


def early_tiles():
    gy = lax.axis_index("gy")
    return jnp.where(gy < 3, 1, 0).astype(jnp.int32)


def is_even(axis):
    return lax.axis_index(axis) % 2 == 0


def load_kernel(
    air_in, spread_in, east_in, north_in, land_in, inc_in, idx_in, water_in, ocean_in, driver_in,
    mixing_in, w1_in, bias_in, w2_in,
    send1_ref, send2_ref, air_ref, coef_ref, w1_ref, bias_ref, w2_ref, last_ref,
    cell_ref, count_ref, acc_ref, land_ref, idx_ref, water_ref, ocean_ref, driver_ref, mixing_ref,
    inc_ref, numbers, raw_bias, raw_w1, turned, sem,
):
    used = []

    def fetch(source, target):
        copy = pltpu.make_async_copy(source, target, sem.at[len(used)])
        copy.start()
        used.append(copy)
        return copy

    def rows(lo, size):
        return [
            fetch(
                air_in.at[:, pl.ds(lo, size), lanes_of(half)],
                air_ref.at[half, :, pl.ds(lo, size), :],
            )
            for half in range(2)
        ]

    prep = [fetch(inc_in, inc_ref), fetch(idx_in, idx_ref)]
    low = rows(0, 8)
    high = rows(24, 8)
    rest = rows(8, 16)
    rest += [
        fetch(w1_in, raw_w1),
        fetch(w2_in, w2_ref),
        fetch(bias_in, raw_bias),
        fetch(spread_in, numbers.at[pl.ds(0, 1)]),
        fetch(east_in, numbers.at[pl.ds(1, 1)]),
        fetch(north_in, numbers.at[pl.ds(2, 1)]),
        fetch(land_in, land_ref),
        fetch(water_in, water_ref),
        fetch(driver_in, driver_ref),
        fetch(mixing_in, mixing_ref),
        fetch(ocean_in, ocean_ref),
    ]
    for copy in prep:
        copy.wait()
    group_rows(idx_ref, inc_ref, turned, cell_ref, count_ref)
    acc_ref[...] = jnp.zeros_like(acc_ref)
    for copy in low + high:
        copy.wait()
    upper = jnp.where(is_even("gy"), 30, 0)
    for send, first in ((send1_ref, upper), (send2_ref, 30 - upper)):
        for half in range(2):
            flat = air_ref.at[half].reshape(64 * 32, LANES)
            for k in range(2):
                send[pl.ds(k * 64, 64), lanes_of(half)] = flat[pl.ds(first + k, 64, stride=32), :]
    for copy in rest:
        copy.wait()
    w1_ref[...] = raw_w1[...] * jnp.asarray(0.5, BF16)
    bias_ref[...] = raw_bias[...] * 0.5
    spread, east, north = (numbers[i : i + 1] for i in range(3))
    coef_ref[0:1] = 1.0 - 4.0 * spread
    coef_ref[1:2] = spread - 0.5 * east
    coef_ref[2:3] = spread + 0.5 * east
    coef_ref[3:4] = spread - 0.5 * north
    coef_ref[4:5] = spread + 0.5 * north
    lane = iota((1, LANES), 1)
    first = w2_ref[:, :LANES].astype(F32)
    second = pltpu.roll(w2_ref[:, LANES:].astype(F32), 1, 1)
    last_ref[...] = jnp.where(lane == 0, first, jnp.where(lane == 1, second, 0.0)).astype(BF16)
    matrix_refs = (w1_ref, bias_ref, w2_ref, last_ref)
    tiles(
        jnp.int32(0), early_tiles(), air_ref, coef_ref, matrix_refs, cell_ref, count_ref, acc_ref
    )


VMEM = pl.BlockSpec(memory_space=pltpu.VMEM)


def params(size):
    return pltpu.CompilerParams(vmem_limit_bytes=size << 20)


def cost(flops):
    return pl.CostEstimate(flops=flops, bytes_accessed=1 << 20, transcendentals=1 << 10)


def load(arrays):
    shapes = [
        ((LANES, 256), F32),
        ((LANES, 256), F32),
        ((2, 64, 32, LANES), F32),
        ((8, 256), F32),
        ((256, 512), BF16),
        ((1, 512), F32),
        ((512, 256), BF16),
        ((512, LANES), BF16),
        ((24, LANES), jnp.int32),
        ((24, LANES), F32),
        ((LANES, 16), F32),
        ((32, 64), F32),
        ((32, 64), jnp.int32),
        ((16, 32), jnp.int32),
        ((2, 32, 16, 80), F32),
        ((2, 16, 32), F32),
        ((80, 80), F32),
    ]
    return pl.pallas_call(
        load_kernel,
        out_shape=[jax.ShapeDtypeStruct(*shape) for shape in shapes],
        in_specs=[pl.BlockSpec(memory_space=pl.ANY)] * 14,
        out_specs=[VMEM] * len(shapes),
        scratch_shapes=[
            pltpu.VMEM((8, 1024), jnp.int32),
            pltpu.VMEM((8, 256), F32),
            pltpu.VMEM((1, 512), F32),
            pltpu.VMEM((256, 512), BF16),
            pltpu.VMEM((LANES, LANES), F32),
            pltpu.SemaphoreType.DMA((24,)),
        ],
        compiler_params=params(24),
        cost_estimate=cost(1 << 20),
    )(*[pltpu.with_memory_space_constraint(array, pltpu.HBM) for array in arrays])


def ocean_fields(water, driver_ref, ocean_ref, mixing_ref):
    levels = mixing_ref.shape[0]
    wide = jnp.concatenate([mixing_ref[...], jnp.zeros((levels, LANES - levels), F32)], 1)
    tall = jnp.concatenate([wide, jnp.zeros((LANES - levels, LANES), F32)], 0)
    turned = jnp.transpose(tall)
    column = (iota((LANES, 1), 0) == 0).astype(F32)
    total = jnp.zeros((1, 1), F32)

    def pair(_, carry):
        column, total = carry
        row = jnp.sum(column * tall, axis=0, keepdims=True)
        total = total + row[:, 0:1]
        column = jnp.sum(turned * row, axis=1, keepdims=True)
        return column, total + column[0:1]

    column, total = lax.fori_loop(0, PAIRS, pair, (column, total))
    row = jnp.transpose(jnp.broadcast_to(column, (LANES, LANES)))[0:1, :levels]
    fields = []
    for field in range(2):
        block = ocean_ref[field]
        mixed = jnp.transpose(jnp.sum(block * row, axis=2))
        mixed = mixed + (OCEAN_STEP * total) * driver_ref[field]
        fields.append(jnp.where(water == 1, mixed, jnp.transpose(block[:, :, 0])))
    return fields


def land_sums(land, cells):
    lands = jnp.concatenate([land[y : y + 1] for y in range(32)], 1)
    places = jnp.concatenate([cells[y : y + 1] for y in range(32)], 1)
    first, second = one_hots(places)
    sums = scatter([lands, jnp.tanh(lands)], first, second)
    ones = first.astype(F32).astype(BF16)
    return sums, lax.dot_general(ones, second, NT, preferred_element_type=F32)


def middle_kernel(
    air_ref, coef_ref, w1_ref, bias_ref, w2_ref, last_ref, cell_ref, count_ref, land_ref, idx_ref,
    water_ref, ocean_ref, driver_ref, mixing_ref, acc_ref, side_ref,
):
    water = water_ref[...]
    fields = ocean_fields(water, driver_ref, ocean_ref, mixing_ref)
    sums, count = land_sums(land_ref[...], idx_ref[...])
    land = jnp.transpose(sums[0:32] + sums[32:64])
    warm = jnp.transpose(sums[64:96] + sums[96:128])
    count = jnp.transpose(count)
    side_ref[0] = fields[0]
    side_ref[1] = fields[1]
    side_ref[2] = jnp.where(water == 1, count * fields[0], land)
    side_ref[3] = jnp.where(water == 1, count * jnp.tanh(fields[0]), warm)
    side_ref[4] = jnp.maximum(count, 1.0)
    acc_ref[...] = jnp.zeros_like(acc_ref)
    early = early_tiles()
    matrix_refs = (w1_ref, bias_ref, w2_ref, last_ref)
    tiles(
        early, early + 1, air_ref, coef_ref, matrix_refs, cell_ref, count_ref, acc_ref
    )


def middle(core, others):
    return pl.pallas_call(
        middle_kernel,
        out_shape=[
            jax.ShapeDtypeStruct((LANES, 16), F32),
            jax.ShapeDtypeStruct((5, 16, 32), F32),
        ],
        in_specs=[VMEM] * 14,
        out_specs=[VMEM] * 2,
        compiler_params=params(24),
        cost_estimate=cost(1 << 30),
    )(*core, *others)


def by_side(axis, first, second):
    even = is_even(axis)
    return jnp.where(even, second, first), jnp.where(even, first, second)


def slab_kernel(air_ref, recv1_ref, recv2_ref, pair_ref, cross_ref):
    even = is_even("gx")
    ylow, yhigh = by_side("gy", recv1_ref[...], recv2_ref[...])
    for half in range(2):
        lanes = lanes_of(half)
        low = air_ref[half, 0:2].reshape(64, LANES)
        high = air_ref[half, 62:64].reshape(64, LANES)
        pair_ref[0:64, lanes] = jnp.where(even, high, low)
        cross_ref[0:64, lanes] = jnp.where(even, low, high)
    low = jnp.concatenate([ylow[64:65], yhigh[0:1], jnp.zeros((6, 256), F32)], 0)
    high = jnp.concatenate([ylow[127:128], yhigh[63:64], jnp.zeros((6, 256), F32)], 0)
    pair_ref[64:72] = jnp.where(even, high, low)
    cross_ref[64:72] = jnp.where(even, low, high)


def x_slabs(air, recv1, recv2):
    return pl.pallas_call(
        slab_kernel,
        out_shape=[jax.ShapeDtypeStruct((72, 256), F32)] * 2,
        in_specs=[VMEM] * 3,
        out_specs=[VMEM] * 2,
        compiler_params=params(16),
        cost_estimate=cost(1 << 10),
    )(air, recv1, recv2)


def late_kernel(
    air_ref, coef_ref, w1_ref, bias_ref, w2_ref, last_ref, cell_ref, count_ref, acc_ref
):
    acc_ref[...] = jnp.zeros_like(acc_ref)
    matrix_refs = (w1_ref, bias_ref, w2_ref, last_ref)
    tiles(
        early_tiles() + 1, jnp.int32(TILES), air_ref, coef_ref, matrix_refs, cell_ref, count_ref,
        acc_ref,
    )


def late(core):
    return pl.pallas_call(
        late_kernel,
        out_shape=jax.ShapeDtypeStruct((LANES, 16), F32),
        in_specs=[VMEM] * 8,
        out_specs=VMEM,
        compiler_params=params(24),
        cost_estimate=cost(1 << 30),
    )(*core)


def shift_down(block, edge):
    return jnp.where(iota(block.shape, 1) == 0, edge, pltpu.roll(block, 1, 1))


def shift_up(block, edge):
    size = block.shape[1]
    return jnp.where(iota(block.shape, 1) == size - 1, edge, pltpu.roll(block, size - 1, 1))


def y_edge_state(half, air_ref, coefs, ylow, yhigh, before, after, low_corner, high_corner):
    flat = air_ref.at[half].reshape(64 * 32, LANES)

    def column(halo, corner, inner, at, low_side):
        far, near = (0, 1) if low_side else (1, 0)
        minus_y = corner[0:1] if at == 0 else halo[near, at - 1 : at]
        plus_y = corner[1:2] if at == 31 else halo[near, at + 1 : at + 2]
        centre = halo[near, at : at + 1]
        outer = halo[far, at : at + 1]
        plus_x, minus_x = (inner, outer) if low_side else (outer, inner)
        return combine(coefs, centre, plus_x, minus_x, plus_y, minus_y)

    def step(block, left, right):
        centre = block[1:-1]
        plus_x = shift_up(centre, jnp.stack(right, 0))
        minus_x = shift_down(centre, jnp.stack(left, 0))
        return combine(coefs, centre, plus_x, minus_x, block[2:], block[:-2])

    states = []
    for low in (True, False):
        ys = range(4) if low else range(28, 32)
        own = jnp.stack([flat[pl.ds(y, 64, stride=32), :] for y in ys], 0)
        if low:
            block = jnp.concatenate([ylow, own], 0)
            left = [low_corner[0:1]] + [before[1, y : y + 1] for y in (0, 1, 2)]
            right = [high_corner[0:1]] + [after[0, y : y + 1] for y in (0, 1, 2)]
            targets = (0, 1)
        else:
            block = jnp.concatenate([own, yhigh], 0)
            left = [before[1, y : y + 1] for y in (29, 30, 31)] + [low_corner[1:2]]
            right = [after[0, y : y + 1] for y in (29, 30, 31)] + [high_corner[1:2]]
            targets = (30, 31)
        block = step(block, left, right)
        left = [column(before, low_corner, air_ref[half, 0, y : y + 1, :], y, True) for y in targets]
        right = [
            column(after, high_corner, air_ref[half, 63, y : y + 1, :], y, False) for y in targets
        ]
        states.append(step(block, left, right).reshape(LANES, LANES))
    return jnp.concatenate(states, 0)


def x_edge_state(half, air_ref, coefs, before, after):
    low = jnp.concatenate([before, air_ref[half, 0:4]], 0)
    high = jnp.concatenate([air_ref[half, 60:64], after], 0)
    ends = [advance(advance(block, coefs), coefs).reshape(64, LANES) for block in (low, high)]
    return jnp.concatenate(ends, 0)


def edge_kernel(
    air_ref, coef_ref, w1_ref, bias_ref, w2_ref, last_ref, cell_ref, count_ref, recv1_ref,
    recv2_ref, pair_ref, cross_ref, side_ref, acc0_ref, acc1_ref, acc2_ref, out_ref,
):
    state = []
    for half in range(2):
        lanes = lanes_of(half)
        coefs = coefs_of(coef_ref, half)
        ylow, yhigh = by_side("gy", recv1_ref[:, lanes], recv2_ref[:, lanes])
        xlow, xhigh = by_side("gx", pair_ref[:, lanes], cross_ref[:, lanes])
        before = xlow[:64].reshape(2, 32, LANES)
        after = xhigh[:64].reshape(2, 32, LANES)
        by_x = y_edge_state(
            half,
            air_ref,
            coefs,
            ylow.reshape(2, 64, LANES),
            yhigh.reshape(2, 64, LANES),
            before,
            after,
            xlow[64:66],
            xhigh[64:66],
        )
        by_y = x_edge_state(half, air_ref, coefs, before, after)
        state.append(jnp.concatenate([by_y, by_x], 0))
    groups = [GROUPS * TILES + g for g in range(3)]
    matrices = matrices_of(w1_ref, bias_ref, w2_ref, last_ref)
    acc = finish(state, groups, matrices, cell_ref, count_ref)
    acc = acc + (acc0_ref[...] + acc1_ref[...] + acc2_ref[...])
    heat = jnp.transpose(acc[0:32] + acc[32:64])
    vapour = jnp.transpose(acc[64:96] + acc[96:128])
    below = side_ref[4]
    ocean = lax.axis_index("sect") == 1
    flux = THERMAL_FACTOR * (side_ref[2] - heat) / below
    out_ref[0] = jnp.where(ocean, side_ref[0], flux)
    flux = WETNESS_FACTOR * (side_ref[3] - vapour) / below
    out_ref[1] = jnp.where(ocean, side_ref[1], flux)


def edges(core, halos, others):
    return pl.pallas_call(
        edge_kernel,
        out_shape=jax.ShapeDtypeStruct((2, 16, 32), F32),
        in_specs=[VMEM] * 16,
        out_specs=VMEM,
        compiler_params=params(24),
        cost_estimate=cost(1 << 28),
    )(*core, *halos, *others)


def exchanges(axis, first):
    sizes = [lax.axis_size(name) for name in AXES]
    size = lax.axis_size(axis)
    pairs = []
    for device in range(sizes[0] * sizes[1] * sizes[2]):
        at = [device // (sizes[1] * sizes[2]), device // sizes[2] % sizes[1], device % sizes[2]]
        dim = AXES.index(axis)
        step = 1 if (at[dim] - first) % 2 == 0 else -1
        at[dim] = (at[dim] + step) % size
        pairs.append((device, (at[0] * sizes[1] + at[1]) * sizes[2] + at[2]))
    return pairs


def shards(
    air_profile_matrix,
    spreading_numbers,
    eastward_advection_number,
    northward_advection_number,
    landmass_warmth,
    physics_increments,
    underlying_water_index,
    water_indicator,
    waterbody_profiles,
    waterbody_drivers,
    inverted_blending_matrix,
    entry_layer_matrix,
    entry_layer_offset,
    exit_layer_matrix,
):
    loaded = load(
        (
            air_profile_matrix,
            spreading_numbers.reshape(1, -1),
            eastward_advection_number.reshape(1, -1),
            northward_advection_number.reshape(1, -1),
            landmass_warmth.T,
            physics_increments.T,
            underlying_water_index.T,
            water_indicator.T,
            waterbody_profiles.transpose(0, 2, 3, 1),
            waterbody_drivers.transpose(0, 2, 1),
            inverted_blending_matrix,
            entry_layer_matrix,
            entry_layer_offset.reshape(1, -1),
            exit_layer_matrix,
        )
    )
    send1, send2 = loaded[:2]
    core = loaded[2:10]
    acc0 = loaded[10]
    recv1 = lax.ppermute(send1, AXES, exchanges("gy", 0))
    recv2 = lax.ppermute(send2, AXES, exchanges("gy", 1))
    acc1, sides = middle(core, loaded[11:])
    acc1, recv1, recv2 = lax.optimization_barrier((acc1, recv1, recv2))
    send_pair, send_cross = x_slabs(core[0], recv1, recv2)
    cross = lax.ppermute(send_cross, AXES, exchanges("gx", 1))
    pair = lax.ppermute(send_pair, AXES, exchanges("gx", 0))
    acc2 = late(core)
    acc2, pair, cross = lax.optimization_barrier((acc2, pair, cross))
    result = edges(core, (recv1, recv2, pair, cross), (sides, acc0, acc1, acc2))
    return result.transpose(0, 2, 1)[None]


def solution(mesh):
    in_specs = (
        P("gx", "gy", None),
        P(),
        P(),
        P(),
        P("gx", "gy"),
        P(None, "gy"),
        P("gx", "gy"),
        P("gx", "gy"),
        P(None, None, "gx", "gy"),
        P(None, "gx", "gy"),
        P(),
        P(),
        P(),
        P(),
    )
    out_specs = P("sect", None, "gx", "gy")
    return jax.shard_map(shards, mesh=mesh, in_specs=in_specs, out_specs=out_specs, check_vma=False)
```

```python
import jax
import jax.numpy as jnp
from jax import lax
from jax.experimental import pallas as pl
from jax.experimental.pallas import tpu as pltpu
from jax.sharding import PartitionSpec as P

BS = 4
PAIRS = 6
THERMAL_FACTOR = 0.8
WETNESS_FACTOR = 0.6
OCEAN_STEP = 0.1
TANH_SCALE = 0.7978845608028654
TANH_CUBE = 0.044715

GROUPS = 5
TILES = 3
TILE_CHUNKS = (320, 320)
EDGE_CHUNKS = (384,)
LANES = 128
NT = (((1,), (1,)), ((), ()))
F32 = jnp.float32
BF16 = jnp.bfloat16
AXES = ("sect", "gx", "gy")


def iota(shape, dim):
    return lax.broadcasted_iota(jnp.int32, shape, dim)


def combine(coefs, centre, plus_x, minus_x, plus_y, minus_y):
    c0, cxp, cxm, cyp, cym = coefs
    return c0 * centre + cxp * plus_x + cxm * minus_x + cyp * plus_y + cym * minus_y


def advance(block, coefs):
    centre = block[1:-1]
    size = centre.shape[1]
    plus_y = pltpu.roll(centre, size - 1, 1)
    minus_y = pltpu.roll(centre, 1, 1)
    return combine(coefs, centre, block[2:], block[:-2], plus_y, minus_y)


def lanes_of(half):
    return pl.ds(half * LANES, LANES)


def coefs_of(coef_ref, half):
    return [coef_ref[i : i + 1, lanes_of(half)] for i in range(5)]


def hidden_of(state, w1, bias):
    inputs = jnp.concatenate([part.astype(BF16) for part in state], 1)
    half = jnp.dot(inputs, w1, preferred_element_type=F32) + bias
    inner = half * (half * half * (8.0 * TANH_SCALE * TANH_CUBE) + 2.0 * TANH_SCALE)
    return (half * jnp.tanh(inner) + half).astype(BF16)


def physics(state, counts, matrices, sizes):
    w1, bias, w2, w2_last = matrices
    places = [sum(sizes[:i]) for i in range(len(sizes))]
    states = [[part[at : at + n] for part in state] for at, n in zip(places, sizes)]
    counts = [counts[at : at + n] for at, n in zip(places, sizes)]
    lane = iota((1, LANES), 1)
    for index in range(3):
        for chunk, needs in enumerate(counts):
            hidden = hidden_of(states[chunk], w1, bias)
            delta = jnp.dot(hidden, w2, preferred_element_type=F32)
            parts = [delta[:, :LANES], delta[:, LANES:]]
            if index:
                needed = needs > float(index)
                parts = [jnp.where(needed, part, 0.0) for part in parts]
            states[chunk] = [old + part for old, part in zip(states[chunk], parts)]
    kept = []
    for (first, second), needs in zip(states, counts):
        hidden = hidden_of([first, second], w1, bias)
        delta = jnp.dot(hidden, w2_last, preferred_element_type=F32)
        both = jnp.where(lane == 0, first, pltpu.roll(second, 1, 1))
        kept.append(both + jnp.where(needs > 3.0, delta, 0.0))
    return jnp.concatenate(kept, 0)


def expand_counts(row):
    square = (LANES, LANES)
    diagonal = jnp.where(iota(square, 0) == iota(square, 1), row, 0.0).astype(BF16)
    return jnp.dot(diagonal, jnp.ones(square, BF16), preferred_element_type=F32)


def split(row):
    high = row.astype(BF16).astype(F32)
    return high, row - high


def one_hots(cells):
    n = cells.shape[1]
    first = iota((32, n), 0) == jnp.right_shift(cells, 4)
    second = (iota((16, n), 0) == jnp.bitwise_and(cells, 15)) & (cells >= 0)
    return first, second.astype(F32).astype(BF16)


def scatter(values, first, second):
    rows = []
    for value in values:
        for part in split(value):
            rows.append(jnp.where(first, part, 0.0))
    stacked = jnp.concatenate(rows, 0).astype(BF16)
    return lax.dot_general(stacked, second, NT, preferred_element_type=F32)


def scatter_columns(kept, cells):
    n = kept.shape[0]
    rows = [jnp.transpose(kept[i : i + LANES])[:2] for i in range(0, n, LANES)]
    flat = jnp.concatenate(rows, 1)
    first, second = one_hots(cells)
    return scatter([flat[0:1], flat[1:2]], first, second)


def column_codes(idx_ref, inc_ref):
    gx = lax.axis_index("gx")
    start = pl.multiple_of((gx // 2) * LANES, LANES)
    block = inc_ref[:, pl.ds(start, LANES)].astype(F32)
    block = jnp.where(gx % 2 == 1, pltpu.roll(block, 64, 1), block)
    spread = (iota((32, 8), 0) // BS == iota((32, 8), 1)).astype(F32)
    counts = jnp.dot(spread.astype(BF16), block.astype(BF16), preferred_element_type=F32)
    cells = idx_ref[...].astype(F32)
    return jnp.concatenate([cells, jnp.zeros_like(cells)], 1) * 8.0 + counts


def group_rows(idx_ref, inc_ref, turned, cell_ref, count_ref):
    code = column_codes(idx_ref, inc_ref)
    turned[...] = jnp.transpose(jnp.concatenate([code, jnp.zeros((96, LANES), F32)], 0))
    count = GROUPS * TILES
    parts = [turned[pl.ds(2 + j, count, stride=4), :][:, :32] for j in range(4)]
    inner = jnp.concatenate(parts, 1)
    along_y = jnp.concatenate([turned[i : i + 1, :][:, :32] for i in (0, 1, 62, 63)], 1)
    along_x = [
        jnp.concatenate([code[i : i + 1, :64], code[i + 1 : i + 2, :64]], 1) for i in (0, 30)
    ]
    whole = jnp.concatenate([inner] + along_x + [along_y], 0).astype(jnp.int32)
    cells = jnp.right_shift(whole, 3)
    row = iota(whole.shape, 0)
    place = jnp.bitwise_and(iota(whole.shape, 1), jnp.where(row < count, 31, 63))
    masked = (place < 2) | (place >= jnp.where(row < count, 30, 62))
    masked = masked & (row < count + 2)
    cell_ref[pl.ds(0, count + 3), :] = jnp.where(masked, -1, cells)
    count_ref[pl.ds(0, count + 3), :] = jnp.bitwise_and(whole, 7).astype(F32)


def row_at(ref, index):
    return ref[pl.ds(index, 1), :]


def matrices_of(w1_ref, bias_ref, w2_ref, last_ref):
    return w1_ref[...], bias_ref[...], w2_ref[...], last_ref[...]


def tile_state(air_ref, coef_ref, tile):
    state = []
    for half in range(2):
        block = air_ref[half, pl.ds(tile * (4 * GROUPS), 4 * GROUPS + 4)]
        coefs = coefs_of(coef_ref, half)
        state.append(advance(advance(block, coefs), coefs).reshape(GROUPS * LANES, LANES))
    return state


def finish(state, groups, matrices, cell_ref, count_ref, sizes):
    needs = [expand_counts(row_at(count_ref, g)) for g in groups]
    kept = physics(state, jnp.concatenate(needs, 0), matrices, sizes)
    cells = jnp.concatenate([row_at(cell_ref, g) for g in groups], 1)
    return scatter_columns(kept, cells)


def tiles(lo, hi, air_ref, coef_ref, matrix_refs, cell_ref, count_ref, acc_ref):
    @pl.loop(lo, hi)
    def _(tile):
        state = tile_state(air_ref, coef_ref, tile)
        groups = [tile * GROUPS + g for g in range(GROUPS)]
        matrices = matrices_of(*matrix_refs)
        acc_ref[...] += finish(state, groups, matrices, cell_ref, count_ref, TILE_CHUNKS)


def early_tiles():
    gy = lax.axis_index("gy")
    return jnp.where(gy < 4, 1, 0).astype(jnp.int32)


def middle_tiles():
    late = lax.axis_index("gy") >= 4
    return jnp.where(late & (lax.axis_index("gx") % 8 == 1), 2, 1).astype(jnp.int32)


def is_even(axis):
    return lax.axis_index(axis) % 2 == 0


def side_turn():
    gy = lax.axis_index("gy")
    return jnp.where(gy == 0, 0, 1)


def load_kernel(
    air_in, spread_in, east_in, north_in, land_in, inc_in, idx_in, water_in, ocean_in, driver_in,
    mixing_in, w1_in, bias_in, w2_in,
    send1_ref, send2_ref, air_ref, coef_ref, w1_ref, bias_ref, w2_ref, last_ref,
    cell_ref, count_ref, acc_ref, side_ref, land_ref, idx_ref, water_ref, ocean_ref, driver_ref,
    mixing_ref, inc_ref, numbers, raw_bias, raw_w1, turned, sem,
):
    used = []

    def fetch(source, target):
        copy = pltpu.make_async_copy(source, target, sem.at[len(used)])
        copy.start()
        used.append(copy)
        return copy

    def rows(lo, size):
        return [
            fetch(
                air_in.at[:, pl.ds(lo, size), lanes_of(half)],
                air_ref.at[half, :, pl.ds(lo, size), :],
            )
            for half in range(2)
        ]

    prep = [fetch(inc_in, inc_ref), fetch(idx_in, idx_ref)]
    low = rows(0, 8)
    high = rows(24, 8)
    layers = [
        fetch(w1_in, raw_w1),
        fetch(w2_in, w2_ref),
        fetch(bias_in, raw_bias),
        fetch(spread_in, numbers.at[pl.ds(0, 1)]),
        fetch(east_in, numbers.at[pl.ds(1, 1)]),
        fetch(north_in, numbers.at[pl.ds(2, 1)]),
    ]
    rest = rows(8, 16)
    rest += [
        fetch(land_in, land_ref),
        fetch(water_in, water_ref),
        fetch(driver_in, driver_ref),
        fetch(mixing_in, mixing_ref),
        fetch(ocean_in, ocean_ref),
    ]
    acc_ref[...] = jnp.zeros_like(acc_ref)
    for copy in prep:
        copy.wait()
    group_rows(idx_ref, inc_ref, turned, cell_ref, count_ref)
    for copy in low + high:
        copy.wait()
    upper = jnp.where(is_even("gy"), 30, 0)
    for send, first in ((send1_ref, upper), (send2_ref, 30 - upper)):
        for half in range(2):
            flat = air_ref.at[half].reshape(64 * 32, LANES)
            for k in range(2):
                send[pl.ds(k * 64, 64), lanes_of(half)] = flat[pl.ds(first + k, 64, stride=32), :]
    for copy in layers:
        copy.wait()
    w1_ref[...] = raw_w1[...] * jnp.asarray(0.5, BF16)
    bias_ref[...] = raw_bias[...] * 0.5
    spread, east, north = (numbers[i : i + 1] for i in range(3))
    coef_ref[0:1] = 1.0 - 4.0 * spread
    coef_ref[1:2] = spread - 0.5 * east
    coef_ref[2:3] = spread + 0.5 * east
    coef_ref[3:4] = spread - 0.5 * north
    coef_ref[4:5] = spread + 0.5 * north
    lane = iota((1, LANES), 1)
    first = w2_ref[:, :LANES].astype(F32)
    second = pltpu.roll(w2_ref[:, LANES:].astype(F32), 1, 1)
    last_ref[...] = jnp.where(lane == 0, first, jnp.where(lane == 1, second, 0.0)).astype(BF16)
    for copy in rest:
        copy.wait()
    side_refs = (land_ref, idx_ref, water_ref, ocean_ref, driver_ref, mixing_ref)
    side_parts(0, side_refs, side_ref)
    matrix_refs = (w1_ref, bias_ref, w2_ref, last_ref)
    tiles(
        jnp.int32(0), early_tiles(), air_ref, coef_ref, matrix_refs, cell_ref, count_ref, acc_ref
    )


VMEM = pl.BlockSpec(memory_space=pltpu.VMEM)


def params(size):
    return pltpu.CompilerParams(vmem_limit_bytes=size << 20)


def cost(flops):
    return pl.CostEstimate(flops=flops, bytes_accessed=1 << 20, transcendentals=1 << 10)


def load(arrays):
    shapes = [
        ((LANES, 256), F32),
        ((LANES, 256), F32),
        ((2, 64, 32, LANES), F32),
        ((8, 256), F32),
        ((256, 512), BF16),
        ((1, 512), F32),
        ((512, 256), BF16),
        ((512, LANES), BF16),
        ((24, LANES), jnp.int32),
        ((24, LANES), F32),
        ((LANES, 16), F32),
        ((5, 16, 32), F32),
        ((32, 64), F32),
        ((32, 64), jnp.int32),
        ((16, 32), jnp.int32),
        ((2, 32, 16, 80), F32),
        ((2, 16, 32), F32),
        ((80, 80), F32),
    ]
    return pl.pallas_call(
        load_kernel,
        out_shape=[jax.ShapeDtypeStruct(*shape) for shape in shapes],
        in_specs=[pl.BlockSpec(memory_space=pl.ANY)] * 14,
        out_specs=[VMEM] * len(shapes),
        scratch_shapes=[
            pltpu.VMEM((8, 1024), jnp.int32),
            pltpu.VMEM((8, 256), F32),
            pltpu.VMEM((1, 512), F32),
            pltpu.VMEM((256, 512), BF16),
            pltpu.VMEM((LANES, LANES), F32),
            pltpu.SemaphoreType.DMA((24,)),
        ],
        compiler_params=params(24),
        cost_estimate=cost(1 << 20),
    )(*[pltpu.with_memory_space_constraint(array, pltpu.HBM) for array in arrays])


def ocean_fields(water, driver_ref, ocean_ref, mixing_ref):
    levels = mixing_ref.shape[0]
    wide = jnp.concatenate([mixing_ref[...], jnp.zeros((levels, LANES - levels), F32)], 1)
    tall = jnp.concatenate([wide, jnp.zeros((LANES - levels, LANES), F32)], 0)
    turned = jnp.transpose(tall)
    column = (iota((LANES, 1), 0) == 0).astype(F32)
    total = jnp.zeros((1, 1), F32)

    def pair(_, carry):
        column, total = carry
        row = jnp.sum(column * tall, axis=0, keepdims=True)
        total = total + row[:, 0:1]
        column = jnp.sum(turned * row, axis=1, keepdims=True)
        return column, total + column[0:1]

    column, total = lax.fori_loop(0, PAIRS, pair, (column, total))
    row = jnp.transpose(jnp.broadcast_to(column, (LANES, LANES)))[0:1, :levels]
    fields = []
    for field in range(2):
        block = ocean_ref[field]
        mixed = jnp.transpose(jnp.sum(block * row, axis=2))
        mixed = mixed + (OCEAN_STEP * total) * driver_ref[field]
        fields.append(jnp.where(water == 1, mixed, jnp.transpose(block[:, :, 0])))
    return fields


def land_sums(land, cells):
    lands = jnp.concatenate([land[y : y + 1] for y in range(32)], 1)
    places = jnp.concatenate([cells[y : y + 1] for y in range(32)], 1)
    first, second = one_hots(places)
    sums = scatter([lands, jnp.tanh(lands)], first, second)
    ones = first.astype(F32).astype(BF16)
    return sums, lax.dot_general(ones, second, NT, preferred_element_type=F32)


def side_parts(turn, refs, side_ref):
    land_ref, idx_ref, water_ref, ocean_ref, driver_ref, mixing_ref = refs

    @pl.when(side_turn() == turn)
    def _():
        water = water_ref[...]
        fields = ocean_fields(water, driver_ref, ocean_ref, mixing_ref)
        sums, count = land_sums(land_ref[...], idx_ref[...])
        land = jnp.transpose(sums[0:32] + sums[32:64])
        warm = jnp.transpose(sums[64:96] + sums[96:128])
        count = jnp.transpose(count)
        side_ref[0] = fields[0]
        side_ref[1] = fields[1]
        side_ref[2] = jnp.where(water == 1, count * fields[0], land)
        side_ref[3] = jnp.where(water == 1, count * jnp.tanh(fields[0]), warm)
        side_ref[4] = jnp.maximum(count, 1.0)


def middle_kernel(
    air_ref, coef_ref, w1_ref, bias_ref, w2_ref, last_ref, cell_ref, count_ref, land_ref, idx_ref,
    water_ref, ocean_ref, driver_ref, mixing_ref, acc_ref, side_ref,
):
    side_refs = (land_ref, idx_ref, water_ref, ocean_ref, driver_ref, mixing_ref)
    side_parts(1, side_refs, side_ref)
    acc_ref[...] = jnp.zeros_like(acc_ref)
    early = early_tiles()
    matrix_refs = (w1_ref, bias_ref, w2_ref, last_ref)
    tiles(early, early + middle_tiles(), air_ref, coef_ref, matrix_refs, cell_ref, count_ref, acc_ref)


def middle(core, others):
    return pl.pallas_call(
        middle_kernel,
        out_shape=[
            jax.ShapeDtypeStruct((LANES, 16), F32),
            jax.ShapeDtypeStruct((5, 16, 32), F32),
        ],
        in_specs=[VMEM] * 14,
        out_specs=[VMEM] * 2,
        compiler_params=params(24),
        cost_estimate=cost(1 << 30),
    )(*core, *others)


def by_side(axis, first, second):
    even = is_even(axis)
    return jnp.where(even, second, first), jnp.where(even, first, second)


def slab_kernel(air_ref, recv1_ref, recv2_ref, pair_ref, cross_ref):
    even = is_even("gx")
    ylow, yhigh = by_side("gy", recv1_ref[...], recv2_ref[...])
    for half in range(2):
        lanes = lanes_of(half)
        low = air_ref[half, 0:2].reshape(64, LANES)
        high = air_ref[half, 62:64].reshape(64, LANES)
        pair_ref[0:64, lanes] = jnp.where(even, high, low)
        cross_ref[0:64, lanes] = jnp.where(even, low, high)
    low = jnp.concatenate([ylow[64:65], yhigh[0:1], jnp.zeros((6, 256), F32)], 0)
    high = jnp.concatenate([ylow[127:128], yhigh[63:64], jnp.zeros((6, 256), F32)], 0)
    pair_ref[64:72] = jnp.where(even, high, low)
    cross_ref[64:72] = jnp.where(even, low, high)


def x_slabs(air, recv1, recv2):
    return pl.pallas_call(
        slab_kernel,
        out_shape=[jax.ShapeDtypeStruct((72, 256), F32)] * 2,
        in_specs=[VMEM] * 3,
        out_specs=[VMEM] * 2,
        compiler_params=params(16),
        cost_estimate=cost(1 << 10),
    )(air, recv1, recv2)


def late_kernel(
    air_ref, coef_ref, w1_ref, bias_ref, w2_ref, last_ref, cell_ref, count_ref, acc_ref
):
    acc_ref[...] = jnp.zeros_like(acc_ref)
    matrix_refs = (w1_ref, bias_ref, w2_ref, last_ref)
    first = early_tiles() + middle_tiles()
    tiles(first, jnp.int32(TILES), air_ref, coef_ref, matrix_refs, cell_ref, count_ref, acc_ref)


def late(core):
    return pl.pallas_call(
        late_kernel,
        out_shape=jax.ShapeDtypeStruct((LANES, 16), F32),
        in_specs=[VMEM] * 8,
        out_specs=VMEM,
        compiler_params=params(24),
        cost_estimate=cost(1 << 30),
    )(*core)


def y_edge_state(half, air_ref, coefs, ylow, yhigh):
    flat = air_ref.at[half].reshape(64 * 32, LANES)

    def step(block):
        centre = block[1:-1]
        plus_x = pltpu.roll(centre, 63, 1)
        minus_x = pltpu.roll(centre, 1, 1)
        return combine(coefs, centre, plus_x, minus_x, block[2:], block[:-2])

    states = []
    for low in (True, False):
        ys = range(4) if low else range(28, 32)
        own = jnp.stack([flat[pl.ds(y, 64, stride=32), :] for y in ys], 0)
        halo = (ylow if low else yhigh).reshape(2, 64, LANES)
        block = jnp.concatenate([halo, own] if low else [own, halo], 0)
        states.append(step(step(block)).reshape(LANES, LANES))
    return states


def x_edge_state(half, air_ref, coefs, ylow, yhigh, xlow, xhigh):
    def with_ends(row, first, last):
        at = iota(row.shape, 0)
        size = row.shape[0]
        plus_y = jnp.where(at == size - 1, last, pltpu.roll(row, size - 1, 0))
        minus_y = jnp.where(at == 0, first, pltpu.roll(row, 1, 0))
        return plus_y, minus_y

    def own(x):
        return air_ref[half, x]

    def beyond(x, y):
        slab = ylow if y < 0 else yhigh
        at = (y + 2 if y < 0 else y - 32) * 64 + x
        return slab[at : at + 1]

    done = []
    for low in (True, False):
        halo = xlow if low else xhigh
        near, far = (halo[32:64], halo[0:32]) if low else (halo[0:32], halo[32:64])
        xs = [0, 1, 2, 3] if low else [63, 62, 61, 60]
        rows = [far, near] + [own(x) for x in xs]
        ends = [None, (halo[64:65], halo[65:66])] + [(beyond(x, -1), beyond(x, 32)) for x in xs]
        outer = [None, None] + [(beyond(x, -2), beyond(x, 33)) for x in xs]

        def apply(centre, outward, inward, plus_y, minus_y):
            plus_x, minus_x = (inward, outward) if low else (outward, inward)
            return combine(coefs, centre, plus_x, minus_x, plus_y, minus_y)

        once = {}
        for i in range(1, 5):
            plus_y, minus_y = with_ends(rows[i], *ends[i])
            once[i] = apply(rows[i], rows[i - 1], rows[i + 1], plus_y, minus_y)
        twice = []
        for i in (2, 3):
            first = apply(
                ends[i][0], ends[i - 1][0], ends[i + 1][0], rows[i][0:1], outer[i][0]
            )
            last = apply(
                ends[i][1], ends[i - 1][1], ends[i + 1][1], outer[i][1], rows[i][31:32]
            )
            plus_y, minus_y = with_ends(once[i], first, last)
            twice.append(apply(once[i], once[i - 1], once[i + 1], plus_y, minus_y))
        done += twice if low else twice[::-1]
    return jnp.concatenate(done, 0)


def edge_kernel(
    air_ref, coef_ref, w1_ref, bias_ref, w2_ref, last_ref, cell_ref, count_ref, recv1_ref,
    recv2_ref, pair_ref, cross_ref, acc0_ref, acc1_ref, acc2_ref, side0_ref, side1_ref,
    out_ref,
):
    state = []
    for half in range(2):
        lanes = lanes_of(half)
        ylow, yhigh = by_side("gy", recv1_ref[:, lanes], recv2_ref[:, lanes])
        xlow, xhigh = by_side("gx", pair_ref[:, lanes], cross_ref[:, lanes])
        coefs = coefs_of(coef_ref, half)
        along_x = y_edge_state(half, air_ref, coefs, ylow, yhigh)
        along_y = x_edge_state(half, air_ref, coefs, ylow, yhigh, xlow, xhigh)
        state.append(jnp.concatenate(along_x + [along_y], 0))
    matrices = matrices_of(w1_ref, bias_ref, w2_ref, last_ref)
    groups = [GROUPS * TILES + g for g in range(3)]
    acc = finish(state, groups, matrices, cell_ref, count_ref, EDGE_CHUNKS)
    acc = acc + (acc0_ref[...] + acc1_ref[...] + acc2_ref[...])
    heat = jnp.transpose(acc[0:32] + acc[32:64])
    vapour = jnp.transpose(acc[64:96] + acc[96:128])
    turn = side_turn()

    def side(index):
        return jnp.where(turn == 0, side0_ref[index], side1_ref[index])

    below = side(4)
    ocean = lax.axis_index("sect") == 1
    flux = THERMAL_FACTOR * (side(2) - heat) / below
    out_ref[0] = jnp.where(ocean, side(0), flux)
    flux = WETNESS_FACTOR * (side(3) - vapour) / below
    out_ref[1] = jnp.where(ocean, side(1), flux)


def edges(core, halos, others):
    return pl.pallas_call(
        edge_kernel,
        out_shape=jax.ShapeDtypeStruct((2, 16, 32), F32),
        in_specs=[VMEM] * 17,
        out_specs=VMEM,
        compiler_params=params(24),
        cost_estimate=cost(1 << 28),
    )(*core, *halos, *others)


def exchanges(axis, first):
    sizes = [lax.axis_size(name) for name in AXES]
    size = lax.axis_size(axis)
    pairs = []
    for device in range(sizes[0] * sizes[1] * sizes[2]):
        at = [device // (sizes[1] * sizes[2]), device // sizes[2] % sizes[1], device % sizes[2]]
        dim = AXES.index(axis)
        step = 1 if (at[dim] - first) % 2 == 0 else -1
        at[dim] = (at[dim] + step) % size
        pairs.append((device, (at[0] * sizes[1] + at[1]) * sizes[2] + at[2]))
    return pairs


def shards(
    air_profile_matrix,
    spreading_numbers,
    eastward_advection_number,
    northward_advection_number,
    landmass_warmth,
    physics_increments,
    underlying_water_index,
    water_indicator,
    waterbody_profiles,
    waterbody_drivers,
    inverted_blending_matrix,
    entry_layer_matrix,
    entry_layer_offset,
    exit_layer_matrix,
):
    loaded = load(
        (
            air_profile_matrix,
            spreading_numbers.reshape(1, -1),
            eastward_advection_number.reshape(1, -1),
            northward_advection_number.reshape(1, -1),
            landmass_warmth.T,
            physics_increments.T,
            underlying_water_index.T,
            water_indicator.T,
            waterbody_profiles.transpose(0, 2, 3, 1),
            waterbody_drivers.transpose(0, 2, 1),
            inverted_blending_matrix,
            entry_layer_matrix,
            entry_layer_offset.reshape(1, -1),
            exit_layer_matrix,
        )
    )
    send1, send2 = loaded[:2]
    core = loaded[2:10]
    acc0, side0 = loaded[10:12]
    recv1 = lax.ppermute(send1, AXES, exchanges("gy", 0))
    recv2 = lax.ppermute(send2, AXES, exchanges("gy", 1))
    acc1, side1 = middle(core, loaded[12:])
    acc1, recv1, recv2 = lax.optimization_barrier((acc1, recv1, recv2))
    send_pair, send_cross = x_slabs(core[0], recv1, recv2)
    cross = lax.ppermute(send_cross, AXES, exchanges("gx", 1))
    pair = lax.ppermute(send_pair, AXES, exchanges("gx", 0))
    acc2 = late(core)
    acc2, cross, pair = lax.optimization_barrier((acc2, cross, pair))
    result = edges(
        core, (recv1, recv2, pair, cross), (acc0, acc1, acc2, side0, side1)
    )
    return result.transpose(0, 2, 1)[None]


def solution(mesh):
    in_specs = (
        P("gx", "gy", None),
        P(),
        P(),
        P(),
        P("gx", "gy"),
        P(None, "gy"),
        P("gx", "gy"),
        P("gx", "gy"),
        P(None, None, "gx", "gy"),
        P(None, "gx", "gy"),
        P(),
        P(),
        P(),
        P(),
    )
    out_specs = P("sect", None, "gx", "gy")
    return jax.shard_map(shards, mesh=mesh, in_specs=in_specs, out_specs=out_specs, check_vma=False)
```

```python
import jax
import jax.numpy as jnp
from jax import lax
from jax.experimental import pallas as pl
from jax.experimental.pallas import tpu as pltpu
from jax.sharding import PartitionSpec as P

BS = 4
PAIRS = 6
THERMAL_FACTOR = 0.8
WETNESS_FACTOR = 0.6
OCEAN_STEP = 0.1
TANH_SCALE = 0.7978845608028654
TANH_CUBE = 0.044715

GROUPS = 5
TILES = 3
TILE_CHUNKS = (320, 320)
EDGE_CHUNKS = (384,)
LANES = 128
NT = (((1,), (1,)), ((), ()))
F32 = jnp.float32
BF16 = jnp.bfloat16
AXES = ("sect", "gx", "gy")


def iota(shape, dim):
    return lax.broadcasted_iota(jnp.int32, shape, dim)


def combine(coefs, centre, plus_x, minus_x, plus_y, minus_y):
    c0, cxp, cxm, cyp, cym = coefs
    return c0 * centre + cxp * plus_x + cxm * minus_x + cyp * plus_y + cym * minus_y


def advance(block, coefs):
    centre = block[1:-1]
    size = centre.shape[1]
    plus_y = pltpu.roll(centre, size - 1, 1)
    minus_y = pltpu.roll(centre, 1, 1)
    return combine(coefs, centre, block[2:], block[:-2], plus_y, minus_y)


def lanes_of(half):
    return pl.ds(half * LANES, LANES)


def coefs_of(coef_ref, half):
    return [coef_ref[i : i + 1, lanes_of(half)] for i in range(5)]


def hidden_of(state, w1, bias):
    inputs = jnp.concatenate([part.astype(BF16) for part in state], 1)
    half = jnp.dot(inputs, w1, preferred_element_type=F32) + bias
    inner = half * (half * half * (8.0 * TANH_SCALE * TANH_CUBE) + 2.0 * TANH_SCALE)
    return (half * jnp.tanh(inner) + half).astype(BF16)


def physics(state, counts, matrices, sizes):
    w1, bias, w2, w2_last = matrices
    places = [sum(sizes[:i]) for i in range(len(sizes))]
    states = [[part[at : at + n] for part in state] for at, n in zip(places, sizes)]
    counts = [counts[at : at + n] for at, n in zip(places, sizes)]
    lane = iota((1, LANES), 1)
    for index in range(3):
        for chunk, needs in enumerate(counts):
            hidden = hidden_of(states[chunk], w1, bias)
            delta = jnp.dot(hidden, w2, preferred_element_type=F32)
            parts = [delta[:, :LANES], delta[:, LANES:]]
            if index:
                needed = needs > float(index)
                parts = [jnp.where(needed, part, 0.0) for part in parts]
            states[chunk] = [old + part for old, part in zip(states[chunk], parts)]
    kept = []
    for (first, second), needs in zip(states, counts):
        hidden = hidden_of([first, second], w1, bias)
        delta = jnp.dot(hidden, w2_last, preferred_element_type=F32)
        both = jnp.where(lane == 0, first, pltpu.roll(second, 1, 1))
        kept.append(both + jnp.where(needs > 3.0, delta, 0.0))
    return jnp.concatenate(kept, 0)


def expand_counts(row):
    square = (LANES, LANES)
    diagonal = jnp.where(iota(square, 0) == iota(square, 1), row, 0.0).astype(BF16)
    return jnp.dot(diagonal, jnp.ones(square, BF16), preferred_element_type=F32)


def split(row):
    high = row.astype(BF16).astype(F32)
    return high, row - high


def one_hots(cells):
    n = cells.shape[1]
    first = iota((32, n), 0) == jnp.right_shift(cells, 4)
    second = (iota((16, n), 0) == jnp.bitwise_and(cells, 15)) & (cells >= 0)
    return first, second.astype(F32).astype(BF16)


def scatter(values, first, second):
    rows = []
    for value in values:
        for part in split(value):
            rows.append(jnp.where(first, part, 0.0))
    stacked = jnp.concatenate(rows, 0).astype(BF16)
    return lax.dot_general(stacked, second, NT, preferred_element_type=F32)


def scatter_columns(kept, cells):
    n = kept.shape[0]
    rows = [jnp.transpose(kept[i : i + LANES])[:2] for i in range(0, n, LANES)]
    flat = jnp.concatenate(rows, 1)
    first, second = one_hots(cells)
    return scatter([flat[0:1], flat[1:2]], first, second)


def column_codes(idx_ref, inc_ref):
    gx = lax.axis_index("gx")
    start = pl.multiple_of((gx // 2) * LANES, LANES)
    block = inc_ref[:, pl.ds(start, LANES)].astype(F32)
    block = jnp.where(gx % 2 == 1, pltpu.roll(block, 64, 1), block)
    spread = (iota((32, 8), 0) // BS == iota((32, 8), 1)).astype(F32)
    counts = jnp.dot(spread.astype(BF16), block.astype(BF16), preferred_element_type=F32)
    cells = idx_ref[...].astype(F32)
    return jnp.concatenate([cells, jnp.zeros_like(cells)], 1) * 8.0 + counts


def group_rows(idx_ref, inc_ref, turned, cell_ref, count_ref):
    code = column_codes(idx_ref, inc_ref)
    turned[...] = jnp.transpose(jnp.concatenate([code, jnp.zeros((96, LANES), F32)], 0))
    count = GROUPS * TILES
    parts = [turned[pl.ds(2 + j, count, stride=4), :][:, :32] for j in range(4)]
    inner = jnp.concatenate(parts, 1)
    along_y = jnp.concatenate([turned[i : i + 1, :][:, :32] for i in (0, 1, 62, 63)], 1)
    along_x = [
        jnp.concatenate([code[i : i + 1, :64], code[i + 1 : i + 2, :64]], 1) for i in (0, 30)
    ]
    whole = jnp.concatenate([inner] + along_x + [along_y], 0).astype(jnp.int32)
    cells = jnp.right_shift(whole, 3)
    row = iota(whole.shape, 0)
    place = jnp.bitwise_and(iota(whole.shape, 1), jnp.where(row < count, 31, 63))
    masked = (place < 2) | (place >= jnp.where(row < count, 30, 62))
    masked = masked & (row < count + 2)
    cell_ref[pl.ds(0, count + 3), :] = jnp.where(masked, -1, cells)
    count_ref[pl.ds(0, count + 3), :] = jnp.bitwise_and(whole, 7).astype(F32)


def row_at(ref, index):
    return ref[pl.ds(index, 1), :]


def matrices_of(w1_ref, bias_ref, w2_ref, last_ref):
    return w1_ref[...], bias_ref[...], w2_ref[...], last_ref[...]


def tile_state(air_ref, coef_ref, tile):
    state = []
    for half in range(2):
        block = air_ref[half, pl.ds(tile * (4 * GROUPS), 4 * GROUPS + 4)]
        coefs = coefs_of(coef_ref, half)
        state.append(advance(advance(block, coefs), coefs).reshape(GROUPS * LANES, LANES))
    return state


def finish(state, groups, matrices, cell_ref, count_ref, sizes):
    needs = [expand_counts(row_at(count_ref, g)) for g in groups]
    kept = physics(state, jnp.concatenate(needs, 0), matrices, sizes)
    cells = jnp.concatenate([row_at(cell_ref, g) for g in groups], 1)
    return scatter_columns(kept, cells)


def tiles(lo, hi, air_ref, coef_ref, matrix_refs, cell_ref, count_ref, acc_ref):
    @pl.loop(lo, hi)
    def _(tile):
        state = tile_state(air_ref, coef_ref, tile)
        groups = [tile * GROUPS + g for g in range(GROUPS)]
        matrices = matrices_of(*matrix_refs)
        acc_ref[...] += finish(state, groups, matrices, cell_ref, count_ref, TILE_CHUNKS)


def early_tiles():
    gy = lax.axis_index("gy")
    return jnp.where(gy < 3, 1, 0).astype(jnp.int32)


def loads_all():
    return lax.axis_index("gy") < 4


def middle_tiles():
    return jnp.where(lax.axis_index("gx") % 8 == 1, 2, 1).astype(jnp.int32)


def is_even(axis):
    return lax.axis_index(axis) % 2 == 0


def side_turn():
    gy = lax.axis_index("gy")
    return jnp.where((gy == 0) | (gy == 3), 0, 1)


class Copies:
    def __init__(self, sem, first):
        self.sem = sem
        self.next = first
        self.started = []

    def copy(self, place):
        index, ends = self.started[place]
        return pltpu.make_async_copy(*ends(), self.sem.at[index])

    def fetch(self, ends):
        self.started.append((self.next, ends))
        self.next += 1
        self.copy(len(self.started) - 1).start()

    def rows(self, air_in, air_ref, lo, size):
        for half in range(2):
            self.fetch(
                lambda half=half: (
                    air_in.at[:, pl.ds(lo, size), lanes_of(half)],
                    air_ref.at[half, :, pl.ds(lo, size), :],
                )
            )

    def wait(self):
        for place in range(len(self.started)):
            self.copy(place).wait()


def fetch_layers(copies, sources, raw, w2_ref):
    spread_in, east_in, north_in, w1_in, bias_in, w2_in = sources
    raw_w1, raw_bias, numbers = raw
    copies.fetch(lambda: (w1_in, raw_w1))
    copies.fetch(lambda: (w2_in, w2_ref))
    copies.fetch(lambda: (bias_in, raw_bias))
    for row, source in enumerate((spread_in, east_in, north_in)):
        copies.fetch(lambda row=row, source=source: (source, numbers.at[pl.ds(row, 1)]))


def prepare_layers(raw, coef_ref, w1_ref, bias_ref, w2_ref, last_ref):
    raw_w1, raw_bias, numbers = raw
    w1_ref[...] = raw_w1[...] * jnp.asarray(0.5, BF16)
    bias_ref[...] = raw_bias[...] * 0.5
    spread, east, north = (numbers[i : i + 1] for i in range(3))
    coef_ref[0:1] = 1.0 - 4.0 * spread
    coef_ref[1:2] = spread - 0.5 * east
    coef_ref[2:3] = spread + 0.5 * east
    coef_ref[3:4] = spread - 0.5 * north
    coef_ref[4:5] = spread + 0.5 * north
    lane = iota((1, LANES), 1)
    first = w2_ref[:, :LANES].astype(F32)
    second = pltpu.roll(w2_ref[:, LANES:].astype(F32), 1, 1)
    last_ref[...] = jnp.where(lane == 0, first, jnp.where(lane == 1, second, 0.0)).astype(BF16)


def load_kernel(
    air_in, land_in, inc_in, idx_in, water_in, ocean_in, driver_in, mixing_in, spread_in, east_in,
    north_in, w1_in, bias_in, w2_in,
    send1_ref, send2_ref, air_ref, coef_ref, w1_ref, bias_ref, w2_ref, last_ref,
    cell_ref, count_ref, acc_ref, side_ref, idx_ref, land_ref, water_ref, ocean_ref, driver_ref,
    mixing_ref, inc_ref, numbers, raw_bias, raw_w1, turned, sem,
):
    early = loads_all()
    ours = side_turn() == 0
    raw = (raw_w1, raw_bias, numbers)
    columns = Copies(sem, 0)
    columns.fetch(lambda: (inc_in, inc_ref))
    columns.fetch(lambda: (idx_in, idx_ref))
    slabs = Copies(sem, columns.next)
    slabs.rows(air_in, air_ref, 0, 8)
    slabs.rows(air_in, air_ref, 24, 8)
    layers = Copies(sem, slabs.next)

    @pl.when(early)
    def _():
        fetch_layers(layers, (spread_in, east_in, north_in, w1_in, bias_in, w2_in), raw, w2_ref)
        layers.rows(air_in, air_ref, 8, 16)

    others = Copies(sem, layers.next)
    sides = (land_in, water_in, ocean_in, driver_in, mixing_in)
    side_refs = (land_ref, water_ref, ocean_ref, driver_ref, mixing_ref)

    for source, target in zip(sides, side_refs):
        others.fetch(lambda source=source, target=target: (source, target))
    acc_ref[...] = jnp.zeros_like(acc_ref)
    columns.wait()
    group_rows(idx_ref, inc_ref, turned, cell_ref, count_ref)
    slabs.wait()
    upper = jnp.where(is_even("gy"), 30, 0)
    for send, first in ((send1_ref, upper), (send2_ref, 30 - upper)):
        for half in range(2):
            flat = air_ref.at[half].reshape(64 * 32, LANES)
            for k in range(2):
                send[pl.ds(k * 64, 64), lanes_of(half)] = flat[pl.ds(first + k, 64, stride=32), :]

    others.wait()

    @pl.when(ours)
    def _():
        side_parts(idx_ref, side_refs, side_ref)

    @pl.when(early)
    def _():
        layers.wait()
        prepare_layers(raw, coef_ref, w1_ref, bias_ref, w2_ref, last_ref)
        matrix_refs = (w1_ref, bias_ref, w2_ref, last_ref)
        tiles(
            jnp.int32(0), early_tiles(), air_ref, coef_ref, matrix_refs, cell_ref, count_ref,
            acc_ref,
        )


VMEM = pl.BlockSpec(memory_space=pltpu.VMEM)


def params(size):
    return pltpu.CompilerParams(vmem_limit_bytes=size << 20)


def cost(flops):
    return pl.CostEstimate(flops=flops, bytes_accessed=1 << 20, transcendentals=1 << 10)


SIDE = [
    ((32, 64), F32),
    ((16, 32), jnp.int32),
    ((2, 32, 16, 80), F32),
    ((2, 16, 32), F32),
    ((80, 80), F32),
]
LAYER_SCRATCH = [
    pltpu.VMEM((8, 256), F32),
    pltpu.VMEM((1, 512), F32),
    pltpu.VMEM((256, 512), BF16),
]
CORE = [
    ((2, 64, 32, LANES), F32),
    ((8, 256), F32),
    ((256, 512), BF16),
    ((1, 512), F32),
    ((512, 256), BF16),
    ((512, LANES), BF16),
]


def shapes_of(shapes):
    return [jax.ShapeDtypeStruct(*shape) for shape in shapes]


def load(arrays):
    shapes = [((LANES, 256), F32)] * 2 + CORE
    shapes += [
        ((24, LANES), jnp.int32),
        ((24, LANES), F32),
        ((LANES, 16), F32),
        ((5, 16, 32), F32),
        ((32, 64), jnp.int32),
    ] + SIDE
    return pl.pallas_call(
        load_kernel,
        out_shape=shapes_of(shapes),
        in_specs=[pl.BlockSpec(memory_space=pl.ANY)] * 14,
        out_specs=[VMEM] * len(shapes),
        scratch_shapes=[pltpu.VMEM((8, 1024), jnp.int32)]
        + LAYER_SCRATCH
        + [pltpu.VMEM((LANES, LANES), F32), pltpu.SemaphoreType.DMA((24,))],
        compiler_params=params(24),
        cost_estimate=cost(1 << 20),
    )(*arrays)


def ocean_fields(water, driver_ref, ocean_ref, mixing_ref):
    levels = mixing_ref.shape[0]
    matrix = mixing_ref[...]
    wide = jnp.concatenate([matrix, jnp.zeros((levels, LANES - levels), F32)], 1)
    tall = jnp.concatenate([wide, jnp.zeros((LANES - levels, LANES), F32)], 0)
    turned = jnp.transpose(tall)[:levels]
    column = (iota((levels, 1), 0) == 0).astype(F32)
    total = jnp.zeros((1, 1), F32)
    for _ in range(PAIRS):
        row = jnp.sum(column * wide, axis=0, keepdims=True)
        total = total + row[:, 0:1]
        column = jnp.sum(turned * row, axis=1, keepdims=True)
        total = total + column[0:1]
    spread = jnp.concatenate(
        [jnp.broadcast_to(column, (levels, LANES)), jnp.zeros((LANES - levels, LANES), F32)], 0
    )
    row = jnp.transpose(spread)[0:1, :levels]
    fields = []
    for field in range(2):
        block = ocean_ref[field]
        mixed = jnp.transpose(jnp.sum(block * row, axis=2))
        mixed = mixed + (OCEAN_STEP * total) * driver_ref[field]
        fields.append(jnp.where(water == 1, mixed, jnp.transpose(block[:, :, 0])))
    return fields


def land_sums(land, cells):
    lands = jnp.concatenate([land[y : y + 1] for y in range(32)], 1)
    places = jnp.concatenate([cells[y : y + 1] for y in range(32)], 1)
    first, second = one_hots(places)
    sums = scatter([lands, jnp.tanh(lands)], first, second)
    ones = first.astype(F32).astype(BF16)
    return sums, lax.dot_general(ones, second, NT, preferred_element_type=F32)


def side_parts(idx_ref, refs, side_ref):
    land_ref, water_ref, ocean_ref, driver_ref, mixing_ref = refs
    water = water_ref[...]
    fields = ocean_fields(water, driver_ref, ocean_ref, mixing_ref)
    sums, count = land_sums(land_ref[...], idx_ref[...])
    land = jnp.transpose(sums[0:32] + sums[32:64])
    warm = jnp.transpose(sums[64:96] + sums[96:128])
    count = jnp.transpose(count)
    side_ref[0] = fields[0]
    side_ref[1] = fields[1]
    side_ref[2] = jnp.where(water == 1, count * fields[0], land)
    side_ref[3] = jnp.where(water == 1, count * jnp.tanh(fields[0]), warm)
    side_ref[4] = jnp.maximum(count, 1.0)


def middle_kernel(
    air_old, coef_old, w1_old, bias_old, w2_old, last_old, cell_ref, count_ref, idx_ref, land_ref,
    water_ref, ocean_ref, driver_ref, mixing_ref, air_in, spread_in, east_in, north_in, w1_in,
    bias_in, w2_in,
    air_ref, coef_ref, w1_ref, bias_ref, w2_ref, last_ref, acc_ref, side_ref,
    numbers, raw_bias, raw_w1, sem,
):
    early = early_tiles()
    raw = (raw_w1, raw_bias, numbers)
    layers = Copies(sem, 0)

    @pl.when(jnp.logical_not(loads_all()))
    def _():
        fetch_layers(layers, (spread_in, east_in, north_in, w1_in, bias_in, w2_in), raw, w2_ref)
        layers.rows(air_in, air_ref, 8, 16)

    @pl.when(side_turn() == 1)
    def _():
        side_refs = (land_ref, water_ref, ocean_ref, driver_ref, mixing_ref)
        side_parts(idx_ref, side_refs, side_ref)

    @pl.when(jnp.logical_not(loads_all()))
    def _():
        layers.wait()
        prepare_layers(raw, coef_ref, w1_ref, bias_ref, w2_ref, last_ref)

    acc_ref[...] = jnp.zeros_like(acc_ref)
    matrix_refs = (w1_ref, bias_ref, w2_ref, last_ref)
    tiles(
        early, early + middle_tiles(), air_ref, coef_ref, matrix_refs, cell_ref, count_ref, acc_ref
    )


def middle(core, sides, sources):
    shapes = CORE + [((LANES, 16), F32), ((5, 16, 32), F32)]
    return pl.pallas_call(
        middle_kernel,
        out_shape=shapes_of(shapes),
        in_specs=[VMEM] * 14 + [pl.BlockSpec(memory_space=pl.ANY)] * 7,
        out_specs=[VMEM] * len(shapes),
        input_output_aliases={i: i for i in range(len(CORE))},
        scratch_shapes=LAYER_SCRATCH + [pltpu.SemaphoreType.DMA((24,))],
        compiler_params=params(24),
        cost_estimate=cost(1 << 30),
    )(*core, *sides, *sources)


def by_side(axis, first, second):
    even = is_even(axis)
    return jnp.where(even, second, first), jnp.where(even, first, second)


def slab_kernel(air_ref, recv1_ref, recv2_ref, pair_ref, cross_ref):
    even = is_even("gx")
    ylow, yhigh = by_side("gy", recv1_ref[...], recv2_ref[...])
    for half in range(2):
        lanes = lanes_of(half)
        low = air_ref[half, 0:2].reshape(64, LANES)
        high = air_ref[half, 62:64].reshape(64, LANES)
        pair_ref[0:64, lanes] = jnp.where(even, high, low)
        cross_ref[0:64, lanes] = jnp.where(even, low, high)
    low = jnp.concatenate([ylow[64:65], yhigh[0:1], jnp.zeros((6, 256), F32)], 0)
    high = jnp.concatenate([ylow[127:128], yhigh[63:64], jnp.zeros((6, 256), F32)], 0)
    pair_ref[64:72] = jnp.where(even, high, low)
    cross_ref[64:72] = jnp.where(even, low, high)


def x_slabs(air, recv1, recv2):
    return pl.pallas_call(
        slab_kernel,
        out_shape=[jax.ShapeDtypeStruct((72, 256), F32)] * 2,
        in_specs=[VMEM] * 3,
        out_specs=[VMEM] * 2,
        compiler_params=params(16),
        cost_estimate=cost(1 << 10),
    )(air, recv1, recv2)


def late_kernel(
    air_ref, coef_ref, w1_ref, bias_ref, w2_ref, last_ref, cell_ref, count_ref, recv1_ref,
    recv2_ref, send1_ref, send2_ref, acc_ref, edge_ref,
):
    acc_ref[...] = jnp.zeros_like(acc_ref)
    for half in range(2):
        lanes = lanes_of(half)
        ylow, yhigh = by_side("gy", recv1_ref[:, lanes], recv2_ref[:, lanes])
        first, last = by_side("gy", send1_ref[:, lanes], send2_ref[:, lanes])
        along_x = y_edge_state(half, air_ref, coefs_of(coef_ref, half), ylow, yhigh, first, last)
        edge_ref[half] = jnp.concatenate(along_x, 0)
    matrix_refs = (w1_ref, bias_ref, w2_ref, last_ref)
    first = early_tiles() + middle_tiles()
    tiles(first, jnp.int32(TILES), air_ref, coef_ref, matrix_refs, cell_ref, count_ref, acc_ref)


def late(core, halos):
    return pl.pallas_call(
        late_kernel,
        out_shape=[
            jax.ShapeDtypeStruct((LANES, 16), F32),
            jax.ShapeDtypeStruct((2, 2 * LANES, LANES), F32),
        ],
        in_specs=[VMEM] * 12,
        out_specs=[VMEM] * 2,
        compiler_params=params(24),
        cost_estimate=cost(1 << 30),
    )(*core, *halos)


def y_edge_state(half, air_ref, coefs, ylow, yhigh, first, last):
    flat = air_ref.at[half].reshape(64 * 32, LANES)

    def step(block):
        centre = block[1:-1]
        plus_x = pltpu.roll(centre, 63, 1)
        minus_x = pltpu.roll(centre, 1, 1)
        return combine(coefs, centre, plus_x, minus_x, block[2:], block[:-2])

    states = []
    for low in (True, False):
        ys = (2, 3) if low else (28, 29)
        inner = jnp.stack([flat[pl.ds(y, 64, stride=32), :] for y in ys], 0)
        outer = (first if low else last).reshape(2, 64, LANES)
        halo = (ylow if low else yhigh).reshape(2, 64, LANES)
        block = jnp.concatenate([halo, outer, inner] if low else [inner, outer, halo], 0)
        states.append(step(step(block)).reshape(LANES, LANES))
    return states


def x_edge_state(half, air_ref, coefs, ylow, yhigh, xlow, xhigh):
    def with_ends(row, first, last):
        at = iota(row.shape, 0)
        size = row.shape[0]
        plus_y = jnp.where(at == size - 1, last, pltpu.roll(row, size - 1, 0))
        minus_y = jnp.where(at == 0, first, pltpu.roll(row, 1, 0))
        return plus_y, minus_y

    def own(x):
        return air_ref[half, x]

    def beyond(x, y):
        slab = ylow if y < 0 else yhigh
        at = (y + 2 if y < 0 else y - 32) * 64 + x
        return slab[at : at + 1]

    done = []
    for low in (True, False):
        halo = xlow if low else xhigh
        near, far = (halo[32:64], halo[0:32]) if low else (halo[0:32], halo[32:64])
        xs = [0, 1, 2, 3] if low else [63, 62, 61, 60]
        rows = [far, near] + [own(x) for x in xs]
        ends = [None, (halo[64:65], halo[65:66])] + [(beyond(x, -1), beyond(x, 32)) for x in xs]
        outer = [None, None] + [(beyond(x, -2), beyond(x, 33)) for x in xs]

        def apply(centre, outward, inward, plus_y, minus_y):
            plus_x, minus_x = (inward, outward) if low else (outward, inward)
            return combine(coefs, centre, plus_x, minus_x, plus_y, minus_y)

        once = {}
        for i in range(1, 5):
            plus_y, minus_y = with_ends(rows[i], *ends[i])
            once[i] = apply(rows[i], rows[i - 1], rows[i + 1], plus_y, minus_y)
        twice = []
        for i in (2, 3):
            first = apply(
                ends[i][0], ends[i - 1][0], ends[i + 1][0], rows[i][0:1], outer[i][0]
            )
            last = apply(
                ends[i][1], ends[i - 1][1], ends[i + 1][1], outer[i][1], rows[i][31:32]
            )
            plus_y, minus_y = with_ends(once[i], first, last)
            twice.append(apply(once[i], once[i - 1], once[i + 1], plus_y, minus_y))
        done += twice if low else twice[::-1]
    return jnp.concatenate(done, 0)


def edge_kernel(
    air_ref, coef_ref, w1_ref, bias_ref, w2_ref, last_ref, cell_ref, count_ref, recv1_ref,
    recv2_ref, pair_ref, cross_ref, edge_ref, acc0_ref, acc1_ref, acc2_ref, side0_ref, side1_ref,
    out_ref,
):
    state = []
    for half in range(2):
        lanes = lanes_of(half)
        ylow, yhigh = by_side("gy", recv1_ref[:, lanes], recv2_ref[:, lanes])
        xlow, xhigh = by_side("gx", pair_ref[:, lanes], cross_ref[:, lanes])
        coefs = coefs_of(coef_ref, half)
        along_y = x_edge_state(half, air_ref, coefs, ylow, yhigh, xlow, xhigh)
        state.append(jnp.concatenate([edge_ref[half], along_y], 0))
    matrices = matrices_of(w1_ref, bias_ref, w2_ref, last_ref)
    groups = [GROUPS * TILES + g for g in range(3)]
    acc = finish(state, groups, matrices, cell_ref, count_ref, EDGE_CHUNKS)
    acc = acc + (acc0_ref[...] + acc1_ref[...] + acc2_ref[...])
    heat = jnp.transpose(acc[0:32] + acc[32:64])
    vapour = jnp.transpose(acc[64:96] + acc[96:128])
    turn = side_turn()

    def side(index):
        return jnp.where(turn == 0, side0_ref[index], side1_ref[index])

    below = side(4)
    ocean = lax.axis_index("sect") == 1
    flux = THERMAL_FACTOR * (side(2) - heat) / below
    out_ref[0] = jnp.where(ocean, side(0), flux)
    flux = WETNESS_FACTOR * (side(3) - vapour) / below
    out_ref[1] = jnp.where(ocean, side(1), flux)


def edges(core, halos, others):
    return pl.pallas_call(
        edge_kernel,
        out_shape=jax.ShapeDtypeStruct((2, 16, 32), F32),
        in_specs=[VMEM] * 18,
        out_specs=VMEM,
        compiler_params=params(24),
        cost_estimate=cost(1 << 28),
    )(*core, *halos, *others)


def exchanges(axis, first):
    sizes = [lax.axis_size(name) for name in AXES]
    size = lax.axis_size(axis)
    pairs = []
    for device in range(sizes[0] * sizes[1] * sizes[2]):
        at = [device // (sizes[1] * sizes[2]), device // sizes[2] % sizes[1], device % sizes[2]]
        dim = AXES.index(axis)
        step = 1 if (at[dim] - first) % 2 == 0 else -1
        at[dim] = (at[dim] + step) % size
        pairs.append((device, (at[0] * sizes[1] + at[1]) * sizes[2] + at[2]))
    return pairs


def shards(
    air_profile_matrix,
    spreading_numbers,
    eastward_advection_number,
    northward_advection_number,
    landmass_warmth,
    physics_increments,
    underlying_water_index,
    water_indicator,
    waterbody_profiles,
    waterbody_drivers,
    inverted_blending_matrix,
    entry_layer_matrix,
    entry_layer_offset,
    exit_layer_matrix,
):
    air = air_profile_matrix
    sides = (
        landmass_warmth.T,
        water_indicator.T,
        waterbody_profiles.transpose(0, 2, 3, 1),
        waterbody_drivers.transpose(0, 2, 1),
        inverted_blending_matrix,
    )
    layers = (
        spreading_numbers.reshape(1, -1),
        eastward_advection_number.reshape(1, -1),
        northward_advection_number.reshape(1, -1),
        entry_layer_matrix,
        entry_layer_offset.reshape(1, -1),
        exit_layer_matrix,
    )
    columns = (physics_increments.T, underlying_water_index.T)
    air, sides, layers, columns = jax.tree.map(
        lambda array: pltpu.with_memory_space_constraint(array, pltpu.HBM),
        (air, sides, layers, columns),
    )
    loaded = load((air, sides[0], *columns, *sides[1:], *layers))
    send1, send2 = loaded[:2]
    acc0, side0 = loaded[10:12]
    recv2 = lax.ppermute(send2, AXES, exchanges("gy", 1))
    recv1 = lax.ppermute(send1, AXES, exchanges("gy", 0))
    *core, acc1, side1 = middle(loaded[2:10], loaded[12:], (air, *layers))
    core += loaded[8:10]
    acc1, recv2, recv1 = lax.optimization_barrier((acc1, recv2, recv1))
    send_pair, send_cross = x_slabs(core[0], recv1, recv2)
    cross = lax.ppermute(send_cross, AXES, exchanges("gx", 1))
    pair = lax.ppermute(send_pair, AXES, exchanges("gx", 0))
    acc2, edge = late(core, (recv1, recv2, send1, send2))
    acc2, cross, pair = lax.optimization_barrier((acc2, cross, pair))
    result = edges(
        core, (recv1, recv2, pair, cross), (edge, acc0, acc1, acc2, side0, side1)
    )
    return result.transpose(0, 2, 1)[None]


def solution(mesh):
    in_specs = (
        P("gx", "gy", None),
        P(),
        P(),
        P(),
        P("gx", "gy"),
        P(None, "gy"),
        P("gx", "gy"),
        P("gx", "gy"),
        P(None, None, "gx", "gy"),
        P(None, "gx", "gy"),
        P(),
        P(),
        P(),
        P(),
    )
    out_specs = P("sect", None, "gx", "gy")
    return jax.shard_map(shards, mesh=mesh, in_specs=in_specs, out_specs=out_specs, check_vma=False)
```

```python
import jax
import jax.numpy as jnp
from jax import lax
from jax.experimental import pallas as pl
from jax.experimental.pallas import tpu as pltpu
from jax.sharding import PartitionSpec as P

BS = 4
PAIRS = 6
THERMAL_FACTOR = 0.8
WETNESS_FACTOR = 0.6
OCEAN_STEP = 0.1
TANH_SCALE = 0.7978845608028654
TANH_CUBE = 0.044715

GROUPS = 5
TILES = 3
TILE_CHUNKS = (320, 320)
EDGE_CHUNKS = (384,)
LANES = 128
NT = (((1,), (1,)), ((), ()))
F32 = jnp.float32
BF16 = jnp.bfloat16
AXES = ("sect", "gx", "gy")


def iota(shape, dim):
    return lax.broadcasted_iota(jnp.int32, shape, dim)


def combine(coefs, centre, plus_x, minus_x, plus_y, minus_y):
    c0, cxp, cxm, cyp, cym = coefs
    return c0 * centre + cxp * plus_x + cxm * minus_x + cyp * plus_y + cym * minus_y


def advance(block, coefs):
    centre = block[1:-1]
    size = centre.shape[1]
    plus_y = pltpu.roll(centre, size - 1, 1)
    minus_y = pltpu.roll(centre, 1, 1)
    return combine(coefs, centre, block[2:], block[:-2], plus_y, minus_y)


def lanes_of(half):
    return pl.ds(half * LANES, LANES)


def coefs_of(coef_ref, half):
    return [coef_ref[i : i + 1, lanes_of(half)] for i in range(5)]


def hidden_of(state, w1, bias):
    inputs = jnp.concatenate([part.astype(BF16) for part in state], 1)
    half = jnp.dot(inputs, w1, preferred_element_type=F32) + bias
    inner = half * (half * half * (8.0 * TANH_SCALE * TANH_CUBE) + 2.0 * TANH_SCALE)
    return (half * jnp.tanh(inner) + half).astype(BF16)


def physics(state, counts, matrices, sizes):
    w1, bias, w2, w2_last = matrices
    places = [sum(sizes[:i]) for i in range(len(sizes))]
    states = [[part[at : at + n] for part in state] for at, n in zip(places, sizes)]
    counts = [counts[at : at + n] for at, n in zip(places, sizes)]
    lane = iota((1, LANES), 1)
    for index in range(3):
        for chunk, needs in enumerate(counts):
            hidden = hidden_of(states[chunk], w1, bias)
            delta = jnp.dot(hidden, w2, preferred_element_type=F32)
            parts = [delta[:, :LANES], delta[:, LANES:]]
            if index:
                needed = needs > float(index)
                parts = [jnp.where(needed, part, 0.0) for part in parts]
            states[chunk] = [old + part for old, part in zip(states[chunk], parts)]
    kept = []
    for (first, second), needs in zip(states, counts):
        hidden = hidden_of([first, second], w1, bias)
        delta = jnp.dot(hidden, w2_last, preferred_element_type=F32)
        both = jnp.where(lane == 0, first, pltpu.roll(second, 1, 1))
        kept.append(both + jnp.where(needs > 3.0, delta, 0.0))
    return jnp.concatenate(kept, 0)


def expand_counts(row):
    square = (LANES, LANES)
    diagonal = jnp.where(iota(square, 0) == iota(square, 1), row, 0.0).astype(BF16)
    return jnp.dot(diagonal, jnp.ones(square, BF16), preferred_element_type=F32)


def split(row):
    high = row.astype(BF16).astype(F32)
    return high, row - high


def one_hots(cells):
    n = cells.shape[1]
    first = iota((32, n), 0) == jnp.right_shift(cells, 4)
    second = (iota((16, n), 0) == jnp.bitwise_and(cells, 15)) & (cells >= 0)
    return first, second.astype(F32).astype(BF16)


def scatter(values, first, second):
    rows = []
    for value in values:
        for part in split(value):
            rows.append(jnp.where(first, part, 0.0))
    stacked = jnp.concatenate(rows, 0).astype(BF16)
    return lax.dot_general(stacked, second, NT, preferred_element_type=F32)


def scatter_columns(kept, cells):
    n = kept.shape[0]
    rows = [jnp.transpose(kept[i : i + LANES])[:2] for i in range(0, n, LANES)]
    flat = jnp.concatenate(rows, 1)
    first, second = one_hots(cells)
    return scatter([flat[0:1], flat[1:2]], first, second)


def column_codes(idx_ref, inc_ref):
    gx = lax.axis_index("gx")
    start = pl.multiple_of((gx // 2) * LANES, LANES)
    block = inc_ref[:, pl.ds(start, LANES)].astype(F32)
    block = jnp.where(gx % 2 == 1, pltpu.roll(block, 64, 1), block)
    spread = (iota((32, 8), 0) // BS == iota((32, 8), 1)).astype(F32)
    counts = jnp.dot(spread.astype(BF16), block.astype(BF16), preferred_element_type=F32)
    cells = idx_ref[...].astype(F32)
    return jnp.concatenate([cells, jnp.zeros_like(cells)], 1) * 8.0 + counts


def group_rows(idx_ref, inc_ref, turned, cell_ref, count_ref):
    code = column_codes(idx_ref, inc_ref)
    turned[...] = jnp.transpose(jnp.concatenate([code, jnp.zeros((96, LANES), F32)], 0))
    count = GROUPS * TILES
    parts = [turned[pl.ds(2 + j, count, stride=4), :][:, :32] for j in range(4)]
    inner = jnp.concatenate(parts, 1)
    along_y = jnp.concatenate([turned[i : i + 1, :][:, :32] for i in (0, 1, 62, 63)], 1)
    along_x = [
        jnp.concatenate([code[i : i + 1, :64], code[i + 1 : i + 2, :64]], 1) for i in (0, 30)
    ]
    whole = jnp.concatenate([inner] + along_x + [along_y], 0).astype(jnp.int32)
    cells = jnp.right_shift(whole, 3)
    row = iota(whole.shape, 0)
    place = jnp.bitwise_and(iota(whole.shape, 1), jnp.where(row < count, 31, 63))
    masked = (place < 2) | (place >= jnp.where(row < count, 30, 62))
    masked = masked & (row < count + 2)
    cell_ref[pl.ds(0, count + 3), :] = jnp.where(masked, -1, cells)
    count_ref[pl.ds(0, count + 3), :] = jnp.bitwise_and(whole, 7).astype(F32)


def row_at(ref, index):
    return ref[pl.ds(index, 1), :]


def matrices_of(w1_ref, bias_ref, w2_ref, last_ref):
    return w1_ref[...], bias_ref[...], w2_ref[...], last_ref[...]


def tile_state(air_ref, coef_ref, tile):
    state = []
    for half in range(2):
        block = air_ref[half, pl.ds(tile * (4 * GROUPS), 4 * GROUPS + 4)]
        coefs = coefs_of(coef_ref, half)
        state.append(advance(advance(block, coefs), coefs).reshape(GROUPS * LANES, LANES))
    return state


def finish(state, groups, matrices, cell_ref, count_ref, sizes):
    needs = [expand_counts(row_at(count_ref, g)) for g in groups]
    kept = physics(state, jnp.concatenate(needs, 0), matrices, sizes)
    cells = jnp.concatenate([row_at(cell_ref, g) for g in groups], 1)
    return scatter_columns(kept, cells)


def add_tile(tile, refs):
    air_ref, coef_ref, matrix_refs, cell_ref, count_ref, acc_ref = refs
    state = tile_state(air_ref, coef_ref, tile)
    groups = [tile * GROUPS + g for g in range(GROUPS)]
    matrices = matrices_of(*matrix_refs)
    acc_ref[...] += finish(state, groups, matrices, cell_ref, count_ref, TILE_CHUNKS)


def tiles(lo, hi, *refs):
    @pl.loop(lo, hi)
    def _(tile):
        add_tile(tile, refs)


def early_tiles():
    gy = lax.axis_index("gy")
    return jnp.where(gy < 2, 1, 0).astype(jnp.int32)


def loads_all():
    return lax.axis_index("gy") < 4


def middle_tiles():
    return jnp.where(lax.axis_index("gx") % 8 == 1, 2, 1).astype(jnp.int32)


def is_even(axis):
    return lax.axis_index(axis) % 2 == 0


def side_turn():
    gy = lax.axis_index("gy")
    return jnp.where((gy < 4) & (gy != 1), 0, 1)


class Copies:
    def __init__(self, sem, first):
        self.sem = sem
        self.next = first
        self.started = []

    def copy(self, place):
        index, ends = self.started[place]
        return pltpu.make_async_copy(*ends(), self.sem.at[index])

    def fetch(self, ends):
        self.started.append((self.next, ends))
        self.next += 1
        self.copy(len(self.started) - 1).start()

    def rows(self, air_in, air_ref, lo, size):
        for half in range(2):
            self.fetch(
                lambda half=half: (
                    air_in.at[:, pl.ds(lo, size), lanes_of(half)],
                    air_ref.at[half, pl.ds(0, 64), pl.ds(lo, size), :],
                )
            )

    def wait(self):
        for place in range(len(self.started)):
            self.copy(place).wait()


def fetch_layers(copies, sources, raw, w2_ref):
    spread_in, east_in, north_in, w1_in, bias_in, w2_in = sources
    raw_w1, raw_bias, numbers = raw
    copies.fetch(lambda: (w1_in, raw_w1))
    copies.fetch(lambda: (w2_in, w2_ref))
    copies.fetch(lambda: (bias_in, raw_bias))
    for row, source in enumerate((spread_in, east_in, north_in)):
        copies.fetch(lambda row=row, source=source: (source, numbers.at[pl.ds(row, 1)]))


def prepare_layers(raw, coef_ref, w1_ref, bias_ref, w2_ref, last_ref):
    raw_w1, raw_bias, numbers = raw
    w1_ref[...] = raw_w1[...] * jnp.asarray(0.5, BF16)
    bias_ref[...] = raw_bias[...] * 0.5
    spread, east, north = (numbers[i : i + 1] for i in range(3))
    coef_ref[0:1] = 1.0 - 4.0 * spread
    coef_ref[1:2] = spread - 0.5 * east
    coef_ref[2:3] = spread + 0.5 * east
    coef_ref[3:4] = spread - 0.5 * north
    coef_ref[4:5] = spread + 0.5 * north
    lane = iota((1, LANES), 1)
    first = w2_ref[:, :LANES].astype(F32)
    second = pltpu.roll(w2_ref[:, LANES:].astype(F32), 1, 1)
    last_ref[...] = jnp.where(lane == 0, first, jnp.where(lane == 1, second, 0.0)).astype(BF16)


def load_kernel(
    air_in, land_in, inc_in, idx_in, water_in, ocean_in, driver_in, mixing_in, spread_in, east_in,
    north_in, w1_in, bias_in, w2_in,
    send1_ref, send2_ref, air_ref, coef_ref, w1_ref, bias_ref, w2_ref, last_ref,
    cell_ref, count_ref, acc_ref, side_ref, idx_ref, land_ref, water_ref, ocean_ref, driver_ref,
    mixing_ref, inc_ref, numbers, raw_bias, raw_w1, turned, sem,
):
    early = loads_all()
    ours = side_turn() == 0
    raw = (raw_w1, raw_bias, numbers)
    columns = Copies(sem, 0)
    columns.fetch(lambda: (inc_in, inc_ref))
    columns.fetch(lambda: (idx_in, idx_ref))
    slabs = Copies(sem, columns.next)
    slabs.rows(air_in, air_ref, 0, 8)
    slabs.rows(air_in, air_ref, 24, 8)
    layers = Copies(sem, slabs.next)

    @pl.when(early)
    def _():
        fetch_layers(layers, (spread_in, east_in, north_in, w1_in, bias_in, w2_in), raw, w2_ref)
        layers.rows(air_in, air_ref, 8, 16)

    others = Copies(sem, layers.next)
    sides = (land_in, water_in, ocean_in, driver_in, mixing_in)
    side_refs = (land_ref, water_ref, ocean_ref, driver_ref, mixing_ref)

    for source, target in zip(sides, side_refs):
        others.fetch(lambda source=source, target=target: (source, target))
    acc_ref[...] = jnp.zeros_like(acc_ref)
    columns.wait()
    group_rows(idx_ref, inc_ref, turned, cell_ref, count_ref)
    slabs.wait()
    upper = jnp.where(is_even("gy"), 30, 0)
    for send, first in ((send1_ref, upper), (send2_ref, 30 - upper)):
        for half in range(2):
            flat = air_ref.at[half].reshape(65 * 32, LANES)
            for k in range(2):
                send[pl.ds(k * 64, 64), lanes_of(half)] = flat[pl.ds(first + k, 64, stride=32), :]

    others.wait()

    @pl.when(early)
    def _():
        layers.wait()
        prepare_layers(raw, coef_ref, w1_ref, bias_ref, w2_ref, last_ref)

    matrix_refs = (w1_ref, bias_ref, w2_ref, last_ref)
    tile_refs = (air_ref, coef_ref, matrix_refs, cell_ref, count_ref, acc_ref)
    some = early_tiles() > 0

    @pl.when(ours & jnp.logical_not(some))
    def _():
        side_parts(idx_ref, side_refs, side_ref)

    @pl.when(ours & some)
    def _():
        side_parts(idx_ref, side_refs, side_ref)
        add_tile(jnp.int32(0), tile_refs)

    @pl.when(jnp.logical_not(ours) & some)
    def _():
        add_tile(jnp.int32(0), tile_refs)


VMEM = pl.BlockSpec(memory_space=pltpu.VMEM)


def params(size):
    return pltpu.CompilerParams(vmem_limit_bytes=size << 20)


def cost(flops):
    return pl.CostEstimate(flops=flops, bytes_accessed=1 << 20, transcendentals=1 << 10)


SIDE = [
    ((32, 64), F32),
    ((16, 32), jnp.int32),
    ((2, 32, 16, 80), F32),
    ((2, 16, 32), F32),
    ((80, 80), F32),
]
LAYER_SCRATCH = [
    pltpu.VMEM((8, 256), F32),
    pltpu.VMEM((1, 512), F32),
    pltpu.VMEM((256, 512), BF16),
]
CORE = [
    ((2, 65, 32, LANES), F32),
    ((8, 256), F32),
    ((256, 512), BF16),
    ((1, 512), F32),
    ((512, 256), BF16),
    ((512, LANES), BF16),
]


def shapes_of(shapes):
    return [jax.ShapeDtypeStruct(*shape) for shape in shapes]


def load(arrays):
    shapes = [((LANES, 256), F32)] * 2 + CORE
    shapes += [
        ((24, LANES), jnp.int32),
        ((24, LANES), F32),
        ((LANES, 16), F32),
        ((5, 16, 32), F32),
        ((32, 64), jnp.int32),
    ] + SIDE
    return pl.pallas_call(
        load_kernel,
        out_shape=shapes_of(shapes),
        in_specs=[pl.BlockSpec(memory_space=pl.ANY)] * 14,
        out_specs=[VMEM] * len(shapes),
        scratch_shapes=[pltpu.VMEM((8, 1024), jnp.int32)]
        + LAYER_SCRATCH
        + [pltpu.VMEM((LANES, LANES), F32), pltpu.SemaphoreType.DMA((24,))],
        compiler_params=params(24),
        cost_estimate=cost(1 << 20),
    )(*arrays)


def ocean_fields(water, driver_ref, ocean_ref, mixing_ref):
    levels = mixing_ref.shape[0]
    matrix = mixing_ref[...]
    wide = jnp.concatenate([matrix, jnp.zeros((levels, LANES - levels), F32)], 1)
    tall = jnp.concatenate([wide, jnp.zeros((LANES - levels, LANES), F32)], 0)
    turned = jnp.transpose(tall)[:levels]
    column = (iota((levels, 1), 0) == 0).astype(F32)
    total = jnp.zeros((1, 1), F32)
    for _ in range(PAIRS):
        row = jnp.sum(column * wide, axis=0, keepdims=True)
        total = total + row[:, 0:1]
        column = jnp.sum(turned * row, axis=1, keepdims=True)
        total = total + column[0:1]
    spread = jnp.concatenate(
        [jnp.broadcast_to(column, (levels, LANES)), jnp.zeros((LANES - levels, LANES), F32)], 0
    )
    row = jnp.transpose(spread)[0:1, :levels]
    fields = []
    for field in range(2):
        block = ocean_ref[field]
        mixed = jnp.transpose(jnp.sum(block * row, axis=2))
        mixed = mixed + (OCEAN_STEP * total) * driver_ref[field]
        fields.append(jnp.where(water == 1, mixed, jnp.transpose(block[:, :, 0])))
    return fields


def land_sums(land, cells):
    lands = jnp.concatenate([land[y : y + 1] for y in range(32)], 1)
    places = jnp.concatenate([cells[y : y + 1] for y in range(32)], 1)
    first, second = one_hots(places)
    sums = scatter([lands, jnp.tanh(lands)], first, second)
    ones = first.astype(F32).astype(BF16)
    return sums, lax.dot_general(ones, second, NT, preferred_element_type=F32)


def side_parts(idx_ref, refs, side_ref):
    land_ref, water_ref, ocean_ref, driver_ref, mixing_ref = refs
    water = water_ref[...]
    fields = ocean_fields(water, driver_ref, ocean_ref, mixing_ref)
    sums, count = land_sums(land_ref[...], idx_ref[...])
    land = jnp.transpose(sums[0:32] + sums[32:64])
    warm = jnp.transpose(sums[64:96] + sums[96:128])
    count = jnp.transpose(count)
    side_ref[0] = fields[0]
    side_ref[1] = fields[1]
    side_ref[2] = jnp.where(water == 1, count * fields[0], land)
    side_ref[3] = jnp.where(water == 1, count * jnp.tanh(fields[0]), warm)
    side_ref[4] = jnp.maximum(count, 1.0)


def middle_kernel(
    air_old, coef_old, w1_old, bias_old, w2_old, last_old, cell_ref, count_ref, idx_ref, land_ref,
    water_ref, ocean_ref, driver_ref, mixing_ref, air_in, spread_in, east_in, north_in, w1_in,
    bias_in, w2_in,
    air_ref, coef_ref, w1_ref, bias_ref, w2_ref, last_ref, acc_ref, side_ref,
    numbers, raw_bias, raw_w1, sem,
):
    early = early_tiles()
    raw = (raw_w1, raw_bias, numbers)
    layers = Copies(sem, 0)

    @pl.when(jnp.logical_not(loads_all()))
    def _():
        fetch_layers(layers, (spread_in, east_in, north_in, w1_in, bias_in, w2_in), raw, w2_ref)
        layers.rows(air_in, air_ref, 8, 16)

    ours = side_turn() == 1
    side_refs = (land_ref, water_ref, ocean_ref, driver_ref, mixing_ref)
    matrix_refs = (w1_ref, bias_ref, w2_ref, last_ref)
    tile_refs = (air_ref, coef_ref, matrix_refs, cell_ref, count_ref, acc_ref)
    acc_ref[...] = jnp.zeros_like(acc_ref)
    both = ours & loads_all()

    @pl.when(ours & jnp.logical_not(both))
    def _():
        side_parts(idx_ref, side_refs, side_ref)

    @pl.when(jnp.logical_not(loads_all()))
    def _():
        layers.wait()
        prepare_layers(raw, coef_ref, w1_ref, bias_ref, w2_ref, last_ref)

    @pl.when(both)
    def _():
        side_parts(idx_ref, side_refs, side_ref)
        add_tile(early, tile_refs)

    tiles(early + both.astype(jnp.int32), early + middle_tiles(), *tile_refs)


def middle(core, sides, sources):
    shapes = CORE + [((LANES, 16), F32), ((5, 16, 32), F32)]
    return pl.pallas_call(
        middle_kernel,
        out_shape=shapes_of(shapes),
        in_specs=[VMEM] * 14 + [pl.BlockSpec(memory_space=pl.ANY)] * 7,
        out_specs=[VMEM] * len(shapes),
        input_output_aliases={i: i for i in range(len(CORE))},
        scratch_shapes=LAYER_SCRATCH + [pltpu.SemaphoreType.DMA((24,))],
        compiler_params=params(24),
        cost_estimate=cost(1 << 30),
    )(*core, *sides, *sources)


def by_side(axis, first, second):
    even = is_even(axis)
    return jnp.where(even, second, first), jnp.where(even, first, second)


def slab_kernel(air_ref, recv1_ref, recv2_ref, pair_ref, cross_ref):
    even = is_even("gx")
    ylow, yhigh = by_side("gy", recv1_ref[...], recv2_ref[...])
    for half in range(2):
        lanes = lanes_of(half)
        low = air_ref[half, 0:2].reshape(64, LANES)
        high = air_ref[half, 62:64].reshape(64, LANES)
        pair_ref[0:64, lanes] = jnp.where(even, high, low)
        cross_ref[0:64, lanes] = jnp.where(even, low, high)
    low = jnp.concatenate([ylow[64:65], yhigh[0:1], jnp.zeros((6, 256), F32)], 0)
    high = jnp.concatenate([ylow[127:128], yhigh[63:64], jnp.zeros((6, 256), F32)], 0)
    pair_ref[64:72] = jnp.where(even, high, low)
    cross_ref[64:72] = jnp.where(even, low, high)


def x_slabs(air, recv1, recv2):
    return pl.pallas_call(
        slab_kernel,
        out_shape=[jax.ShapeDtypeStruct((72, 256), F32)] * 2,
        in_specs=[VMEM] * 3,
        out_specs=[VMEM] * 2,
        compiler_params=params(16),
        cost_estimate=cost(1 << 10),
    )(air, recv1, recv2)


def late_kernel(
    air_ref, coef_ref, w1_ref, bias_ref, w2_ref, last_ref, cell_ref, count_ref, recv1_ref,
    recv2_ref, send1_ref, send2_ref, acc_ref, edge_ref,
):
    acc_ref[...] = jnp.zeros_like(acc_ref)
    for half in range(2):
        lanes = lanes_of(half)
        ylow, yhigh = by_side("gy", recv1_ref[:, lanes], recv2_ref[:, lanes])
        first, last = by_side("gy", send1_ref[:, lanes], send2_ref[:, lanes])
        along_x = y_edge_state(half, air_ref, coefs_of(coef_ref, half), ylow, yhigh, first, last)
        edge_ref[half] = jnp.concatenate(along_x, 0)
    matrix_refs = (w1_ref, bias_ref, w2_ref, last_ref)
    first = early_tiles() + middle_tiles()
    tiles(first, jnp.int32(TILES), air_ref, coef_ref, matrix_refs, cell_ref, count_ref, acc_ref)


def late(core, halos):
    return pl.pallas_call(
        late_kernel,
        out_shape=[
            jax.ShapeDtypeStruct((LANES, 16), F32),
            jax.ShapeDtypeStruct((2, 2 * LANES, LANES), F32),
        ],
        in_specs=[VMEM] * 12,
        out_specs=[VMEM] * 2,
        compiler_params=params(24),
        cost_estimate=cost(1 << 30),
    )(*core, *halos)


def y_edge_state(half, air_ref, coefs, ylow, yhigh, first, last):
    flat = air_ref.at[half].reshape(65 * 32, LANES)

    def step(block):
        centre = block[1:-1]
        plus_x = pltpu.roll(centre, 63, 1)
        minus_x = pltpu.roll(centre, 1, 1)
        return combine(coefs, centre, plus_x, minus_x, block[2:], block[:-2])

    states = []
    for low in (True, False):
        ys = (2, 3) if low else (28, 29)
        inner = jnp.stack([flat[pl.ds(y, 64, stride=32), :] for y in ys], 0)
        outer = (first if low else last).reshape(2, 64, LANES)
        halo = (ylow if low else yhigh).reshape(2, 64, LANES)
        block = jnp.concatenate([halo, outer, inner] if low else [inner, outer, halo], 0)
        states.append(step(step(block)).reshape(LANES, LANES))
    return states


def x_edge_state(half, air_ref, coefs, ylow, yhigh, xlow, xhigh):
    def with_ends(row, first, last):
        at = iota(row.shape, 0)
        size = row.shape[0]
        plus_y = jnp.where(at == size - 1, last, pltpu.roll(row, size - 1, 0))
        minus_y = jnp.where(at == 0, first, pltpu.roll(row, 1, 0))
        return plus_y, minus_y

    def own(x):
        return air_ref[half, x]

    def beyond(x, y):
        slab = ylow if y < 0 else yhigh
        at = (y + 2 if y < 0 else y - 32) * 64 + x
        return slab[at : at + 1]

    done = []
    for low in (True, False):
        halo = xlow if low else xhigh
        near, far = (halo[32:64], halo[0:32]) if low else (halo[0:32], halo[32:64])
        xs = [0, 1, 2, 3] if low else [63, 62, 61, 60]
        rows = [far, near] + [own(x) for x in xs]
        ends = [None, (halo[64:65], halo[65:66])] + [(beyond(x, -1), beyond(x, 32)) for x in xs]
        outer = [None, None] + [(beyond(x, -2), beyond(x, 33)) for x in xs]

        def apply(centre, outward, inward, plus_y, minus_y):
            plus_x, minus_x = (inward, outward) if low else (outward, inward)
            return combine(coefs, centre, plus_x, minus_x, plus_y, minus_y)

        once = {}
        for i in range(1, 5):
            plus_y, minus_y = with_ends(rows[i], *ends[i])
            once[i] = apply(rows[i], rows[i - 1], rows[i + 1], plus_y, minus_y)
        twice = []
        for i in (2, 3):
            first = apply(
                ends[i][0], ends[i - 1][0], ends[i + 1][0], rows[i][0:1], outer[i][0]
            )
            last = apply(
                ends[i][1], ends[i - 1][1], ends[i + 1][1], outer[i][1], rows[i][31:32]
            )
            plus_y, minus_y = with_ends(once[i], first, last)
            twice.append(apply(once[i], once[i - 1], once[i + 1], plus_y, minus_y))
        done += twice if low else twice[::-1]
    return jnp.concatenate(done, 0)


def edge_kernel(
    air_ref, coef_ref, w1_ref, bias_ref, w2_ref, last_ref, cell_ref, count_ref, recv1_ref,
    recv2_ref, pair_ref, cross_ref, edge_ref, acc0_ref, acc1_ref, acc2_ref, side0_ref, side1_ref,
    out_ref,
):
    state = []
    for half in range(2):
        lanes = lanes_of(half)
        ylow, yhigh = by_side("gy", recv1_ref[:, lanes], recv2_ref[:, lanes])
        xlow, xhigh = by_side("gx", pair_ref[:, lanes], cross_ref[:, lanes])
        coefs = coefs_of(coef_ref, half)
        along_y = x_edge_state(half, air_ref, coefs, ylow, yhigh, xlow, xhigh)
        state.append(jnp.concatenate([edge_ref[half], along_y], 0))
    matrices = matrices_of(w1_ref, bias_ref, w2_ref, last_ref)
    groups = [GROUPS * TILES + g for g in range(3)]
    acc = finish(state, groups, matrices, cell_ref, count_ref, EDGE_CHUNKS)
    acc = acc + (acc0_ref[...] + acc1_ref[...] + acc2_ref[...])
    heat = jnp.transpose(acc[0:32] + acc[32:64])
    vapour = jnp.transpose(acc[64:96] + acc[96:128])
    turn = side_turn()

    def side(index):
        return jnp.where(turn == 0, side0_ref[index], side1_ref[index])

    below = side(4)
    ocean = lax.axis_index("sect") == 1
    flux = THERMAL_FACTOR * (side(2) - heat) / below
    out_ref[0] = jnp.where(ocean, side(0), flux)
    flux = WETNESS_FACTOR * (side(3) - vapour) / below
    out_ref[1] = jnp.where(ocean, side(1), flux)


def edges(core, halos, others):
    return pl.pallas_call(
        edge_kernel,
        out_shape=jax.ShapeDtypeStruct((2, 16, 32), F32),
        in_specs=[VMEM] * 18,
        out_specs=VMEM,
        compiler_params=params(24),
        cost_estimate=cost(1 << 28),
    )(*core, *halos, *others)


def exchanges(axis, first):
    sizes = [lax.axis_size(name) for name in AXES]
    size = lax.axis_size(axis)
    pairs = []
    for device in range(sizes[0] * sizes[1] * sizes[2]):
        at = [device // (sizes[1] * sizes[2]), device // sizes[2] % sizes[1], device % sizes[2]]
        dim = AXES.index(axis)
        step = 1 if (at[dim] - first) % 2 == 0 else -1
        at[dim] = (at[dim] + step) % size
        pairs.append((device, (at[0] * sizes[1] + at[1]) * sizes[2] + at[2]))
    return pairs


def shards(
    air_profile_matrix,
    spreading_numbers,
    eastward_advection_number,
    northward_advection_number,
    landmass_warmth,
    physics_increments,
    underlying_water_index,
    water_indicator,
    waterbody_profiles,
    waterbody_drivers,
    inverted_blending_matrix,
    entry_layer_matrix,
    entry_layer_offset,
    exit_layer_matrix,
):
    air = air_profile_matrix
    sides = (
        landmass_warmth.T,
        water_indicator.T,
        waterbody_profiles.transpose(0, 2, 3, 1),
        waterbody_drivers.transpose(0, 2, 1),
        inverted_blending_matrix,
    )
    layers = (
        spreading_numbers.reshape(1, -1),
        eastward_advection_number.reshape(1, -1),
        northward_advection_number.reshape(1, -1),
        entry_layer_matrix,
        entry_layer_offset.reshape(1, -1),
        exit_layer_matrix,
    )
    columns = (physics_increments.T, underlying_water_index.T)
    air, sides, layers, columns = jax.tree.map(
        lambda array: pltpu.with_memory_space_constraint(array, pltpu.HBM),
        (air, sides, layers, columns),
    )
    loaded = load((air, sides[0], *columns, *sides[1:], *layers))
    send1, send2 = loaded[:2]
    acc0, side0 = loaded[10:12]
    recv2 = lax.ppermute(send2, AXES, exchanges("gy", 1))
    recv1 = lax.ppermute(send1, AXES, exchanges("gy", 0))
    *core, acc1, side1 = middle(loaded[2:10], loaded[12:], (air, *layers))
    core += loaded[8:10]
    acc1, recv2, recv1 = lax.optimization_barrier((acc1, recv2, recv1))
    send_pair, send_cross = x_slabs(core[0], recv1, recv2)
    cross = lax.ppermute(send_cross, AXES, exchanges("gx", 1))
    pair = lax.ppermute(send_pair, AXES, exchanges("gx", 0))
    acc2, edge = late(core, (recv1, recv2, send1, send2))
    acc2, cross, pair = lax.optimization_barrier((acc2, cross, pair))
    result = edges(
        core, (recv1, recv2, pair, cross), (edge, acc0, acc1, acc2, side0, side1)
    )
    return result.transpose(0, 2, 1)[None]


def solution(mesh):
    in_specs = (
        P("gx", "gy", None),
        P(),
        P(),
        P(),
        P("gx", "gy"),
        P(None, "gy"),
        P("gx", "gy"),
        P("gx", "gy"),
        P(None, None, "gx", "gy"),
        P(None, "gx", "gy"),
        P(),
        P(),
        P(),
        P(),
    )
    out_specs = P("sect", None, "gx", "gy")
    return jax.shard_map(shards, mesh=mesh, in_specs=in_specs, out_specs=out_specs, check_vma=False)
```

```python
import jax
import jax.numpy as jnp
from jax import lax
from jax.experimental import pallas as pl
from jax.experimental.pallas import tpu as pltpu
from jax.sharding import PartitionSpec as P

BS = 4
PAIRS = 6
THERMAL_FACTOR = 0.8
WETNESS_FACTOR = 0.6
OCEAN_STEP = 0.1
TANH_SCALE = 0.7978845608028654
TANH_CUBE = 0.044715

GROUPS = 5
TILES = 3
TILE_CHUNKS = (320, 320)
EDGE_CHUNKS = (384,)
LANES = 128
NT = (((1,), (1,)), ((), ()))
F32 = jnp.float32
BF16 = jnp.bfloat16
AXES = ("sect", "gx", "gy")


def iota(shape, dim):
    return lax.broadcasted_iota(jnp.int32, shape, dim)


def combine(coefs, centre, plus_x, minus_x, plus_y, minus_y):
    c0, cxp, cxm, cyp, cym = coefs
    return c0 * centre + cxp * plus_x + cxm * minus_x + cyp * plus_y + cym * minus_y


def advance(block, coefs):
    centre = block[1:-1]
    size = centre.shape[1]
    plus_y = pltpu.roll(centre, size - 1, 1)
    minus_y = pltpu.roll(centre, 1, 1)
    return combine(coefs, centre, block[2:], block[:-2], plus_y, minus_y)


def lanes_of(half):
    return pl.ds(half * LANES, LANES)


def coefs_of(coef_ref, half):
    return [coef_ref[i : i + 1, lanes_of(half)] for i in range(5)]


def hidden_of(state, w1, bias):
    inputs = jnp.concatenate([part.astype(BF16) for part in state], 1)
    half = jnp.dot(inputs, w1, preferred_element_type=F32) + bias
    inner = half * (half * half * (8.0 * TANH_SCALE * TANH_CUBE) + 2.0 * TANH_SCALE)
    return (half * jnp.tanh(inner) + half).astype(BF16)


def physics(state, counts, matrices, sizes):
    w1, bias, w2, w2_last = matrices
    places = [sum(sizes[:i]) for i in range(len(sizes))]
    states = [[part[at : at + n] for part in state] for at, n in zip(places, sizes)]
    counts = [counts[at : at + n] for at, n in zip(places, sizes)]
    lane = iota((1, LANES), 1)
    for index in range(3):
        for chunk, needs in enumerate(counts):
            hidden = hidden_of(states[chunk], w1, bias)
            delta = jnp.dot(hidden, w2, preferred_element_type=F32)
            parts = [delta[:, :LANES], delta[:, LANES:]]
            if index:
                needed = needs > float(index)
                parts = [jnp.where(needed, part, 0.0) for part in parts]
            states[chunk] = [old + part for old, part in zip(states[chunk], parts)]
    kept = []
    for (first, second), needs in zip(states, counts):
        hidden = hidden_of([first, second], w1, bias)
        delta = jnp.dot(hidden, w2_last, preferred_element_type=F32)
        both = jnp.where(lane == 0, first, pltpu.roll(second, 1, 1))
        kept.append(both + jnp.where(needs > 3.0, delta, 0.0))
    return jnp.concatenate(kept, 0)


def expand_counts(row):
    square = (LANES, LANES)
    diagonal = jnp.where(iota(square, 0) == iota(square, 1), row, 0.0).astype(BF16)
    return jnp.dot(diagonal, jnp.ones(square, BF16), preferred_element_type=F32)


def split(row):
    high = row.astype(BF16).astype(F32)
    return high, row - high


def one_hots(cells):
    n = cells.shape[1]
    first = iota((32, n), 0) == jnp.right_shift(cells, 4)
    second = (iota((16, n), 0) == jnp.bitwise_and(cells, 15)) & (cells >= 0)
    return first, second.astype(F32).astype(BF16)


def scatter(values, first, second):
    rows = []
    for value in values:
        for part in split(value):
            rows.append(jnp.where(first, part, 0.0))
    stacked = jnp.concatenate(rows, 0).astype(BF16)
    return lax.dot_general(stacked, second, NT, preferred_element_type=F32)


def scatter_columns(kept, cells):
    n = kept.shape[0]
    rows = [jnp.transpose(kept[i : i + LANES])[:2] for i in range(0, n, LANES)]
    flat = jnp.concatenate(rows, 1)
    first, second = one_hots(cells)
    return scatter([flat[0:1], flat[1:2]], first, second)


def column_codes(idx_ref, inc_ref):
    gx = lax.axis_index("gx")
    start = pl.multiple_of((gx // 2) * LANES, LANES)
    block = inc_ref[:, pl.ds(start, LANES)].astype(F32)
    block = jnp.where(gx % 2 == 1, pltpu.roll(block, 64, 1), block)
    spread = (iota((32, 8), 0) // BS == iota((32, 8), 1)).astype(F32)
    counts = jnp.dot(spread.astype(BF16), block.astype(BF16), preferred_element_type=F32)
    cells = idx_ref[...].astype(F32)
    return jnp.concatenate([cells, jnp.zeros_like(cells)], 1) * 8.0 + counts


def group_rows(idx_ref, inc_ref, turned, cell_ref, count_ref):
    code = column_codes(idx_ref, inc_ref)
    turned[...] = jnp.transpose(jnp.concatenate([code, jnp.zeros((96, LANES), F32)], 0))
    count = GROUPS * TILES
    parts = [turned[pl.ds(2 + j, count, stride=4), :][:, :32] for j in range(4)]
    inner = jnp.concatenate(parts, 1)
    along_y = jnp.concatenate([turned[i : i + 1, :][:, :32] for i in (0, 1, 62, 63)], 1)
    along_x = [
        jnp.concatenate([code[i : i + 1, :64], code[i + 1 : i + 2, :64]], 1) for i in (0, 30)
    ]
    whole = jnp.concatenate([inner] + along_x + [along_y], 0).astype(jnp.int32)
    cells = jnp.right_shift(whole, 3)
    row = iota(whole.shape, 0)
    place = jnp.bitwise_and(iota(whole.shape, 1), jnp.where(row < count, 31, 63))
    masked = (place < 2) | (place >= jnp.where(row < count, 30, 62))
    masked = masked & (row < count + 2)
    cell_ref[pl.ds(0, count + 3), :] = jnp.where(masked, -1, cells)
    count_ref[pl.ds(0, count + 3), :] = jnp.bitwise_and(whole, 7).astype(F32)


def row_at(ref, index):
    return ref[pl.ds(index, 1), :]


def matrices_of(w1_ref, bias_ref, w2_ref, last_ref):
    return w1_ref[...], bias_ref[...], w2_ref[...], last_ref[...]


def tile_state(air_ref, coef_ref, tile):
    state = []
    for half in range(2):
        block = air_ref[half, pl.ds(tile * (4 * GROUPS), 4 * GROUPS + 4)]
        coefs = coefs_of(coef_ref, half)
        state.append(advance(advance(block, coefs), coefs).reshape(GROUPS * LANES, LANES))
    return state


def finish(state, groups, matrices, cell_ref, count_ref, sizes):
    needs = [expand_counts(row_at(count_ref, g)) for g in groups]
    kept = physics(state, jnp.concatenate(needs, 0), matrices, sizes)
    cells = jnp.concatenate([row_at(cell_ref, g) for g in groups], 1)
    return scatter_columns(kept, cells)


def add_tile(tile, refs):
    air_ref, coef_ref, matrix_refs, cell_ref, count_ref, acc_ref = refs
    state = tile_state(air_ref, coef_ref, tile)
    groups = [tile * GROUPS + g for g in range(GROUPS)]
    matrices = matrices_of(*matrix_refs)
    acc_ref[...] += finish(state, groups, matrices, cell_ref, count_ref, TILE_CHUNKS)


def tiles(lo, hi, *refs):
    @pl.loop(lo, hi)
    def _(tile):
        add_tile(tile, refs)


def early_tiles():
    gy = lax.axis_index("gy")
    return jnp.where(gy < 2, 1, 0).astype(jnp.int32)


def loads_all():
    return lax.axis_index("gy") < 4


def middle_tiles():
    place = lax.axis_index("gx") % 8
    waiting = (place == 1) | ((place == 3) & (lax.axis_index("gy") >= 2))
    return jnp.where(waiting, 2, 1).astype(jnp.int32)


def is_even(axis):
    return lax.axis_index(axis) % 2 == 0


def side_turn():
    gy = lax.axis_index("gy")
    return jnp.where((gy < 4) & (gy != 1), 0, 1)


class Copies:
    def __init__(self, sem, first):
        self.sem = sem
        self.next = first
        self.started = []

    def copy(self, place):
        index, ends = self.started[place]
        return pltpu.make_async_copy(*ends(), self.sem.at[index])

    def fetch(self, ends):
        self.started.append((self.next, ends))
        self.next += 1
        self.copy(len(self.started) - 1).start()

    def rows(self, air_in, air_ref, lo, size):
        for half in range(2):
            self.fetch(
                lambda half=half: (
                    air_in.at[:, pl.ds(lo, size), lanes_of(half)],
                    air_ref.at[half, pl.ds(0, 64), pl.ds(lo, size), :],
                )
            )

    def wait(self):
        for place in range(len(self.started)):
            self.copy(place).wait()


def fetch_layers(copies, sources, raw, w2_ref):
    spread_in, east_in, north_in, w1_in, bias_in, w2_in = sources
    raw_w1, raw_bias, numbers = raw
    copies.fetch(lambda: (w1_in, raw_w1))
    copies.fetch(lambda: (w2_in, w2_ref))
    copies.fetch(lambda: (bias_in, raw_bias))
    for row, source in enumerate((spread_in, east_in, north_in)):
        copies.fetch(lambda row=row, source=source: (source, numbers.at[pl.ds(row, 1)]))


def prepare_layers(raw, coef_ref, w1_ref, bias_ref, w2_ref, last_ref):
    raw_w1, raw_bias, numbers = raw
    w1_ref[...] = raw_w1[...] * jnp.asarray(0.5, BF16)
    bias_ref[...] = raw_bias[...] * 0.5
    spread, east, north = (numbers[i : i + 1] for i in range(3))
    coef_ref[0:1] = 1.0 - 4.0 * spread
    coef_ref[1:2] = spread - 0.5 * east
    coef_ref[2:3] = spread + 0.5 * east
    coef_ref[3:4] = spread - 0.5 * north
    coef_ref[4:5] = spread + 0.5 * north
    lane = iota((1, LANES), 1)
    first = w2_ref[:, :LANES].astype(F32)
    second = pltpu.roll(w2_ref[:, LANES:].astype(F32), 1, 1)
    last_ref[...] = jnp.where(lane == 0, first, jnp.where(lane == 1, second, 0.0)).astype(BF16)


def load_kernel(
    air_in, land_in, inc_in, idx_in, water_in, ocean_in, driver_in, mixing_in, spread_in, east_in,
    north_in, w1_in, bias_in, w2_in,
    send1_ref, send2_ref, air_ref, coef_ref, w1_ref, bias_ref, w2_ref, last_ref,
    cell_ref, count_ref, acc_ref, side_ref, idx_ref, land_ref, water_ref, ocean_ref, driver_ref,
    mixing_ref, inc_ref, numbers, raw_bias, raw_w1, turned, sem,
):
    early = loads_all()
    ours = side_turn() == 0
    raw = (raw_w1, raw_bias, numbers)
    columns = Copies(sem, 0)
    columns.fetch(lambda: (inc_in, inc_ref))
    columns.fetch(lambda: (idx_in, idx_ref))
    slabs = Copies(sem, columns.next)
    slabs.rows(air_in, air_ref, 0, 8)
    slabs.rows(air_in, air_ref, 24, 8)
    layers = Copies(sem, slabs.next)

    @pl.when(early)
    def _():
        fetch_layers(layers, (spread_in, east_in, north_in, w1_in, bias_in, w2_in), raw, w2_ref)
        layers.rows(air_in, air_ref, 8, 16)

    others = Copies(sem, layers.next)
    sides = (land_in, water_in, ocean_in, driver_in, mixing_in)
    side_refs = (land_ref, water_ref, ocean_ref, driver_ref, mixing_ref)

    for source, target in zip(sides, side_refs):
        others.fetch(lambda source=source, target=target: (source, target))
    acc_ref[...] = jnp.zeros_like(acc_ref)
    columns.wait()
    group_rows(idx_ref, inc_ref, turned, cell_ref, count_ref)
    slabs.wait()
    upper = jnp.where(is_even("gy"), 30, 0)
    for send, first in ((send1_ref, upper), (send2_ref, 30 - upper)):
        for half in range(2):
            flat = air_ref.at[half].reshape(65 * 32, LANES)
            for k in range(2):
                send[pl.ds(k * 64, 64), lanes_of(half)] = flat[pl.ds(first + k, 64, stride=32), :]

    others.wait()

    @pl.when(early)
    def _():
        layers.wait()
        prepare_layers(raw, coef_ref, w1_ref, bias_ref, w2_ref, last_ref)

    matrix_refs = (w1_ref, bias_ref, w2_ref, last_ref)
    tile_refs = (air_ref, coef_ref, matrix_refs, cell_ref, count_ref, acc_ref)
    some = early_tiles() > 0

    @pl.when(ours & jnp.logical_not(some))
    def _():
        side_parts(idx_ref, side_refs, side_ref)

    @pl.when(ours & some)
    def _():
        side_parts(idx_ref, side_refs, side_ref)
        add_tile(jnp.int32(0), tile_refs)

    @pl.when(jnp.logical_not(ours) & some)
    def _():
        add_tile(jnp.int32(0), tile_refs)


VMEM = pl.BlockSpec(memory_space=pltpu.VMEM)


def params(size):
    return pltpu.CompilerParams(vmem_limit_bytes=size << 20)


def cost(flops):
    return pl.CostEstimate(flops=flops, bytes_accessed=1 << 20, transcendentals=1 << 10)


SIDE = [
    ((32, 64), F32),
    ((16, 32), jnp.int32),
    ((2, 32, 16, 80), F32),
    ((2, 16, 32), F32),
    ((80, 80), F32),
]
LAYER_SCRATCH = [
    pltpu.VMEM((8, 256), F32),
    pltpu.VMEM((1, 512), F32),
    pltpu.VMEM((256, 512), BF16),
]
CORE = [
    ((2, 65, 32, LANES), F32),
    ((8, 256), F32),
    ((256, 512), BF16),
    ((1, 512), F32),
    ((512, 256), BF16),
    ((512, LANES), BF16),
]


def shapes_of(shapes):
    return [jax.ShapeDtypeStruct(*shape) for shape in shapes]


def load(arrays):
    shapes = [((LANES, 256), F32)] * 2 + CORE
    shapes += [
        ((24, LANES), jnp.int32),
        ((24, LANES), F32),
        ((LANES, 16), F32),
        ((5, 16, 32), F32),
        ((32, 64), jnp.int32),
    ] + SIDE
    return pl.pallas_call(
        load_kernel,
        out_shape=shapes_of(shapes),
        in_specs=[pl.BlockSpec(memory_space=pl.ANY)] * 14,
        out_specs=[VMEM] * len(shapes),
        scratch_shapes=[pltpu.VMEM((8, 1024), jnp.int32)]
        + LAYER_SCRATCH
        + [pltpu.VMEM((LANES, LANES), F32), pltpu.SemaphoreType.DMA((24,))],
        compiler_params=params(24),
        cost_estimate=cost(1 << 20),
    )(*arrays)


def ocean_fields(water, driver_ref, ocean_ref, mixing_ref):
    levels = mixing_ref.shape[0]
    matrix = mixing_ref[...]
    wide = jnp.concatenate([matrix, jnp.zeros((levels, LANES - levels), F32)], 1)
    tall = jnp.concatenate([wide, jnp.zeros((LANES - levels, LANES), F32)], 0)
    turned = jnp.transpose(tall)[:levels]
    column = (iota((levels, 1), 0) == 0).astype(F32)
    total = jnp.zeros((1, 1), F32)
    for _ in range(PAIRS):
        row = jnp.sum(column * wide, axis=0, keepdims=True)
        total = total + row[:, 0:1]
        column = jnp.sum(turned * row, axis=1, keepdims=True)
        total = total + column[0:1]
    spread = jnp.concatenate(
        [jnp.broadcast_to(column, (levels, LANES)), jnp.zeros((LANES - levels, LANES), F32)], 0
    )
    row = jnp.transpose(spread)[0:1, :levels]
    fields = []
    for field in range(2):
        block = ocean_ref[field]
        mixed = jnp.transpose(jnp.sum(block * row, axis=2))
        mixed = mixed + (OCEAN_STEP * total) * driver_ref[field]
        fields.append(jnp.where(water == 1, mixed, jnp.transpose(block[:, :, 0])))
    return fields


def land_sums(land, cells):
    lands = jnp.concatenate([land[y : y + 1] for y in range(32)], 1)
    places = jnp.concatenate([cells[y : y + 1] for y in range(32)], 1)
    first, second = one_hots(places)
    sums = scatter([lands, jnp.tanh(lands)], first, second)
    ones = first.astype(F32).astype(BF16)
    return sums, lax.dot_general(ones, second, NT, preferred_element_type=F32)


def side_parts(idx_ref, refs, side_ref):
    land_ref, water_ref, ocean_ref, driver_ref, mixing_ref = refs
    water = water_ref[...]
    fields = ocean_fields(water, driver_ref, ocean_ref, mixing_ref)
    sums, count = land_sums(land_ref[...], idx_ref[...])
    land = jnp.transpose(sums[0:32] + sums[32:64])
    warm = jnp.transpose(sums[64:96] + sums[96:128])
    count = jnp.transpose(count)
    side_ref[0] = fields[0]
    side_ref[1] = fields[1]
    side_ref[2] = jnp.where(water == 1, count * fields[0], land)
    side_ref[3] = jnp.where(water == 1, count * jnp.tanh(fields[0]), warm)
    side_ref[4] = jnp.maximum(count, 1.0)


def middle_kernel(
    air_old, coef_old, w1_old, bias_old, w2_old, last_old, cell_ref, count_ref, idx_ref, land_ref,
    water_ref, ocean_ref, driver_ref, mixing_ref, air_in, spread_in, east_in, north_in, w1_in,
    bias_in, w2_in,
    air_ref, coef_ref, w1_ref, bias_ref, w2_ref, last_ref, acc_ref, side_ref,
    numbers, raw_bias, raw_w1, sem,
):
    early = early_tiles()
    raw = (raw_w1, raw_bias, numbers)
    layers = Copies(sem, 0)

    @pl.when(jnp.logical_not(loads_all()))
    def _():
        fetch_layers(layers, (spread_in, east_in, north_in, w1_in, bias_in, w2_in), raw, w2_ref)
        layers.rows(air_in, air_ref, 8, 16)

    ours = side_turn() == 1
    side_refs = (land_ref, water_ref, ocean_ref, driver_ref, mixing_ref)
    matrix_refs = (w1_ref, bias_ref, w2_ref, last_ref)
    tile_refs = (air_ref, coef_ref, matrix_refs, cell_ref, count_ref, acc_ref)
    acc_ref[...] = jnp.zeros_like(acc_ref)
    both = ours & loads_all()

    @pl.when(ours & jnp.logical_not(both))
    def _():
        side_parts(idx_ref, side_refs, side_ref)

    @pl.when(jnp.logical_not(loads_all()))
    def _():
        layers.wait()
        prepare_layers(raw, coef_ref, w1_ref, bias_ref, w2_ref, last_ref)

    @pl.when(both)
    def _():
        side_parts(idx_ref, side_refs, side_ref)
        add_tile(early, tile_refs)

    tiles(early + both.astype(jnp.int32), early + middle_tiles(), *tile_refs)


def middle(core, sides, sources):
    shapes = CORE + [((LANES, 16), F32), ((5, 16, 32), F32)]
    return pl.pallas_call(
        middle_kernel,
        out_shape=shapes_of(shapes),
        in_specs=[VMEM] * 14 + [pl.BlockSpec(memory_space=pl.ANY)] * 7,
        out_specs=[VMEM] * len(shapes),
        input_output_aliases={i: i for i in range(len(CORE))},
        scratch_shapes=LAYER_SCRATCH + [pltpu.SemaphoreType.DMA((24,))],
        compiler_params=params(24),
        cost_estimate=cost(1 << 30),
    )(*core, *sides, *sources)


def by_side(axis, first, second):
    even = is_even(axis)
    return jnp.where(even, second, first), jnp.where(even, first, second)


def slab_kernel(air_ref, recv1_ref, recv2_ref, pair_ref, cross_ref):
    even = is_even("gx")
    ylow, yhigh = by_side("gy", recv1_ref[...], recv2_ref[...])
    for half in range(2):
        lanes = lanes_of(half)
        low = air_ref[half, 0:2].reshape(64, LANES)
        high = air_ref[half, 62:64].reshape(64, LANES)
        pair_ref[0:64, lanes] = jnp.where(even, high, low)
        cross_ref[0:64, lanes] = jnp.where(even, low, high)
    low = jnp.concatenate([ylow[64:65], yhigh[0:1], jnp.zeros((6, 256), F32)], 0)
    high = jnp.concatenate([ylow[127:128], yhigh[63:64], jnp.zeros((6, 256), F32)], 0)
    pair_ref[64:72] = jnp.where(even, high, low)
    cross_ref[64:72] = jnp.where(even, low, high)


def x_slabs(air, recv1, recv2):
    return pl.pallas_call(
        slab_kernel,
        out_shape=[jax.ShapeDtypeStruct((72, 256), F32)] * 2,
        in_specs=[VMEM] * 3,
        out_specs=[VMEM] * 2,
        compiler_params=params(16),
        cost_estimate=cost(1 << 10),
    )(air, recv1, recv2)


def late_kernel(
    air_ref, coef_ref, w1_ref, bias_ref, w2_ref, last_ref, cell_ref, count_ref, recv1_ref,
    recv2_ref, send1_ref, send2_ref, acc_ref, edge_ref,
):
    acc_ref[...] = jnp.zeros_like(acc_ref)
    for half in range(2):
        lanes = lanes_of(half)
        ylow, yhigh = by_side("gy", recv1_ref[:, lanes], recv2_ref[:, lanes])
        first, last = by_side("gy", send1_ref[:, lanes], send2_ref[:, lanes])
        along_x = y_edge_state(half, air_ref, coefs_of(coef_ref, half), ylow, yhigh, first, last)
        edge_ref[half] = jnp.concatenate(along_x, 0)
    matrix_refs = (w1_ref, bias_ref, w2_ref, last_ref)
    first = early_tiles() + middle_tiles()
    tiles(first, jnp.int32(TILES), air_ref, coef_ref, matrix_refs, cell_ref, count_ref, acc_ref)


def late(core, halos):
    return pl.pallas_call(
        late_kernel,
        out_shape=[
            jax.ShapeDtypeStruct((LANES, 16), F32),
            jax.ShapeDtypeStruct((2, 2 * LANES, LANES), F32),
        ],
        in_specs=[VMEM] * 12,
        out_specs=[VMEM] * 2,
        compiler_params=params(24),
        cost_estimate=cost(1 << 30),
    )(*core, *halos)


def y_edge_state(half, air_ref, coefs, ylow, yhigh, first, last):
    flat = air_ref.at[half].reshape(65 * 32, LANES)

    def step(block):
        centre = block[1:-1]
        plus_x = pltpu.roll(centre, 63, 1)
        minus_x = pltpu.roll(centre, 1, 1)
        return combine(coefs, centre, plus_x, minus_x, block[2:], block[:-2])

    states = []
    for low in (True, False):
        ys = (2, 3) if low else (28, 29)
        inner = jnp.stack([flat[pl.ds(y, 64, stride=32), :] for y in ys], 0)
        outer = (first if low else last).reshape(2, 64, LANES)
        halo = (ylow if low else yhigh).reshape(2, 64, LANES)
        block = jnp.concatenate([halo, outer, inner] if low else [inner, outer, halo], 0)
        states.append(step(step(block)).reshape(LANES, LANES))
    return states


def x_edge_state(half, air_ref, coefs, ylow, yhigh, xlow, xhigh):
    def with_ends(row, first, last):
        at = iota(row.shape, 0)
        size = row.shape[0]
        plus_y = jnp.where(at == size - 1, last, pltpu.roll(row, size - 1, 0))
        minus_y = jnp.where(at == 0, first, pltpu.roll(row, 1, 0))
        return plus_y, minus_y

    def own(x):
        return air_ref[half, x]

    def beyond(x, y):
        slab = ylow if y < 0 else yhigh
        at = (y + 2 if y < 0 else y - 32) * 64 + x
        return slab[at : at + 1]

    done = []
    for low in (True, False):
        halo = xlow if low else xhigh
        near, far = (halo[32:64], halo[0:32]) if low else (halo[0:32], halo[32:64])
        xs = [0, 1, 2, 3] if low else [63, 62, 61, 60]
        rows = [far, near] + [own(x) for x in xs]
        ends = [None, (halo[64:65], halo[65:66])] + [(beyond(x, -1), beyond(x, 32)) for x in xs]
        outer = [None, None] + [(beyond(x, -2), beyond(x, 33)) for x in xs]

        def apply(centre, outward, inward, plus_y, minus_y):
            plus_x, minus_x = (inward, outward) if low else (outward, inward)
            return combine(coefs, centre, plus_x, minus_x, plus_y, minus_y)

        once = {}
        for i in range(1, 5):
            plus_y, minus_y = with_ends(rows[i], *ends[i])
            once[i] = apply(rows[i], rows[i - 1], rows[i + 1], plus_y, minus_y)
        twice = []
        for i in (2, 3):
            first = apply(
                ends[i][0], ends[i - 1][0], ends[i + 1][0], rows[i][0:1], outer[i][0]
            )
            last = apply(
                ends[i][1], ends[i - 1][1], ends[i + 1][1], outer[i][1], rows[i][31:32]
            )
            plus_y, minus_y = with_ends(once[i], first, last)
            twice.append(apply(once[i], once[i - 1], once[i + 1], plus_y, minus_y))
        done += twice if low else twice[::-1]
    return jnp.concatenate(done, 0)


def edge_kernel(
    air_ref, coef_ref, w1_ref, bias_ref, w2_ref, last_ref, cell_ref, count_ref, recv1_ref,
    recv2_ref, pair_ref, cross_ref, edge_ref, acc0_ref, acc1_ref, acc2_ref, side0_ref, side1_ref,
    out_ref,
):
    state = []
    for half in range(2):
        lanes = lanes_of(half)
        ylow, yhigh = by_side("gy", recv1_ref[:, lanes], recv2_ref[:, lanes])
        xlow, xhigh = by_side("gx", pair_ref[:, lanes], cross_ref[:, lanes])
        coefs = coefs_of(coef_ref, half)
        along_y = x_edge_state(half, air_ref, coefs, ylow, yhigh, xlow, xhigh)
        state.append(jnp.concatenate([edge_ref[half], along_y], 0))
    matrices = matrices_of(w1_ref, bias_ref, w2_ref, last_ref)
    groups = [GROUPS * TILES + g for g in range(3)]
    acc = finish(state, groups, matrices, cell_ref, count_ref, EDGE_CHUNKS)
    acc = acc + (acc0_ref[...] + acc1_ref[...] + acc2_ref[...])
    heat = jnp.transpose(acc[0:32] + acc[32:64])
    vapour = jnp.transpose(acc[64:96] + acc[96:128])
    turn = side_turn()

    def side(index):
        return jnp.where(turn == 0, side0_ref[index], side1_ref[index])

    below = side(4)
    ocean = lax.axis_index("sect") == 1
    flux = THERMAL_FACTOR * (side(2) - heat) / below
    out_ref[0] = jnp.where(ocean, side(0), flux)
    flux = WETNESS_FACTOR * (side(3) - vapour) / below
    out_ref[1] = jnp.where(ocean, side(1), flux)


def edges(core, halos, others):
    return pl.pallas_call(
        edge_kernel,
        out_shape=jax.ShapeDtypeStruct((2, 16, 32), F32),
        in_specs=[VMEM] * 18,
        out_specs=VMEM,
        compiler_params=params(24),
        cost_estimate=cost(1 << 28),
    )(*core, *halos, *others)


def exchanges(axis, first):
    sizes = [lax.axis_size(name) for name in AXES]
    size = lax.axis_size(axis)
    pairs = []
    for device in range(sizes[0] * sizes[1] * sizes[2]):
        at = [device // (sizes[1] * sizes[2]), device // sizes[2] % sizes[1], device % sizes[2]]
        dim = AXES.index(axis)
        step = 1 if (at[dim] - first) % 2 == 0 else -1
        at[dim] = (at[dim] + step) % size
        pairs.append((device, (at[0] * sizes[1] + at[1]) * sizes[2] + at[2]))
    return pairs


def shards(
    air_profile_matrix,
    spreading_numbers,
    eastward_advection_number,
    northward_advection_number,
    landmass_warmth,
    physics_increments,
    underlying_water_index,
    water_indicator,
    waterbody_profiles,
    waterbody_drivers,
    inverted_blending_matrix,
    entry_layer_matrix,
    entry_layer_offset,
    exit_layer_matrix,
):
    air = air_profile_matrix
    sides = (
        landmass_warmth.T,
        water_indicator.T,
        waterbody_profiles.transpose(0, 2, 3, 1),
        waterbody_drivers.transpose(0, 2, 1),
        inverted_blending_matrix,
    )
    layers = (
        spreading_numbers.reshape(1, -1),
        eastward_advection_number.reshape(1, -1),
        northward_advection_number.reshape(1, -1),
        entry_layer_matrix,
        entry_layer_offset.reshape(1, -1),
        exit_layer_matrix,
    )
    columns = (physics_increments.T, underlying_water_index.T)
    air, sides, layers, columns = jax.tree.map(
        lambda array: pltpu.with_memory_space_constraint(array, pltpu.HBM),
        (air, sides, layers, columns),
    )
    loaded = load((air, sides[0], *columns, *sides[1:], *layers))
    send1, send2 = loaded[:2]
    acc0, side0 = loaded[10:12]
    recv2 = lax.ppermute(send2, AXES, exchanges("gy", 1))
    recv1 = lax.ppermute(send1, AXES, exchanges("gy", 0))
    *core, acc1, side1 = middle(loaded[2:10], loaded[12:], (air, *layers))
    core += loaded[8:10]
    acc1, recv2, recv1 = lax.optimization_barrier((acc1, recv2, recv1))
    send_pair, send_cross = x_slabs(core[0], recv1, recv2)
    cross = lax.ppermute(send_cross, AXES, exchanges("gx", 1))
    pair = lax.ppermute(send_pair, AXES, exchanges("gx", 0))
    acc2, edge = late(core, (recv1, recv2, send1, send2))
    acc2, cross, pair = lax.optimization_barrier((acc2, cross, pair))
    result = edges(
        core, (recv1, recv2, pair, cross), (edge, acc0, acc1, acc2, side0, side1)
    )
    return result.transpose(0, 2, 1)[None]


def solution(mesh):
    in_specs = (
        P("gx", "gy", None),
        P(),
        P(),
        P(),
        P("gx", "gy"),
        P(None, "gy"),
        P("gx", "gy"),
        P("gx", "gy"),
        P(None, None, "gx", "gy"),
        P(None, "gx", "gy"),
        P(),
        P(),
        P(),
        P(),
    )
    out_specs = P("sect", None, "gx", "gy")
    return jax.shard_map(shards, mesh=mesh, in_specs=in_specs, out_specs=out_specs, check_vma=False)
```

```python
import jax
import jax.numpy as jnp
from jax import lax
from jax.experimental import pallas as pl
from jax.experimental.pallas import tpu as pltpu
from jax.sharding import PartitionSpec as P

BS = 4
PAIRS = 6
THERMAL_FACTOR = 0.8
WETNESS_FACTOR = 0.6
OCEAN_STEP = 0.1
TANH_SCALE = 0.7978845608028654
TANH_CUBE = 0.044715

GROUPS = 5
TILES = 3
TILE_CHUNKS = (320, 320)
EDGE_CHUNKS = (384,)
LANES = 128
NT = (((1,), (1,)), ((), ()))
F32 = jnp.float32
BF16 = jnp.bfloat16
AXES = ("sect", "gx", "gy")


def iota(shape, dim):
    return lax.broadcasted_iota(jnp.int32, shape, dim)


def combine(coefs, centre, plus_x, minus_x, plus_y, minus_y):
    c0, cxp, cxm, cyp, cym = coefs
    return c0 * centre + cxp * plus_x + cxm * minus_x + cyp * plus_y + cym * minus_y


def advance(block, coefs):
    centre = block[1:-1]
    size = centre.shape[1]
    plus_y = pltpu.roll(centre, size - 1, 1)
    minus_y = pltpu.roll(centre, 1, 1)
    return combine(coefs, centre, block[2:], block[:-2], plus_y, minus_y)


def lanes_of(half):
    return pl.ds(half * LANES, LANES)


def coefs_of(coef_ref, half):
    return [coef_ref[i : i + 1, lanes_of(half)] for i in range(5)]


def hidden_of(state, w1, bias):
    inputs = jnp.concatenate([part.astype(BF16) for part in state], 1)
    half = jnp.dot(inputs, w1, preferred_element_type=F32) + bias
    inner = half * (half * half * (8.0 * TANH_SCALE * TANH_CUBE) + 2.0 * TANH_SCALE)
    return (half * jnp.tanh(inner) + half).astype(BF16)


def physics(state, counts, matrices, sizes):
    w1, bias, w2, w2_last = matrices
    places = [sum(sizes[:i]) for i in range(len(sizes))]
    states = [[part[at : at + n] for part in state] for at, n in zip(places, sizes)]
    counts = [counts[at : at + n] for at, n in zip(places, sizes)]
    lane = iota((1, LANES), 1)
    for index in range(3):
        for chunk, needs in enumerate(counts):
            hidden = hidden_of(states[chunk], w1, bias)
            delta = jnp.dot(hidden, w2, preferred_element_type=F32)
            parts = [delta[:, :LANES], delta[:, LANES:]]
            if index:
                needed = needs > float(index)
                parts = [jnp.where(needed, part, 0.0) for part in parts]
            states[chunk] = [old + part for old, part in zip(states[chunk], parts)]
    kept = []
    for (first, second), needs in zip(states, counts):
        hidden = hidden_of([first, second], w1, bias)
        delta = jnp.dot(hidden, w2_last, preferred_element_type=F32)
        both = jnp.where(lane == 0, first, pltpu.roll(second, 1, 1))
        kept.append(both + jnp.where(needs > 3.0, delta, 0.0))
    return jnp.concatenate(kept, 0)


def expand_counts(row):
    square = (LANES, LANES)
    diagonal = jnp.where(iota(square, 0) == iota(square, 1), row, 0.0).astype(BF16)
    return jnp.dot(diagonal, jnp.ones(square, BF16), preferred_element_type=F32)


def split(row):
    high = row.astype(BF16).astype(F32)
    return high, row - high


def one_hots(cells):
    n = cells.shape[1]
    first = iota((32, n), 0) == jnp.right_shift(cells, 4)
    second = (iota((16, n), 0) == jnp.bitwise_and(cells, 15)) & (cells >= 0)
    return first, second.astype(F32).astype(BF16)


def scatter(values, first, second):
    rows = []
    for value in values:
        for part in split(value):
            rows.append(jnp.where(first, part, 0.0))
    stacked = jnp.concatenate(rows, 0).astype(BF16)
    return lax.dot_general(stacked, second, NT, preferred_element_type=F32)


def scatter_columns(kept, cells):
    n = kept.shape[0]
    rows = [jnp.transpose(kept[i : i + LANES])[:2] for i in range(0, n, LANES)]
    flat = jnp.concatenate(rows, 1)
    first, second = one_hots(cells)
    return scatter([flat[0:1], flat[1:2]], first, second)


def column_codes(idx_ref, inc_ref):
    gx = lax.axis_index("gx")
    start = pl.multiple_of((gx // 2) * LANES, LANES)
    block = inc_ref[:, pl.ds(start, LANES)].astype(F32)
    block = jnp.where(gx % 2 == 1, pltpu.roll(block, 64, 1), block)
    spread = (iota((32, 8), 0) // BS == iota((32, 8), 1)).astype(F32)
    counts = jnp.dot(spread.astype(BF16), block.astype(BF16), preferred_element_type=F32)
    cells = idx_ref[...].astype(F32)
    return jnp.concatenate([cells, jnp.zeros_like(cells)], 1) * 8.0 + counts


def group_rows(idx_ref, inc_ref, turned, cell_ref, count_ref):
    code = column_codes(idx_ref, inc_ref)
    turned[...] = jnp.transpose(jnp.concatenate([code, jnp.zeros((96, LANES), F32)], 0))
    count = GROUPS * TILES
    parts = [turned[pl.ds(2 + j, count, stride=4), :][:, :32] for j in range(4)]
    inner = jnp.concatenate(parts, 1)
    along_y = jnp.concatenate([turned[i : i + 1, :][:, :32] for i in (0, 1, 62, 63)], 1)
    along_x = [
        jnp.concatenate([code[i : i + 1, :64], code[i + 1 : i + 2, :64]], 1) for i in (0, 30)
    ]
    whole = jnp.concatenate([inner] + along_x + [along_y], 0).astype(jnp.int32)
    cells = jnp.right_shift(whole, 3)
    row = iota(whole.shape, 0)
    place = jnp.bitwise_and(iota(whole.shape, 1), jnp.where(row < count, 31, 63))
    masked = (place < 2) | (place >= jnp.where(row < count, 30, 62))
    masked = masked & (row < count + 2)
    cell_ref[pl.ds(0, count + 3), :] = jnp.where(masked, -1, cells)
    count_ref[pl.ds(0, count + 3), :] = jnp.bitwise_and(whole, 7).astype(F32)


def row_at(ref, index):
    return ref[pl.ds(index, 1), :]


def matrices_of(w1_ref, bias_ref, w2_ref, last_ref):
    return w1_ref[...], bias_ref[...], w2_ref[...], last_ref[...]


def tile_state(air_ref, coef_ref, tile):
    state = []
    for half in range(2):
        block = air_ref[half, pl.ds(tile * (4 * GROUPS), 4 * GROUPS + 4)]
        coefs = coefs_of(coef_ref, half)
        state.append(advance(advance(block, coefs), coefs).reshape(GROUPS * LANES, LANES))
    return state


def finish(state, groups, matrices, cell_ref, count_ref, sizes):
    needs = [expand_counts(row_at(count_ref, g)) for g in groups]
    kept = physics(state, jnp.concatenate(needs, 0), matrices, sizes)
    cells = jnp.concatenate([row_at(cell_ref, g) for g in groups], 1)
    return scatter_columns(kept, cells)


def add_tile(tile, refs):
    air_ref, coef_ref, matrix_refs, cell_ref, count_ref, acc_ref = refs
    state = tile_state(air_ref, coef_ref, tile)
    groups = [tile * GROUPS + g for g in range(GROUPS)]
    matrices = matrices_of(*matrix_refs)
    acc_ref[...] += finish(state, groups, matrices, cell_ref, count_ref, TILE_CHUNKS)


def tiles(lo, hi, *refs):
    @pl.loop(lo, hi)
    def _(tile):
        add_tile(tile, refs)


def early_tiles():
    gy = lax.axis_index("gy")
    return jnp.where(gy < 2, 1, 0).astype(jnp.int32)


def loads_all():
    return lax.axis_index("gy") < 4


def middle_tiles():
    place = lax.axis_index("gx") % 8
    waiting = (place == 1) | ((place == 3) & (lax.axis_index("gy") >= 2))
    return jnp.where(waiting, 2, 1).astype(jnp.int32)


def is_even(axis):
    return lax.axis_index(axis) % 2 == 0


def side_turn():
    gy = lax.axis_index("gy")
    return jnp.where((gy < 4) & (gy != 1), 0, 1)


class Copies:
    def __init__(self, sem, first):
        self.sem = sem
        self.next = first
        self.started = []

    def copy(self, place):
        index, ends = self.started[place]
        return pltpu.make_async_copy(*ends(), self.sem.at[index])

    def fetch(self, ends):
        self.started.append((self.next, ends))
        self.next += 1
        self.copy(len(self.started) - 1).start()

    def rows(self, air_in, air_ref, lo, size):
        for half in range(2):
            self.fetch(
                lambda half=half: (
                    air_in.at[:, pl.ds(lo, size), lanes_of(half)],
                    air_ref.at[half, pl.ds(0, 64), pl.ds(lo, size), :],
                )
            )

    def wait(self):
        for place in range(len(self.started)):
            self.copy(place).wait()


def fetch_layers(copies, sources, raw, w2_ref):
    spread_in, east_in, north_in, w1_in, bias_in, w2_in = sources
    raw_w1, raw_bias, numbers = raw
    copies.fetch(lambda: (w1_in, raw_w1))
    copies.fetch(lambda: (w2_in, w2_ref))
    copies.fetch(lambda: (bias_in, raw_bias))
    for row, source in enumerate((spread_in, east_in, north_in)):
        copies.fetch(lambda row=row, source=source: (source, numbers.at[pl.ds(row, 1)]))


def prepare_layers(raw, coef_ref, w1_ref, bias_ref, w2_ref, last_ref):
    raw_w1, raw_bias, numbers = raw
    w1_ref[...] = raw_w1[...] * jnp.asarray(0.5, BF16)
    bias_ref[...] = raw_bias[...] * 0.5
    spread, east, north = (numbers[i : i + 1] for i in range(3))
    coef_ref[0:1] = 1.0 - 4.0 * spread
    coef_ref[1:2] = spread - 0.5 * east
    coef_ref[2:3] = spread + 0.5 * east
    coef_ref[3:4] = spread - 0.5 * north
    coef_ref[4:5] = spread + 0.5 * north
    lane = iota((1, LANES), 1)
    first = w2_ref[:, :LANES].astype(F32)
    second = pltpu.roll(w2_ref[:, LANES:].astype(F32), 1, 1)
    last_ref[...] = jnp.where(lane == 0, first, jnp.where(lane == 1, second, 0.0)).astype(BF16)


def load_kernel(
    air_in, land_in, inc_in, idx_in, water_in, ocean_in, driver_in, mixing_in, spread_in, east_in,
    north_in, w1_in, bias_in, w2_in,
    send1_ref, send2_ref, air_ref, coef_ref, w1_ref, bias_ref, w2_ref, last_ref,
    cell_ref, count_ref, acc_ref, side_ref, idx_ref, land_ref, water_ref, ocean_ref, driver_ref,
    mixing_ref, inc_ref, numbers, raw_bias, raw_w1, turned, sem,
):
    early = loads_all()
    ours = side_turn() == 0
    raw = (raw_w1, raw_bias, numbers)
    columns = Copies(sem, 0)
    columns.fetch(lambda: (inc_in, inc_ref))
    columns.fetch(lambda: (idx_in, idx_ref))
    slabs = Copies(sem, columns.next)
    slabs.rows(air_in, air_ref, 0, 8)
    slabs.rows(air_in, air_ref, 24, 8)
    layers = Copies(sem, slabs.next)

    @pl.when(early)
    def _():
        fetch_layers(layers, (spread_in, east_in, north_in, w1_in, bias_in, w2_in), raw, w2_ref)
        layers.rows(air_in, air_ref, 8, 16)

    others = Copies(sem, layers.next)
    sides = (land_in, water_in, ocean_in, driver_in, mixing_in)
    side_refs = (land_ref, water_ref, ocean_ref, driver_ref, mixing_ref)

    for source, target in zip(sides, side_refs):
        others.fetch(lambda source=source, target=target: (source, target))
    acc_ref[...] = jnp.zeros_like(acc_ref)
    columns.wait()
    group_rows(idx_ref, inc_ref, turned, cell_ref, count_ref)

    def extract(low_send, high_send):
        for place, (send, first) in enumerate(((low_send, 0), (high_send, 30))):
            for half in range(2):
                slabs.copy(2 * place + half).wait()
                flat = air_ref.at[half].reshape(65 * 32, LANES)
                for k in range(2):
                    rows = flat[pl.ds(first + k, 64, stride=32), :]
                    send[pl.ds(k * 64, 64), lanes_of(half)] = rows

    @pl.when(is_even("gy"))
    def _():
        extract(send2_ref, send1_ref)

    @pl.when(jnp.logical_not(is_even("gy")))
    def _():
        extract(send1_ref, send2_ref)

    others.wait()

    @pl.when(early)
    def _():
        layers.wait()
        prepare_layers(raw, coef_ref, w1_ref, bias_ref, w2_ref, last_ref)

    matrix_refs = (w1_ref, bias_ref, w2_ref, last_ref)
    tile_refs = (air_ref, coef_ref, matrix_refs, cell_ref, count_ref, acc_ref)
    some = early_tiles() > 0

    @pl.when(ours & jnp.logical_not(some))
    def _():
        side_parts(idx_ref, side_refs, side_ref)

    @pl.when(ours & some)
    def _():
        side_parts(idx_ref, side_refs, side_ref)
        add_tile(jnp.int32(0), tile_refs)

    @pl.when(jnp.logical_not(ours) & some)
    def _():
        add_tile(jnp.int32(0), tile_refs)


VMEM = pl.BlockSpec(memory_space=pltpu.VMEM)


def params(size):
    return pltpu.CompilerParams(vmem_limit_bytes=size << 20)


def cost(flops):
    return pl.CostEstimate(flops=flops, bytes_accessed=1 << 20, transcendentals=1 << 10)


SIDE = [
    ((32, 64), F32),
    ((16, 32), jnp.int32),
    ((2, 32, 16, 80), F32),
    ((2, 16, 32), F32),
    ((80, 80), F32),
]
LAYER_SCRATCH = [
    pltpu.VMEM((8, 256), F32),
    pltpu.VMEM((1, 512), F32),
    pltpu.VMEM((256, 512), BF16),
]
CORE = [
    ((2, 65, 32, LANES), F32),
    ((8, 256), F32),
    ((256, 512), BF16),
    ((1, 512), F32),
    ((512, 256), BF16),
    ((512, LANES), BF16),
]


def shapes_of(shapes):
    return [jax.ShapeDtypeStruct(*shape) for shape in shapes]


def load(arrays):
    shapes = [((LANES, 256), F32)] * 2 + CORE
    shapes += [
        ((24, LANES), jnp.int32),
        ((24, LANES), F32),
        ((LANES, 16), F32),
        ((5, 16, 32), F32),
        ((32, 64), jnp.int32),
    ] + SIDE
    return pl.pallas_call(
        load_kernel,
        out_shape=shapes_of(shapes),
        in_specs=[pl.BlockSpec(memory_space=pl.ANY)] * 14,
        out_specs=[VMEM] * len(shapes),
        scratch_shapes=[pltpu.VMEM((8, 1024), jnp.int32)]
        + LAYER_SCRATCH
        + [pltpu.VMEM((LANES, LANES), F32), pltpu.SemaphoreType.DMA((24,))],
        compiler_params=params(24),
        cost_estimate=cost(1 << 20),
    )(*arrays)


def ocean_fields(water, driver_ref, ocean_ref, mixing_ref):
    levels = mixing_ref.shape[0]
    matrix = mixing_ref[...]
    wide = jnp.concatenate([matrix, jnp.zeros((levels, LANES - levels), F32)], 1)
    tall = jnp.concatenate([wide, jnp.zeros((LANES - levels, LANES), F32)], 0)
    turned = jnp.transpose(tall)[:levels]
    column = (iota((levels, 1), 0) == 0).astype(F32)
    total = jnp.zeros((1, 1), F32)
    for _ in range(PAIRS):
        row = jnp.sum(column * wide, axis=0, keepdims=True)
        total = total + row[:, 0:1]
        column = jnp.sum(turned * row, axis=1, keepdims=True)
        total = total + column[0:1]
    spread = jnp.concatenate(
        [jnp.broadcast_to(column, (levels, LANES)), jnp.zeros((LANES - levels, LANES), F32)], 0
    )
    row = jnp.transpose(spread)[0:1, :levels]
    fields = []
    for field in range(2):
        block = ocean_ref[field]
        mixed = jnp.transpose(jnp.sum(block * row, axis=2))
        mixed = mixed + (OCEAN_STEP * total) * driver_ref[field]
        fields.append(jnp.where(water == 1, mixed, jnp.transpose(block[:, :, 0])))
    return fields


def land_sums(land, cells):
    lands = jnp.concatenate([land[y : y + 1] for y in range(32)], 1)
    places = jnp.concatenate([cells[y : y + 1] for y in range(32)], 1)
    first, second = one_hots(places)
    sums = scatter([lands, jnp.tanh(lands)], first, second)
    ones = first.astype(F32).astype(BF16)
    return sums, lax.dot_general(ones, second, NT, preferred_element_type=F32)


def side_parts(idx_ref, refs, side_ref):
    land_ref, water_ref, ocean_ref, driver_ref, mixing_ref = refs
    water = water_ref[...]
    fields = ocean_fields(water, driver_ref, ocean_ref, mixing_ref)
    sums, count = land_sums(land_ref[...], idx_ref[...])
    land = jnp.transpose(sums[0:32] + sums[32:64])
    warm = jnp.transpose(sums[64:96] + sums[96:128])
    count = jnp.transpose(count)
    side_ref[0] = fields[0]
    side_ref[1] = fields[1]
    side_ref[2] = jnp.where(water == 1, count * fields[0], land)
    side_ref[3] = jnp.where(water == 1, count * jnp.tanh(fields[0]), warm)
    side_ref[4] = jnp.maximum(count, 1.0)


def middle_kernel(
    air_old, coef_old, w1_old, bias_old, w2_old, last_old, cell_ref, count_ref, idx_ref, land_ref,
    water_ref, ocean_ref, driver_ref, mixing_ref, air_in, spread_in, east_in, north_in, w1_in,
    bias_in, w2_in,
    air_ref, coef_ref, w1_ref, bias_ref, w2_ref, last_ref, acc_ref, side_ref,
    numbers, raw_bias, raw_w1, sem,
):
    early = early_tiles()
    raw = (raw_w1, raw_bias, numbers)
    layers = Copies(sem, 0)

    @pl.when(jnp.logical_not(loads_all()))
    def _():
        fetch_layers(layers, (spread_in, east_in, north_in, w1_in, bias_in, w2_in), raw, w2_ref)
        layers.rows(air_in, air_ref, 8, 16)

    ours = side_turn() == 1
    side_refs = (land_ref, water_ref, ocean_ref, driver_ref, mixing_ref)
    matrix_refs = (w1_ref, bias_ref, w2_ref, last_ref)
    tile_refs = (air_ref, coef_ref, matrix_refs, cell_ref, count_ref, acc_ref)
    acc_ref[...] = jnp.zeros_like(acc_ref)
    both = ours & loads_all()

    @pl.when(ours & jnp.logical_not(both))
    def _():
        side_parts(idx_ref, side_refs, side_ref)

    @pl.when(jnp.logical_not(loads_all()))
    def _():
        layers.wait()
        prepare_layers(raw, coef_ref, w1_ref, bias_ref, w2_ref, last_ref)

    @pl.when(both)
    def _():
        side_parts(idx_ref, side_refs, side_ref)
        add_tile(early, tile_refs)

    tiles(early + both.astype(jnp.int32), early + middle_tiles(), *tile_refs)


def middle(core, sides, sources):
    shapes = CORE + [((LANES, 16), F32), ((5, 16, 32), F32)]
    return pl.pallas_call(
        middle_kernel,
        out_shape=shapes_of(shapes),
        in_specs=[VMEM] * 14 + [pl.BlockSpec(memory_space=pl.ANY)] * 7,
        out_specs=[VMEM] * len(shapes),
        input_output_aliases={i: i for i in range(len(CORE))},
        scratch_shapes=LAYER_SCRATCH + [pltpu.SemaphoreType.DMA((24,))],
        compiler_params=params(24),
        cost_estimate=cost(1 << 30),
    )(*core, *sides, *sources)


def by_side(axis, first, second):
    even = is_even(axis)
    return jnp.where(even, second, first), jnp.where(even, first, second)


def slab_kernel(air_ref, recv1_ref, recv2_ref, pair_ref, cross_ref):
    even = is_even("gx")
    ylow, yhigh = by_side("gy", recv1_ref[...], recv2_ref[...])
    for half in range(2):
        lanes = lanes_of(half)
        low = air_ref[half, 0:2].reshape(64, LANES)
        high = air_ref[half, 62:64].reshape(64, LANES)
        pair_ref[0:64, lanes] = jnp.where(even, high, low)
        cross_ref[0:64, lanes] = jnp.where(even, low, high)
    low = jnp.concatenate([ylow[64:65], yhigh[0:1], jnp.zeros((6, 256), F32)], 0)
    high = jnp.concatenate([ylow[127:128], yhigh[63:64], jnp.zeros((6, 256), F32)], 0)
    pair_ref[64:72] = jnp.where(even, high, low)
    cross_ref[64:72] = jnp.where(even, low, high)


def x_slabs(air, recv1, recv2):
    return pl.pallas_call(
        slab_kernel,
        out_shape=[jax.ShapeDtypeStruct((72, 256), F32)] * 2,
        in_specs=[VMEM] * 3,
        out_specs=[VMEM] * 2,
        compiler_params=params(16),
        cost_estimate=cost(1 << 10),
    )(air, recv1, recv2)


def late_kernel(
    air_ref, coef_ref, w1_ref, bias_ref, w2_ref, last_ref, cell_ref, count_ref, recv1_ref,
    recv2_ref, send1_ref, send2_ref, acc_ref, edge_ref,
):
    acc_ref[...] = jnp.zeros_like(acc_ref)
    for half in range(2):
        lanes = lanes_of(half)
        ylow, yhigh = by_side("gy", recv1_ref[:, lanes], recv2_ref[:, lanes])
        first, last = by_side("gy", send1_ref[:, lanes], send2_ref[:, lanes])
        along_x = y_edge_state(half, air_ref, coefs_of(coef_ref, half), ylow, yhigh, first, last)
        edge_ref[half] = jnp.concatenate(along_x, 0)
    matrix_refs = (w1_ref, bias_ref, w2_ref, last_ref)
    first = early_tiles() + middle_tiles()
    tiles(first, jnp.int32(TILES), air_ref, coef_ref, matrix_refs, cell_ref, count_ref, acc_ref)


def late(core, halos):
    return pl.pallas_call(
        late_kernel,
        out_shape=[
            jax.ShapeDtypeStruct((LANES, 16), F32),
            jax.ShapeDtypeStruct((2, 2 * LANES, LANES), F32),
        ],
        in_specs=[VMEM] * 12,
        out_specs=[VMEM] * 2,
        compiler_params=params(24),
        cost_estimate=cost(1 << 30),
    )(*core, *halos)


def y_edge_state(half, air_ref, coefs, ylow, yhigh, first, last):
    flat = air_ref.at[half].reshape(65 * 32, LANES)

    def step(block):
        centre = block[1:-1]
        plus_x = pltpu.roll(centre, 63, 1)
        minus_x = pltpu.roll(centre, 1, 1)
        return combine(coefs, centre, plus_x, minus_x, block[2:], block[:-2])

    states = []
    for low in (True, False):
        ys = (2, 3) if low else (28, 29)
        inner = jnp.stack([flat[pl.ds(y, 64, stride=32), :] for y in ys], 0)
        outer = (first if low else last).reshape(2, 64, LANES)
        halo = (ylow if low else yhigh).reshape(2, 64, LANES)
        block = jnp.concatenate([halo, outer, inner] if low else [inner, outer, halo], 0)
        states.append(step(step(block)).reshape(LANES, LANES))
    return states


def x_edge_state(half, air_ref, coefs, ylow, yhigh, xlow, xhigh):
    def with_ends(row, first, last):
        at = iota(row.shape, 0)
        size = row.shape[0]
        plus_y = jnp.where(at == size - 1, last, pltpu.roll(row, size - 1, 0))
        minus_y = jnp.where(at == 0, first, pltpu.roll(row, 1, 0))
        return plus_y, minus_y

    def own(x):
        return air_ref[half, x]

    def beyond(x, y):
        slab = ylow if y < 0 else yhigh
        at = (y + 2 if y < 0 else y - 32) * 64 + x
        return slab[at : at + 1]

    done = []
    for low in (True, False):
        halo = xlow if low else xhigh
        near, far = (halo[32:64], halo[0:32]) if low else (halo[0:32], halo[32:64])
        xs = [0, 1, 2, 3] if low else [63, 62, 61, 60]
        rows = [far, near] + [own(x) for x in xs]
        ends = [None, (halo[64:65], halo[65:66])] + [(beyond(x, -1), beyond(x, 32)) for x in xs]
        outer = [None, None] + [(beyond(x, -2), beyond(x, 33)) for x in xs]

        def apply(centre, outward, inward, plus_y, minus_y):
            plus_x, minus_x = (inward, outward) if low else (outward, inward)
            return combine(coefs, centre, plus_x, minus_x, plus_y, minus_y)

        once = {}
        for i in range(1, 5):
            plus_y, minus_y = with_ends(rows[i], *ends[i])
            once[i] = apply(rows[i], rows[i - 1], rows[i + 1], plus_y, minus_y)
        twice = []
        for i in (2, 3):
            first = apply(
                ends[i][0], ends[i - 1][0], ends[i + 1][0], rows[i][0:1], outer[i][0]
            )
            last = apply(
                ends[i][1], ends[i - 1][1], ends[i + 1][1], outer[i][1], rows[i][31:32]
            )
            plus_y, minus_y = with_ends(once[i], first, last)
            twice.append(apply(once[i], once[i - 1], once[i + 1], plus_y, minus_y))
        done += twice if low else twice[::-1]
    return jnp.concatenate(done, 0)


def edge_kernel(
    air_ref, coef_ref, w1_ref, bias_ref, w2_ref, last_ref, cell_ref, count_ref, recv1_ref,
    recv2_ref, pair_ref, cross_ref, edge_ref, acc0_ref, acc1_ref, acc2_ref, side0_ref, side1_ref,
    out_ref,
):
    state = []
    for half in range(2):
        lanes = lanes_of(half)
        ylow, yhigh = by_side("gy", recv1_ref[:, lanes], recv2_ref[:, lanes])
        xlow, xhigh = by_side("gx", pair_ref[:, lanes], cross_ref[:, lanes])
        coefs = coefs_of(coef_ref, half)
        along_y = x_edge_state(half, air_ref, coefs, ylow, yhigh, xlow, xhigh)
        state.append(jnp.concatenate([edge_ref[half], along_y], 0))
    matrices = matrices_of(w1_ref, bias_ref, w2_ref, last_ref)
    groups = [GROUPS * TILES + g for g in range(3)]
    acc = finish(state, groups, matrices, cell_ref, count_ref, EDGE_CHUNKS)
    acc = acc + (acc0_ref[...] + acc1_ref[...] + acc2_ref[...])
    heat = jnp.transpose(acc[0:32] + acc[32:64])
    vapour = jnp.transpose(acc[64:96] + acc[96:128])
    turn = side_turn()

    def side(index):
        return jnp.where(turn == 0, side0_ref[index], side1_ref[index])

    below = side(4)
    ocean = lax.axis_index("sect") == 1
    flux = THERMAL_FACTOR * (side(2) - heat) / below
    out_ref[0] = jnp.where(ocean, side(0), flux)
    flux = WETNESS_FACTOR * (side(3) - vapour) / below
    out_ref[1] = jnp.where(ocean, side(1), flux)


def edges(core, halos, others):
    return pl.pallas_call(
        edge_kernel,
        out_shape=jax.ShapeDtypeStruct((2, 16, 32), F32),
        in_specs=[VMEM] * 18,
        out_specs=VMEM,
        compiler_params=params(24),
        cost_estimate=cost(1 << 28),
    )(*core, *halos, *others)


def exchanges(axis, first):
    sizes = [lax.axis_size(name) for name in AXES]
    size = lax.axis_size(axis)
    pairs = []
    for device in range(sizes[0] * sizes[1] * sizes[2]):
        at = [device // (sizes[1] * sizes[2]), device // sizes[2] % sizes[1], device % sizes[2]]
        dim = AXES.index(axis)
        step = 1 if (at[dim] - first) % 2 == 0 else -1
        at[dim] = (at[dim] + step) % size
        pairs.append((device, (at[0] * sizes[1] + at[1]) * sizes[2] + at[2]))
    return pairs


def shards(
    air_profile_matrix,
    spreading_numbers,
    eastward_advection_number,
    northward_advection_number,
    landmass_warmth,
    physics_increments,
    underlying_water_index,
    water_indicator,
    waterbody_profiles,
    waterbody_drivers,
    inverted_blending_matrix,
    entry_layer_matrix,
    entry_layer_offset,
    exit_layer_matrix,
):
    air = air_profile_matrix
    sides = (
        landmass_warmth.T,
        water_indicator.T,
        waterbody_profiles.transpose(0, 2, 3, 1),
        waterbody_drivers.transpose(0, 2, 1),
        inverted_blending_matrix,
    )
    layers = (
        spreading_numbers.reshape(1, -1),
        eastward_advection_number.reshape(1, -1),
        northward_advection_number.reshape(1, -1),
        entry_layer_matrix,
        entry_layer_offset.reshape(1, -1),
        exit_layer_matrix,
    )
    columns = (physics_increments.T, underlying_water_index.T)
    air, sides, layers, columns = jax.tree.map(
        lambda array: pltpu.with_memory_space_constraint(array, pltpu.HBM),
        (air, sides, layers, columns),
    )
    loaded = load((air, sides[0], *columns, *sides[1:], *layers))
    send1, send2 = loaded[:2]
    acc0, side0 = loaded[10:12]
    recv2 = lax.ppermute(send2, AXES, exchanges("gy", 1))
    recv1 = lax.ppermute(send1, AXES, exchanges("gy", 0))
    *core, acc1, side1 = middle(loaded[2:10], loaded[12:], (air, *layers))
    core += loaded[8:10]
    acc1, recv2, recv1 = lax.optimization_barrier((acc1, recv2, recv1))
    send_pair, send_cross = x_slabs(core[0], recv1, recv2)
    cross = lax.ppermute(send_cross, AXES, exchanges("gx", 1))
    pair = lax.ppermute(send_pair, AXES, exchanges("gx", 0))
    acc2, edge = late(core, (recv1, recv2, send1, send2))
    acc2, cross, pair = lax.optimization_barrier((acc2, cross, pair))
    result = edges(
        core, (recv1, recv2, pair, cross), (edge, acc0, acc1, acc2, side0, side1)
    )
    return result.transpose(0, 2, 1)[None]


def solution(mesh):
    in_specs = (
        P("gx", "gy", None),
        P(),
        P(),
        P(),
        P("gx", "gy"),
        P(None, "gy"),
        P("gx", "gy"),
        P("gx", "gy"),
        P(None, None, "gx", "gy"),
        P(None, "gx", "gy"),
        P(),
        P(),
        P(),
        P(),
    )
    out_specs = P("sect", None, "gx", "gy")
    return jax.shard_map(shards, mesh=mesh, in_specs=in_specs, out_specs=out_specs, check_vma=False)
```
